128 devices in a mesh: lat: 8 (over y, z_lo), lon: 16 (over z_hi, x, core).
Axes of the slice: x: 4, y: 4, z: 4 (z_hi: 2, z_lo: 2; z = z_hi * 2 + z_lo), core: 2. Of those that a mesh axis runs over, the one named last changes fastest.
Arguments:
- state: bfloat16 [8, 48, 192, 192], P(None, 'lat', 'lon'), may hold values from -6 to 6
- lat_valid: int32 [48], replicated, may hold values from 0 to 1, as said below
- norm_gains: float32 [2, 2, 192], replicated, may hold values from 0.1 to 1.9
- qkv_weight: bfloat16 [2, 192, 576], replicated, may hold values from -0.4375 to 0.4375
- proj_weight: bfloat16 [2, 192, 192], replicated, may hold values from -0.4375 to 0.4375
- fc1_weight: bfloat16 [2, 192, 768], replicated, may hold values from -0.4375 to 0.4375
- fc2_weight: bfloat16 [2, 768, 192], replicated, may hold values from -0.21875 to 0.21875
- earth_bias: bfloat16 [2, 8, 4, 19872], P(None, 'lat', None, 'lon'), may hold values from -3 to 3
- merge_gain: float32 [768], replicated, may hold values from 0.1 to 1.9
- merge_weight: bfloat16 [768, 384], replicated, may hold values from -0.21875 to 0.21875
Outputs:
- merged: bfloat16 [8, 24, 96, 384], P(None, 'lat', 'lon')
The draws below stay inside these ranges and needn't reach their ends.
Inputs may be any that keep to these rules, and one draw needn't show every extreme that they name: `lat_valid`: 0 on the first 0 to 3 latitude rows and on the last 1 to 3 rows, 1 on all rows between.
All inputs are finite; a program needn't handle non-finite values.
Results may differ from the reference program's by a relative error of at most 0.015.
Values may be sent and summed in bfloat16 or wider, within the bound.
No kernel may reach another device: no remote copies, remote signals or barrier semaphores. Data moves between devices by JAX's collectives and lax.ppermute only.
A program may use at most 192 MiB of HBM per device.

```python
import jax
import jax.numpy as jnp
from jax import lax

C = 192
HEADS = 6
HIDDEN_SIZE = 768
PL = 8
WPL = 2
WLAT = 6
WLON = 12
SPL = 1
SLAT = 3
SLON = 6
NLAT = 48
NLON = 192
NLAT_WIN = 8
PL_WIN = 4
BIAS_TERMS = 19872


def draw_lat_valid(key, part):
    key = jax.random.fold_in(key, 7)
    top_key = jax.random.fold_in(key, 11)
    bottom_key = jax.random.fold_in(key, 13)
    leading = jax.random.randint(top_key, (), 0, SLAT + 1)
    trailing = jax.random.randint(bottom_key, (), 1, SLAT + 1)
    row_index = jnp.arange(NLAT, dtype=jnp.int32)
    inside = (row_index >= leading) & (row_index < NLAT - trailing)
    return inside.astype(jnp.int32)


def steps_of(key, shape, split, least, largest):
    def one(dim, shards_of):
        heights = jax.random.uniform(jax.random.fold_in(jax.random.fold_in(key, 6), dim), (shards_of,), jnp.float32, least / len(split), largest / len(split))
        return jnp.repeat(jnp.exp(heights), shape[dim] // shards_of).reshape((-1,) + (1,) * (len(shape) - dim - 1))

    loudness = one(*split[0])
    for cut in split[1:]:
        loudness = loudness * one(*cut)
    return loudness


def gaussian(key, dims, deviation, bound, cuts=(), kind=jnp.bfloat16):
    array = jax.random.normal(key, dims, jnp.float32) * deviation
    if len(cuts) > 0:
        array = steps_of(key, dims, cuts, -0.22, 0.18) * array
    return jnp.clip(array, min=-bound, max=bound).astype(kind)


def setup_inputs(seed: int = 0) -> dict:
    keys = jax.random.split(jax.random.key(seed), 11)
    state = gaussian(keys[0], (PL, NLAT, NLON, C), 1.0, 6.0, ((1, 8), (2, 16)))
    lat_valid = draw_lat_valid(jax.random.fold_in(keys[10], 71), 0)
    norm_gains = jnp.clip(1.0 + 0.18 * jax.random.normal(keys[2], (2, 2, C), jnp.float32), 0.1, 1.9)
    qkv_weight = gaussian(keys[3], (2, C, 3 * C), C ** -0.5, 0.4375)
    proj_weight = gaussian(keys[4], (2, C, C), C ** -0.5, 0.4375)
    fc1_weight = gaussian(keys[5], (2, C, HIDDEN_SIZE), C ** -0.5, 0.4375)
    fc2_weight = gaussian(keys[6], (2, HIDDEN_SIZE, C), HIDDEN_SIZE ** -0.5, 0.21875)
    earth_bias = gaussian(keys[7], (2, NLAT_WIN, PL_WIN, BIAS_TERMS), 0.5, 3.0, ((1, 8), (3, 16)))
    merge_gain = jnp.clip(1.0 + 0.18 * jax.random.normal(keys[8], (4 * C,), jnp.float32), 0.1, 1.9)
    merge_weight = gaussian(keys[9], (4 * C, 2 * C), (4 * C) ** -0.5, 0.21875)
    return {"state": state, "lat_valid": lat_valid, "norm_gains": norm_gains, "qkv_weight": qkv_weight, "proj_weight": proj_weight, "fc1_weight": fc1_weight, "fc2_weight": fc2_weight, "earth_bias": earth_bias, "merge_gain": merge_gain, "merge_weight": merge_weight}


def layer_norm(values, scales):
    average = lax.optimization_barrier(jnp.mean(values, axis=-1, keepdims=True))
    centred = values - average
    spread = lax.optimization_barrier(jnp.mean(centred * centred, axis=-1, keepdims=True))
    return centred * lax.rsqrt(spread + 1e-05) * scales

def regions(extent, window, offset, position):
    return jnp.where(position < extent - window, 0, jnp.where(position < extent - offset, 1, 2)).astype(jnp.int32)

def expand_bias(bias_table):
    leading = bias_table.shape[:-1]
    window_cells = WPL * WLAT
    grouped = bias_table.reshape(leading + (HEADS, window_cells, window_cells, 2 * WLON - 1))
    pieces = [grouped[..., WLON - 1 - shift_at:2 * WLON - 1 - shift_at] for shift_at in range(WLON)]
    expanded = jnp.swapaxes(jnp.stack(pieces, axis=-2), -3, -2)
    return expanded.reshape(leading + (HEADS, window_cells * WLON, window_cells * WLON))

def window_attention(projected, bias_dense, key_ok, lat_region, level_region, proj_weight):
    levels, lat_rows, lon_cols, triple = projected.shape
    channels = triple // 3
    head_count = bias_dense.shape[2]
    head_size = channels // head_count
    lat_windows = lat_rows // WLAT
    level_windows = levels // WPL
    lon_windows = lon_cols // WLON
    window_size = WPL * WLAT * WLON
    blocks = projected.reshape(levels, lat_windows, WLAT, lon_cols, triple).transpose(1, 0, 2, 3, 4)
    key_flags = key_ok.reshape(lat_windows, WLAT)
    lat_parts = lat_region.reshape(lat_windows, WLAT)
    level_token = jnp.broadcast_to(level_region.reshape(level_windows, WPL, 1, 1), (level_windows, WPL, WLAT, WLON)).reshape(level_windows, window_size)

    def per_window(pieces):
        stripe, stripe_bias, stripe_flags, stripe_lat = pieces
        windows = stripe.reshape(level_windows, WPL, WLAT, lon_windows, WLON, triple).transpose(0, 3, 1, 2, 4, 5)
        windows = windows.reshape(level_windows, lon_windows, window_size, 3, head_count, head_size)
        queries = windows[:, :, :, 0].astype(jnp.float32)
        key_part = windows[:, :, :, 1].astype(jnp.float32)
        value_part = windows[:, :, :, 2].astype(jnp.float32)
        scores = jnp.einsum('pwqhd,pwkhd->pwhqk', queries, key_part) * head_size ** (-0.5)
        scores = scores + stripe_bias.astype(jnp.float32)[:, None]
        lat_token = jnp.broadcast_to(stripe_lat.reshape(1, WLAT, 1), (WPL, WLAT, WLON)).reshape(window_size)
        flag_token = jnp.broadcast_to(stripe_flags.reshape(1, WLAT, 1), (WPL, WLAT, WLON)).reshape(window_size)
        allowed = (level_token[:, :, None] == level_token[:, None, :]) & (lat_token[:, None] == lat_token[None, :])[None] & flag_token[None, None, :]
        weights = jnp.where(allowed[:, None, None], jnp.exp(scores), 0.0)
        totals = jnp.maximum(lax.optimization_barrier(jnp.sum(weights, axis=-1, keepdims=True)), 1.0)
        shares = (weights / totals).astype(jnp.bfloat16)
        blended = jnp.einsum('pwhqk,pwkhd->pwqhd', shares.astype(jnp.float32), value_part).astype(jnp.bfloat16)
        blended = blended.reshape(level_windows, lon_windows, WPL, WLAT, WLON, channels).transpose(0, 2, 3, 1, 4, 5)
        blended = blended.reshape(levels, WLAT, lon_cols, channels)
        return jnp.dot(blended, proj_weight, preferred_element_type=jnp.float32).astype(jnp.bfloat16)
    results = lax.map(per_window, (blocks, bias_dense, key_flags, lat_parts))
    return results.transpose(1, 0, 2, 3, 4).reshape(levels, lat_rows, lon_cols, channels)

def finish(inputs, attended, norm_scale, fc1_weight, fc2_weight, keep_rows):
    middle = inputs.astype(jnp.float32) + attended.astype(jnp.float32)
    normed_two = layer_norm(middle, norm_scale).astype(jnp.bfloat16)
    hidden = jax.nn.gelu(jnp.dot(normed_two, fc1_weight, preferred_element_type=jnp.float32), approximate=False).astype(jnp.bfloat16)
    outcome = middle + jnp.dot(hidden, fc2_weight, preferred_element_type=jnp.float32)
    return jnp.where(keep_rows, outcome, 0.0).astype(jnp.bfloat16)

def attention_block(inputs, gain_pair, qkv_weight, proj_weight, fc1_weight, fc2_weight, bias_table, lat_valid, shifted):
    levels, lat_rows, lon_cols, channels = inputs.shape
    normed = layer_norm(inputs.astype(jnp.float32), gain_pair[0]).astype(jnp.bfloat16)
    level_index = jnp.arange(levels, dtype=jnp.int32)
    row_index = jnp.arange(lat_rows, dtype=jnp.int32)
    if shifted:
        rolled = jnp.roll(normed, (-SPL, -SLAT, -SLON), axis=(0, 1, 2))
        level_region = regions(levels, WPL, SPL, level_index)
        lat_region = regions(lat_rows, WLAT, SLAT, row_index)
        key_ok = jnp.roll(lat_valid, -SLAT) > 0
    else:
        rolled = normed
        level_region = jnp.zeros((levels,), jnp.int32)
        lat_region = jnp.zeros((lat_rows,), jnp.int32)
        key_ok = lat_valid > 0
    projected = jnp.dot(rolled, qkv_weight, preferred_element_type=jnp.float32).astype(jnp.bfloat16)
    attended = window_attention(projected, expand_bias(bias_table), key_ok, lat_region, level_region, proj_weight)
    if shifted:
        attended = jnp.roll(attended, (SPL, SLAT, SLON), axis=(0, 1, 2))
    keep_rows = (lat_valid > 0)[:, None, None]

    def per_level(paired):
        return finish(paired[0], paired[1], gain_pair[1], fc1_weight, fc2_weight, keep_rows)
    return lax.map(per_level, (inputs, attended))

def reference(state, lat_valid, norm_gains, qkv_weight, proj_weight, fc1_weight, fc2_weight, earth_bias, merge_gain, merge_weight):
    hidden_state = state
    for layer in range(2):
        hidden_state = attention_block(hidden_state, norm_gains[layer], qkv_weight[layer], proj_weight[layer], fc1_weight[layer], fc2_weight[layer], earth_bias[layer], lat_valid, layer == 1)
    levels, lat_rows, lon_cols, channels = hidden_state.shape
    grouped = hidden_state.reshape(levels, lat_rows // 2, 2, lon_cols // 2, 2, channels).transpose(0, 1, 3, 2, 4, 5)
    grouped = grouped.reshape(levels, lat_rows // 2, lon_cols // 2, 4 * channels)
    merge_normed = layer_norm(grouped.astype(jnp.float32), merge_gain).astype(jnp.bfloat16)
    return jnp.dot(merge_normed, merge_weight, preferred_element_type=jnp.float32).astype(jnp.bfloat16)
```

```python
import functools

import jax
import jax.numpy as jnp
import numpy as np
from jax import lax
from jax.experimental import pallas as pl
from jax.experimental.pallas import tpu as pltpu
from jax.sharding import PartitionSpec as P

BF16 = jnp.bfloat16
F32 = jnp.float32
C = 192
HEADS = 6
HEAD_SIZE = 32
HIDDEN = 768
LEVELS, ROWS, COLS = 8, 6, 12
WINDOWS = 4
TOKENS = 144
CELLS = 576
SPAN = 23
HALF = 6 * SPAN
GROUP = 128
KEYS = 2 * GROUP
LATS, LONS = 8, 16
SHARD = 1242
SHIFT = 12.0
MASKED = -1e30


def one_hot(sources, width):
    sources = np.asarray(sources)
    matrix = np.zeros((len(sources), width), np.float32)
    rows = np.nonzero(sources >= 0)[0]
    matrix[rows, sources[rows]] = 1.0
    return jnp.asarray(matrix, BF16)


def quarter_cells():
    return [(1, 1), (0, 1), (1, 0), (0, 0)]


def query_order():
    return [a * 12 + i for i in range(12) for a in range(12)]


def quarter_chunks(qr, qc):
    return [((3 * qr + r) * COLS + 6 * qc) * LEVELS for r in range(3)]


def level_cells(level):
    return pl.ds(level, ROWS * COLS, stride=LEVELS)


def read_window(cells, first_level):
    parts = [
        jnp.concatenate([cells[0, level_cells(level % LEVELS)], cells[1, level_cells(level % LEVELS)]], axis=1)
        for level in (first_level, first_level + 1)
    ]
    return jnp.concatenate(parts, axis=0)[:, :C]


def write_window(cells, first_level, values):
    wide = jnp.concatenate([values, jnp.zeros((TOKENS, 2 * GROUP - C), F32)], axis=1)
    for offset in range(2):
        rows = wide[offset * 72 : (offset + 1) * 72]
        where = level_cells((first_level + offset) % LEVELS)
        cells[0, where] = rows[:, :GROUP]
        cells[1, where] = rows[:, GROUP:]


def read_quarter(cells, qr, qc):
    parts = [
        jnp.concatenate([cells[0, at : at + 48], cells[1, at : at + 48]], axis=1) for at in quarter_chunks(qr, qc)
    ]
    return jnp.concatenate(parts, axis=0)[:, :C]


def write_quarter(cells, qr, qc, values):
    wide = jnp.concatenate([values, jnp.zeros((TOKENS, 2 * GROUP - C), F32)], axis=1)
    for r, at in enumerate(quarter_chunks(qr, qc)):
        cells[0, at : at + 48] = wide[r * 48 : (r + 1) * 48, :GROUP]
        cells[1, at : at + 48] = wide[r * 48 : (r + 1) * 48, GROUP:]


def table_rows(block):
    sources = []
    for lead in (0, 4):
        for key_level in range(2):
            for window in range(WINDOWS):
                for slot in range(16):
                    a = slot - lead
                    inside = 0 <= a < 12
                    sources.append((a * 2 + key_level) * 8 + block * 4 + window if inside else -1)
    return sources


def column_choice(parity):
    matrix = np.zeros((HALF, 6 * GROUP), np.float32)
    for at in range(6):
        i = 2 * at + parity
        for row in range(ROWS):
            for k in range(12):
                matrix[row * SPAN + k - i + 11, at * GROUP + row * 12 + k] = 1.0
    return jnp.asarray(matrix, BF16)


def layer_norm(values, scales):
    average = jnp.mean(values, axis=-1, keepdims=True)
    centred = values - average
    spread = jnp.mean(centred * centred, axis=-1, keepdims=True)
    return centred * lax.rsqrt(spread + 1e-05) * scales


def dot(a, b):
    return jnp.dot(a, b, preferred_element_type=F32)


def dot_transposed(a, b):
    return lax.dot_general(a, b, (((1,), (1,)), ((), ())), preferred_element_type=F32)


def moved(choice, rows):
    return dot(choice, rows).astype(BF16)


def head_lanes(head):
    lane = lax.broadcasted_iota(jnp.int32, (1, C), 1)
    return (lane >= head * HEAD_SIZE) & (lane < (head + 1) * HEAD_SIZE)


def project(normed, qkv_weight, query_choice):
    queries = moved(query_choice, dot(normed, qkv_weight[:, :C]).astype(BF16))
    pad = jnp.zeros((GROUP - 72, C), F32)

    def padded(part):
        return jnp.concatenate([part[:72], pad, part[72:], pad], axis=0).astype(BF16)

    keys = padded(dot(normed, qkv_weight[:, C : 2 * C]))
    values = padded(dot(normed, qkv_weight[:, 2 * C :]))
    ones = jnp.ones((KEYS, KEYS - C), BF16)
    return queries, keys, jnp.concatenate([values, ones], axis=1)


def score(queries, keys):
    stacked = jnp.concatenate(
        [jnp.where(head_lanes(h), queries, jnp.zeros((), BF16)) for h in range(HEADS)], axis=0
    )
    return dot_transposed(stacked, keys) * HEAD_SIZE ** (-0.5)


def blend(scores, values, bias_of):
    weights = []
    for h in range(HEADS):
        part = scores[h * TOKENS : (h + 1) * TOKENS] + bias_of(h)
        weights.append(jnp.exp(part).astype(BF16))
    blended = dot(jnp.concatenate(weights, axis=0), values)
    total = jnp.zeros((TOKENS, C), F32)
    result = jnp.zeros((TOKENS, C), F32)
    for h in range(HEADS):
        part = blended[h * TOKENS : (h + 1) * TOKENS]
        result = jnp.where(head_lanes(h), part[:, :C], result)
        total = jnp.where(head_lanes(h), part[:, C : C + 1], total)
    return (result / jnp.maximum(total, np.exp(-SHIFT))).astype(BF16)


def expanded_bias(z_even, z_odd, window, head):
    rows = []
    for at in range(6):
        lanes = slice(at * GROUP, (at + 1) * GROUP)
        halves = []
        for key_level in range(2):
            first = head * 128 + (key_level * 4 + window) * 16
            top = z_even[first : first + 16, lanes]
            low = z_odd[first : first + 16, lanes]
            halves.append(jnp.concatenate([top[:8], top[8:] + low[:8], low[8:]], axis=0))
        rows.append(jnp.concatenate(halves, axis=1))
    return jnp.concatenate(rows, axis=0)


def expand_tables(table_ref, table_choice, even_ref, odd_ref, z_even, z_odd):
    tops, lows = [], []
    for h in range(HEADS):
        picked = moved(table_choice[...], table_ref[h * 192 : (h + 1) * 192, :HALF])
        tops.append(picked[:128])
        lows.append(picked[128:])
    z_even[...] = dot(jnp.concatenate(tops, axis=0), even_ref[...])
    z_odd[...] = dot(jnp.concatenate(lows, axis=0), odd_ref[...])


def erf_gelu(values):
    return 0.5 * values * (1.0 + lax.erf(values * np.float32(np.sqrt(0.5))))


def feed_forward(middle, gain, fc1, fc2, keep):
    hidden = erf_gelu(dot(layer_norm(middle, gain).astype(BF16), fc1)).astype(BF16)
    return jnp.where(keep, middle + dot_transposed(hidden, fc2), 0.0).astype(BF16)


def pack_piece(piece):
    side = jnp.concatenate(
        [piece[:80, 128:], jnp.concatenate([piece[80:, 128:], piece[:16, 128:]], axis=0)], axis=1
    )
    return jnp.concatenate([piece[:, :128], side], axis=0)


def unpack_piece(packed):
    side = packed[TOKENS:]
    ends = jnp.concatenate([side[:, :64], side[: TOKENS - 80, 64:]], axis=0)
    return jnp.concatenate([packed[:TOKENS], ends], axis=1)


def prepare_masks(lat_valid, first_mask, second_mask, keep):
    lat = lax.axis_index("lat")

    def flag(row):
        return lat_valid[row] > 0

    lane = lax.broadcasted_iota(jnp.int32, (8, KEYS), 1)
    key_row = lax.rem(lane, GROUP) // 12
    mask = jnp.full((8, KEYS), MASKED, F32)
    usable = jnp.full((8, KEYS), MASKED, F32)
    for r in range(ROWS):
        mask = jnp.where((key_row == r) & flag(lat * ROWS + r), -SHIFT, mask)
        rolled = lax.rem(lat * ROWS + 3 + r, LATS * ROWS)
        usable = jnp.where((key_row == r) & flag(rolled), 0.0, usable)
    first_mask[...] = mask
    a = lax.rem(lax.broadcasted_iota(jnp.int32, (TOKENS, 1), 0), 12)
    query_half = jnp.where(lax.rem(a, ROWS) >= 3, 1, 0)
    key_half = jnp.where(key_row[:1] >= 3, 1, 0)
    same_rows = (query_half == key_half) | (lat != LATS - 1)
    same_level = jnp.where(a >= ROWS, 1, 0) == jnp.where(lane[:1] >= GROUP, 1, 0)
    whole = jnp.where(same_rows, usable[:1], MASKED)
    second_mask[0] = whole
    second_mask[1] = jnp.where(same_level, whole, MASKED)
    for half in range(2):
        for r in range(3):
            value = jnp.where(flag(lat * ROWS + 3 * half + r), 1.0, 0.0)
            keep[half, r * 48 : (r + 1) * 48] = jnp.full((48, GROUP), value, F32)


def fetch(sources, held, sems):
    copies = [pltpu.make_async_copy(a, b, sems.at[n]) for n, (a, b) in enumerate(zip(sources, held))]
    for copy in copies:
        copy.start()
    return copies


def sliced(kernel, layers, *refs):
    kernel(*[ref.at[layers[at]] if at in layers else ref for at, ref in enumerate(refs)])


def fetch_kernel(*refs):
    count = len(refs) // 2
    for copy in fetch(refs[:count], refs[count : 2 * count], refs[-1]):
        copy.wait()


def prepare_kernel(mine, proj, fc1, fc2, *refs):
    for copy in fetch((proj, fc1, fc2), refs[:3], refs[3]):
        copy.wait()


def join_kernel(*refs):
    at = 0
    for ref in refs[:-1]:
        if ref.shape[1:] == refs[-1].shape[1:]:
            refs[-1][at : at + ref.shape[0]] = ref[...]
            at += ref.shape[0]


def before_kernel(lat_valid, halves, x, gains, qkv_weight, query_choice, *refs):
    sources, (scores_out, v_out, first_mask, second_mask, keep) = refs[:3], refs[3:8]
    held, (cells, sems) = refs[8:11], refs[11:]
    copies = fetch(sources, held, sems)
    prepare_masks(lat_valid, first_mask, second_mask, keep)
    wide = jnp.concatenate([x[...].astype(F32), jnp.zeros((CELLS, 2 * GROUP - C), F32)], axis=1)
    cells[0] = wide[:, :GROUP]
    cells[1] = wide[:, GROUP:]
    for p in range(WINDOWS):
        normed = layer_norm(read_window(cells, 2 * p), gains[0, 0:1]).astype(BF16)
        q, k, v_out[p] = project(normed, qkv_weight[...], query_choice[...])
        scores_out[p] = score(q, k)
    for copy in copies:
        copy.wait()


def first_quarter(quarter, x, cells, gains, fc1, fc2, keep):
    qr, qc = quarter_cells()[quarter]
    inputs = jnp.concatenate([x[at : at + 48] for at in quarter_chunks(qr, qc)], axis=0)
    middle = inputs.astype(F32) + read_quarter(cells, qr, qc).astype(BF16).astype(F32)
    return feed_forward(middle, gains[0, 1:2], fc1[...], fc2[...], keep[qr][:, :1] > 0)


def first_kernel(mine, theirs, scores, v, first_mask, keep, x, gains, query_choice, proj, fc1, fc2, even, odd, table_choice, sent_lat, sent_lon, sent_both, table_out, out, cells, table_f32, z_even, z_odd):
    me = lax.axis_index("lon")
    for g in range(LONS):
        slot = lax.rem(me // 2 - g // 2 + 8, 4) * 2 + jnp.where(me // 8 == g // 8, 0, 1)
        shard = jnp.where(lax.rem(me, 2) == g % 2, mine[slot], theirs[slot]).astype(F32)
        piece = jnp.concatenate([shard[0], shard[1]], axis=0)
        for n in range(9):
            at = (g * 9 + n) * 8
            table_f32[at : at + 8, :HALF] = piece[:, n * HALF : (n + 1) * HALF]
    table_out[:, :HALF] = table_f32[:, :HALF].astype(BF16)
    expand_tables(table_out, table_choice, even, odd, z_even, z_odd)
    mask = first_mask[0:1]
    for p in range(WINDOWS):
        blended = blend(scores[p], v[p], lambda h: expanded_bias(z_even, z_odd, p, h) + mask)
        write_window(cells, 2 * p, dot(moved(query_choice[...], blended), proj[...]))
    for quarter, target in ((2, sent_lon), (3, sent_both), (1, sent_lat)):
        result = first_quarter(quarter, x, cells, gains, fc1, fc2, keep)
        out[(quarter - 1) * TOKENS : quarter * TOKENS] = result
        target[...] = pack_piece(result)


def bias_kernel(*refs):
    sources, (table, second_mask, even, odd, x, cells, gains, fc1, fc2, keep) = refs[:3], refs[3:13]
    (bias_out, near), held, (z_even, z_odd, sems) = refs[13:15], refs[15:18], refs[18:]
    copies = fetch(sources, held, sems)
    table_choice = held[0]
    near[...] = first_quarter(0, x, cells, gains, fc1, fc2, keep)
    copies[0].wait()
    expand_tables(table, table_choice, even, odd, z_even, z_odd)
    for p in range(WINDOWS):
        for h in range(HEADS):
            whole = expanded_bias(z_even, z_odd, p, h) + second_mask[1 if p == WINDOWS - 1 else 0]
            bias_out[p, h * TOKENS : (h + 1) * TOKENS] = whole.astype(BF16)
    for copy in copies[1:]:
        copy.wait()


def write_normed(cells, quarter, piece, gains):
    qr, qc = quarter_cells()[quarter]
    normed = layer_norm(piece.astype(F32), gains[1, 0:1]).astype(BF16)
    write_quarter(cells, 1 - qr, 1 - qc, normed.astype(F32))


def ready_kernel(near, from_lon, from_both, gains, cells):
    write_normed(cells, 0, near[...], gains)
    write_normed(cells, 2, unpack_piece(from_lon[...]), gains)
    write_normed(cells, 3, unpack_piece(from_both[...]), gains)


def second_kernel(ready, from_lat, bias, gains, qkv_weight, proj, query_choice, own, sent_lat, sent_lon, sent_both, cells, results):
    for quarter in (0, 2, 3):
        qr, qc = quarter_cells()[quarter]
        for at in quarter_chunks(1 - qr, 1 - qc):
            for half in range(2):
                cells[half, at : at + 48] = ready[half, at : at + 48]
    write_normed(cells, 1, unpack_piece(from_lat[...]), gains)
    for p in range(WINDOWS):
        normed = read_window(cells, 2 * p + 1).astype(BF16)
        q, k, v = project(normed, qkv_weight[...], query_choice[...])

        def bias_of(h):
            return bias[p, h * TOKENS : (h + 1) * TOKENS].astype(F32) - SHIFT

        blended = blend(score(q, k), v, bias_of)
        write_window(results, 2 * p + 1, dot(moved(query_choice[...], blended), proj[...]))
    pieces = [read_quarter(results, 1 - qr, 1 - qc).astype(BF16) for qr, qc in quarter_cells()]
    own[...] = pieces[0]
    sent_lat[...] = pack_piece(pieces[1])
    sent_lon[...] = pack_piece(pieces[2])
    sent_both[...] = pack_piece(pieces[3])


def own_kernel(*refs):
    sources, (keep, near, own, gains), result, held, sems = refs[:3], refs[3:7], refs[7], refs[8:11], refs[11]
    copies = fetch(sources, held, sems)
    for copy in copies:
        copy.wait()
    middle = near[...].astype(F32) + own[...].astype(F32)
    result[...] = feed_forward(middle, gains[1, 1:2], held[0][...], held[1][...], keep[1][:, :1] > 0)


def last_kernel(keep, far, done, from_lat, from_lon, from_both, gains, fc1, fc2, merge_gain, merge_weight, merged):
    groups = {}
    for quarter, (qr, qc) in enumerate(quarter_cells()):
        if quarter == 0:
            result = done[...]
        else:
            attended = unpack_piece((from_lat, from_lon, from_both)[quarter - 1][...])
            middle = far[(quarter - 1) * TOKENS : quarter * TOKENS].astype(F32) + attended.astype(F32)
            result = feed_forward(middle, gains[1, 1:2], fc1[...], fc2[...], keep[qr][:, :1] > 0)
        result = result.astype(F32)
        for r in range(3):
            for c in range(6):
                at = (r * 6 + c) * LEVELS
                groups[3 * qr + r, 6 * qc + c] = result[at : at + LEVELS]
    parts = [
        jnp.concatenate([groups[2 * r + dr, 2 * c + dc] for r in range(3) for c in range(6)], axis=0)
        for dr in range(2)
        for dc in range(2)
    ]
    average = sum(jnp.sum(part, axis=-1, keepdims=True) for part in parts) / (4 * C)
    parts = [part - average for part in parts]
    spread = sum(jnp.sum(part * part, axis=-1, keepdims=True) for part in parts) / (4 * C)
    scale = lax.rsqrt(spread + 1e-05)
    total = jnp.zeros((TOKENS, 2 * C), F32)
    for d, part in enumerate(parts):
        normed = (part * scale * merge_gain[d : d + 1]).astype(BF16)
        total = total + dot(normed, merge_weight[d * C : (d + 1) * C])
    merged[...] = total.astype(BF16)


VMEM_SPEC = pl.BlockSpec(memory_space=pltpu.VMEM)
SMEM_SPEC = pl.BlockSpec(memory_space=pltpu.SMEM)


def call(kernel, name, micros, outs, scratch, *operands, in_specs=None):
    return pl.pallas_call(
        kernel,
        name=name,
        out_shape=outs,
        in_specs=in_specs or [VMEM_SPEC] * len(operands),
        out_specs=jax.tree.map(lambda _: VMEM_SPEC, outs),
        scratch_shapes=scratch,
        cost_estimate=pl.CostEstimate(flops=int(micros * 1e9), bytes_accessed=2**20, transcendentals=0),
        compiler_params=pltpu.CompilerParams(vmem_limit_bytes=16 * 2**20),
    )(*operands)


def shape(*dims, dtype=BF16):
    return jax.ShapeDtypeStruct(dims, dtype)


def sent(block, distance_lat, distance_lon):
    route = []
    for i in range(LATS):
        for j in range(LONS):
            to = ((i + distance_lat) % LATS) * LONS + (j + distance_lon) % LONS
            route.append((i * LONS + j, to))
    return lax.ppermute(block, ("lat", "lon"), route)


def turned(block, place):
    route = []
    for j in range(LONS):
        z, x, core = place(j // 8, j // 2 % 4, j % 2)
        route.append((j, z * 8 + x * 2 + core))
    return lax.ppermute(block, "lon", route)


def shards(state, lat_valid, norm_gains, qkv_weight, proj_weight, fc1_weight, fc2_weight, earth_bias, merge_gain, merge_weight):
    shard = earth_bias[:, 0]
    cells = pltpu.VMEM((2, CELLS, GROUP), F32)
    z_scratch = [pltpu.VMEM((768, 768), F32), pltpu.VMEM((768, 768), F32)]
    packed = shape(224, 128)

    def in_hbm(array):
        return pltpu.with_memory_space_constraint(array, pltpu.HBM)

    def like(arrays):
        return [shape(*array.shape, dtype=array.dtype) for array in arrays]

    hbm_spec = pl.BlockSpec(memory_space=pltpu.HBM)
    fc2_turned = jnp.swapaxes(fc2_weight, 1, 2)
    early = [
        shard[None],
        state.transpose(1, 2, 0, 3).reshape(CELLS, C),
        norm_gains,
        qkv_weight,
        one_hot(query_order(), TOKENS),
    ]
    constants = [column_choice(0), column_choice(1), one_hot(table_rows(0), 192)]
    layer = [shape(C, C), shape(C, HIDDEN), shape(C, HIDDEN)]
    other_half = turned(shard, lambda z, x, core: (1 - z, x, core))
    held_shard, x, gains, qkv0, query_choice = call(
        functools.partial(sliced, fetch_kernel, {3: 0}),
        "fetch",
        1.4,
        like(early[:3]) + [shape(C, 3 * C)] + like(early[4:]),
        [pltpu.SemaphoreType.DMA((len(early),))],
        *[in_hbm(array) for array in early],
        in_specs=[hbm_spec] * len(early),
    )
    halves = call(join_kernel, "halves", 0.2, shape(2, 2, WINDOWS, SHARD), [], held_shard, other_half[None])
    ring = [turned(halves, lambda z, x, core: (z, (x + hop) % 4, core)) for hop in range(1, 4)]
    scores, v, first_mask, second_mask, keep, even, odd, rows0 = call(
        before_kernel,
        "before",
        2.5,
        [
            shape(WINDOWS, HEADS * TOKENS, KEYS, dtype=F32),
            shape(WINDOWS, KEYS, KEYS),
            shape(8, KEYS, dtype=F32),
            shape(2, TOKENS, KEYS, dtype=F32),
            shape(2, TOKENS, GROUP, dtype=F32),
        ]
        + like(constants),
        [cells, pltpu.SemaphoreType.DMA((len(constants),))],
        in_hbm(lat_valid), halves, x, gains, qkv0, query_choice,
        *[in_hbm(array) for array in constants],
        in_specs=[SMEM_SPEC] + [VMEM_SPEC] * 5 + [hbm_spec] * len(constants),
    )
    mine = call(join_kernel, "mine", 0.3, shape(8, 2, WINDOWS, SHARD), [], halves, *ring, v)
    theirs = turned(mine, lambda z, x, core: (z, x, 1 - core))
    proj0, fc1_0, fc2_0 = call(
        functools.partial(sliced, prepare_kernel, {1: 0, 2: 0, 3: 0}),
        "prepare",
        1.2,
        layer,
        [pltpu.SemaphoreType.DMA((3,))],
        mine, in_hbm(proj_weight), in_hbm(fc1_weight), in_hbm(fc2_turned),
        in_specs=[VMEM_SPEC] + [hbm_spec] * 3,
    )
    to_lat, to_lon, to_both, tables, far, attended = call(
        first_kernel,
        "first",
        4.5,
        [packed, packed, packed, shape(1152, KEYS), shape(3 * TOKENS, C), shape(2, CELLS, GROUP, dtype=F32)],
        [pltpu.VMEM((1152, KEYS), F32)] + z_scratch,
        mine, theirs, scores, v, first_mask, keep, x, gains, query_choice, proj0, fc1_0, fc2_0, even, odd, rows0,
    )
    from_lon, from_both, from_lat = sent(to_lon, 0, -1), sent(to_both, -1, -1), sent(to_lat, -1, 0)
    late = [one_hot(table_rows(1), 192), qkv_weight, proj_weight]
    bias, near, _, qkv1, proj1 = call(
        functools.partial(sliced, bias_kernel, {1: 1, 2: 1}),
        "bias",
        0.2,
        [shape(WINDOWS, HEADS * TOKENS, KEYS), shape(TOKENS, C)]
        + like(late[:1])
        + [shape(C, 3 * C), shape(C, C)],
        z_scratch + [pltpu.SemaphoreType.DMA((len(late),))],
        *[in_hbm(array) for array in late],
        tables, second_mask, even, odd, x, attended, gains, fc1_0, fc2_0, keep,
        in_specs=[hbm_spec] * len(late) + [VMEM_SPEC] * 10,
    )
    ready = call(
        ready_kernel,
        "ready",
        0.6,
        shape(2, CELLS, GROUP, dtype=F32),
        [],
        near, from_lon, from_both, gains,
    )
    own, to_lat, to_lon, to_both = call(
        second_kernel,
        "second",
        4.5,
        [shape(TOKENS, C), packed, packed, packed],
        [cells, cells],
        ready, from_lat, bias, gains, qkv1, proj1, query_choice,
    )
    from_lon, from_both, from_lat = sent(to_lon, 0, 1), sent(to_both, 1, 1), sent(to_lat, 1, 0)
    done, fc1_1, fc2_1, merge = call(
        functools.partial(sliced, own_kernel, {0: 1, 1: 1}),
        "own",
        0.5,
        [shape(TOKENS, C)] + layer[1:] + like([merge_weight]),
        [pltpu.SemaphoreType.DMA((3,))],
        in_hbm(fc1_weight), in_hbm(fc2_turned), in_hbm(merge_weight), keep, near, own, gains,
        in_specs=[hbm_spec] * 3 + [VMEM_SPEC] * 4,
    )
    merged = call(
        last_kernel,
        "last",
        2.0,
        shape(TOKENS, 2 * C),
        [],
        keep, far, done, from_lat, from_lon, from_both, gains, fc1_1, fc2_1, merge_gain.reshape(4, C), merge,
    )
    return merged.reshape(3, 6, LEVELS, 2 * C).transpose(2, 0, 1, 3)


def solution(mesh):
    return jax.shard_map(
        shards,
        mesh=mesh,
        in_specs=(
            P(None, "lat", "lon", None),
            P(),
            P(),
            P(),
            P(),
            P(),
            P(),
            P(None, "lat", None, "lon"),
            P(),
            P(),
        ),
        out_specs=P(None, "lat", "lon", None),
        check_vma=False,
    )
```

```python
import functools

import jax
import jax.numpy as jnp
import numpy as np
from jax import lax
from jax.experimental import pallas as pl
from jax.experimental.pallas import tpu as pltpu
from jax.sharding import PartitionSpec as P

BF16 = jnp.bfloat16
F32 = jnp.float32
C = 192
HEADS = 6
HEAD_SIZE = 32
HIDDEN = 768
LEVELS, ROWS, COLS = 8, 6, 12
WINDOWS = 4
TOKENS = 144
CELLS = 576
RUN = 24
SPAN = 23
HALF = 6 * SPAN
GROUP = 128
KEYS = 2 * GROUP
LATS, LONS = 8, 16
SHARD = 1242
SHIFT = 12.0
MASKED = -1e30


def one_hot(sources, width):
    sources = np.asarray(sources)
    matrix = np.zeros((len(sources), width), np.float32)
    rows = np.nonzero(sources >= 0)[0]
    matrix[rows, sources[rows]] = 1.0
    return jnp.asarray(matrix, BF16)


ROW_HALF = (1, 0, 1, 0)


def own_half(quarter):
    odd = lax.rem(lax.axis_index("lat"), 2)
    return (1 - odd, odd, odd, 1 - odd)[quarter]


def window_half(quarter):
    odd = lax.rem(lax.axis_index("lat"), 2)
    return (odd, odd, 1 - odd, 1 - odd)[quarter]


def query_order():
    return [level * 72 + c * 6 + r for c in range(COLS) for level in range(2) for r in range(ROWS)]


def natural_order():
    return [c * 12 + level * 6 + r for level in range(2) for c in range(COLS) for r in range(ROWS)]


def quarter_runs(qr, qc):
    starts = [qc * (6 * ROWS * LEVELS) + (c * ROWS + 3 * qr) * LEVELS for c in range(6)]
    return [pl.ds(pl.multiple_of(start, LEVELS), RUN) for start in starts]


def level_cells(level):
    return pl.ds(level, ROWS * COLS, stride=LEVELS)


def read_window(cells, first_level):
    parts = [
        jnp.concatenate([cells[0, level_cells(level % LEVELS)], cells[1, level_cells(level % LEVELS)]], axis=1)
        for level in (first_level, first_level + 1)
    ]
    return jnp.concatenate(parts, axis=0)[:, :C]


def write_window(cells, first_level, values):
    wide = jnp.concatenate([values, jnp.zeros((TOKENS, 2 * GROUP - C), F32)], axis=1)
    for offset in range(2):
        rows = wide[offset * 72 : (offset + 1) * 72]
        where = level_cells((first_level + offset) % LEVELS)
        cells[0, where] = rows[:, :GROUP]
        cells[1, where] = rows[:, GROUP:]


def read_quarter(cells, qr, qc):
    parts = [jnp.concatenate([cells[0, run, :], cells[1, run, :]], axis=1) for run in quarter_runs(qr, qc)]
    return jnp.concatenate(parts, axis=0)[:, :C]


def write_quarter(cells, qr, qc, values):
    wide = jnp.concatenate([values, jnp.zeros((TOKENS, 2 * GROUP - C), F32)], axis=1)
    for c, run in enumerate(quarter_runs(qr, qc)):
        cells[0, run, :] = wide[c * RUN : (c + 1) * RUN, :GROUP]
        cells[1, run, :] = wide[c * RUN : (c + 1) * RUN, GROUP:]


def layer_norm(values, scales):
    average = jnp.mean(values, axis=-1, keepdims=True)
    centred = values - average
    spread = jnp.mean(centred * centred, axis=-1, keepdims=True)
    return centred * lax.rsqrt(spread + 1e-05) * scales


def dot(a, b):
    return jnp.dot(a, b, preferred_element_type=F32)


def dot_transposed(a, b):
    return lax.dot_general(a, b, (((1,), (1,)), ((), ())), preferred_element_type=F32)


def moved(choice, rows):
    return dot(choice, rows).astype(BF16)


def head_lanes(head):
    lane = lax.broadcasted_iota(jnp.int32, (1, C), 1)
    return (lane >= head * HEAD_SIZE) & (lane < (head + 1) * HEAD_SIZE)


def project(normed, qkv_weight, orders):
    queries = moved(orders[0], dot(normed, qkv_weight[:, :C]).astype(BF16))
    pad = jnp.zeros((GROUP - 72, C), F32)

    def padded(part):
        return jnp.concatenate([part[:72], pad, part[72:], pad], axis=0).astype(BF16)

    keys = padded(dot(normed, qkv_weight[:, C : 2 * C]))
    values = padded(dot(normed, qkv_weight[:, 2 * C :]))
    ones = jnp.ones((KEYS, KEYS - C), BF16)
    return queries, keys, jnp.concatenate([values, ones], axis=1)


def score(queries, keys):
    stacked = jnp.concatenate(
        [jnp.where(head_lanes(h), queries, jnp.zeros((), BF16)) for h in range(HEADS)], axis=0
    )
    return dot_transposed(stacked, keys) * HEAD_SIZE ** (-0.5)


def blend(scores, values, bias_of):
    weights = []
    for h in range(HEADS):
        part = scores[h * TOKENS : (h + 1) * TOKENS] + bias_of(h)
        weights.append(jnp.exp(part).astype(BF16))
    blended = dot(jnp.concatenate(weights, axis=0), values)
    total = jnp.zeros((TOKENS, C), F32)
    result = jnp.zeros((TOKENS, C), F32)
    for h in range(HEADS):
        part = blended[h * TOKENS : (h + 1) * TOKENS]
        result = jnp.where(head_lanes(h), part[:, :C], result)
        total = jnp.where(head_lanes(h), part[:, C : C + 1], total)
    return (result / jnp.maximum(total, np.exp(-SHIFT))).astype(BF16)


def selected_bias(z_even, z_odd, window, head):
    rows = []
    for at in range(6):
        lanes = slice(at * GROUP, (at + 1) * GROUP)
        halves = []
        for key_level in range(2):
            first = head * 128 + (key_level * 4 + window) * 16
            top = z_even[first : first + 16, lanes]
            low = z_odd[first : first + 16, lanes]
            halves.append(jnp.concatenate([top[:8], top[8:] + low[:8], low[8:]], axis=0))
        rows.append(jnp.concatenate(halves, axis=1))
    return jnp.concatenate(rows, axis=0)


def window_lanes(tile, first):
    turn = (GROUP - first) % GROUP
    near = pltpu.roll(tile[:, :GROUP], turn, 1) if turn else tile[:, :GROUP]
    if first + 72 <= GROUP:
        return near
    lane = lax.broadcasted_iota(jnp.int32, (1, GROUP), 1)
    return jnp.where(lane < GROUP - first, near, pltpu.roll(tile[:, GROUP:], turn, 1))


def expanded_bias(t_top, t_low, window, head):
    halves = []
    for key_level in range(2):
        first = head * 128 + (key_level * 4 + window) * 16
        top_tile, low_tile = t_top[first : first + 16], t_low[first : first + 16]
        rows = []
        for column in range(0, 12, 2):
            top = window_lanes(top_tile, (11 - column) * ROWS)
            low = window_lanes(low_tile, (10 - column) * ROWS)
            rows += [top[:8], top[8:] + low[:8], low[8:]]
        halves.append(jnp.concatenate(rows, axis=0))
    return jnp.concatenate(halves, axis=1)


def picked_rows(table_ref, table_choice):
    tops, lows = [], []
    for h in range(HEADS):
        picked = moved(table_choice, table_ref[h * 192 : (h + 1) * 192, :HALF])
        tops.append(picked[:128])
        lows.append(picked[128:])
    return jnp.concatenate(tops, axis=0), jnp.concatenate(lows, axis=0)


def erf_gelu(values):
    return 0.5 * values * (1.0 + lax.erf(values * np.float32(np.sqrt(0.5))))


def feed_forward(middle, gain, fc1, fc2, keep):
    hidden = erf_gelu(dot(layer_norm(middle, gain).astype(BF16), fc1)).astype(BF16)
    return jnp.where(keep, middle + dot_transposed(hidden, fc2), 0.0).astype(BF16)


def pack_piece(piece):
    side = jnp.concatenate(
        [piece[:80, 128:], jnp.concatenate([piece[80:, 128:], piece[:16, 128:]], axis=0)], axis=1
    )
    return jnp.concatenate([piece[:, :128], side], axis=0)


def unpack_piece(packed):
    side = packed[TOKENS:]
    ends = jnp.concatenate([side[:, :64], side[: TOKENS - 80, 64:]], axis=0)
    return jnp.concatenate([packed[:TOKENS], ends], axis=1)


def prepare_masks(lat_valid, first_mask, second_mask, keep):
    lat = lax.axis_index("lat")

    def flag(row):
        return lat_valid[row] > 0

    lane = lax.broadcasted_iota(jnp.int32, (8, KEYS), 1)
    inner = lax.rem(lane, GROUP)
    key_row = jnp.where(inner < 72, lax.rem(inner, ROWS), -1)
    mask = jnp.full((8, KEYS), MASKED, F32)
    usable = jnp.full((8, KEYS), MASKED, F32)
    for r in range(ROWS):
        mask = jnp.where((key_row == r) & flag(lat * ROWS + r), -SHIFT, mask)
        rolled = lax.rem(lat * ROWS + 3 + r, LATS * ROWS)
        usable = jnp.where((key_row == r) & flag(rolled), 0.0, usable)
    first_mask[...] = mask
    a = lax.rem(lax.broadcasted_iota(jnp.int32, (TOKENS, 1), 0), 12)
    query_half = jnp.where(lax.rem(a, ROWS) >= 3, 1, 0)
    key_half = jnp.where(key_row[:1] >= 3, 1, 0)
    same_rows = (query_half == key_half) | (lat != LATS - 1)
    same_level = jnp.where(a >= ROWS, 1, 0) == jnp.where(lane[:1] >= GROUP, 1, 0)
    whole = jnp.where(same_rows, usable[:1], MASKED)
    second_mask[0] = whole
    second_mask[1] = jnp.where(same_level, whole, MASKED)
    for half in range(2):
        for r in range(3):
            value = jnp.where(flag(lat * ROWS + 3 * half + r), 1.0, 0.0)
            for c in range(6):
                at = (c * 3 + r) * LEVELS
                keep[half, at : at + LEVELS] = jnp.full((LEVELS, GROUP), value, F32)


def fetch(sources, held, sems):
    copies = [pltpu.make_async_copy(a, b, sems.at[n]) for n, (a, b) in enumerate(zip(sources, held))]
    for copy in copies:
        copy.start()
    return copies


def sliced(kernel, layers, *refs):
    kernel(*[ref.at[layers[at]] if at in layers else ref for at, ref in enumerate(refs)])


def fetch_kernel(*refs):
    sources, held, (first_mask, second_mask, keep, flags, sems) = refs[:6], refs[6:11], refs[11:]
    copies = fetch(sources, (flags,) + tuple(held), sems)
    copies[0].wait()
    prepare_masks(flags, first_mask, second_mask, keep)
    for copy in copies[1:]:
        copy.wait()


def choose(row_keys, lane_keys):
    return jnp.where(row_keys == lane_keys, 1.0, 0.0).astype(BF16)


def prepare_kernel(mine, proj, fc1, fc2, *refs):
    copies = fetch((proj, fc1, fc2), refs[:3], refs[-1])
    lanes, rows, columns = refs[3:6]

    def place(shape, axis):
        return lax.broadcasted_iota(jnp.int32, shape, axis)

    at = place((HALF, 1), 0)
    row, position = at // SPAN, lax.rem(at, SPAN)
    lanes[...] = choose(position * ROWS + row, place((HALF, KEYS), 1))
    at = place((256, 1), 0)
    a = lax.rem(at, 16) - 4 * (at // 128)
    source = (a * 2 + lax.rem(at // 64, 2)) * 8 + lax.rem(at // 16, 4)
    for block in range(2):
        rows[block] = choose(jnp.where((a >= 0) & (a < 12), source + 4 * block, -1), place((256, 192), 1))
    lane = place((1, 6 * GROUP), 1)
    inner = lax.rem(lane, GROUP)
    for parity in range(2):
        met = inner // ROWS - (lane // GROUP * 2 + parity) + 11
        wanted = jnp.where(inner < 72, met * ROWS + lax.rem(inner, ROWS), -1)
        columns[parity] = choose(position * ROWS + row, wanted)
    for copy in copies:
        copy.wait()


def join_kernel(*refs):
    at = 0
    for ref in refs[:-1]:
        if ref.shape[1:] == refs[-1].shape[1:]:
            refs[-1][at : at + ref.shape[0]] = ref[...]
            at += ref.shape[0]


def before_kernel(halves, x, gains, qkv_weight, query_choice, *refs):
    sources, (scores_out, v_out, cells), held, sems = refs[:5], refs[5:8], refs[8:13], refs[13]
    copies = fetch(sources, held, sems)
    wide = jnp.concatenate([x[...].astype(F32), jnp.zeros((CELLS, 2 * GROUP - C), F32)], axis=1)
    for r in range(ROWS):
        for c in range(COLS):
            group = wide[(r * COLS + c) * LEVELS : (r * COLS + c + 1) * LEVELS]
            at = (c * ROWS + r) * LEVELS
            cells[0, at : at + LEVELS] = group[:, :GROUP]
            cells[1, at : at + LEVELS] = group[:, GROUP:]
    for p in range(WINDOWS):
        normed = layer_norm(read_window(cells, 2 * p), gains[0, 0:1]).astype(BF16)
        q, k, v_out[p] = project(normed, qkv_weight[...], query_choice)
        scores_out[p] = score(q, k)
    for copy in copies:
        copy.wait()


def first_quarter(quarter, inputs, cells, gains, fc1, fc2, keep):
    qr, qc = ROW_HALF[quarter], own_half(quarter)
    middle = read_quarter(inputs, qr, qc) + read_quarter(cells, qr, qc).astype(BF16).astype(F32)
    return feed_forward(middle, gains[0, 1:2], fc1[...], fc2[...], keep[qr][:, :1] > 0)


def first_kernel(mine, theirs, scores, v, first_mask, keep, inputs, gains, query_choice, proj, fc1, fc2, lanes, rows, sent_lat, sent_lon, sent_both, table_out, out, cells, table_f32, t_top, t_low):
    me = lax.axis_index("lon")
    for g in range(LONS):
        slot = lax.rem(me // 2 - g // 2 + 8, 4) * 2 + jnp.where(me // 8 == g // 8, 0, 1)
        shard = jnp.where(lax.rem(me, 2) == g % 2, mine[slot], theirs[slot]).astype(F32)
        piece = jnp.concatenate([shard[0], shard[1]], axis=0)
        for n in range(9):
            at = (g * 9 + n) * 8
            table_f32[at : at + 8, :HALF] = piece[:, n * HALF : (n + 1) * HALF]
    table_out[:, :HALF] = table_f32[:, :HALF].astype(BF16)
    tops, lows = picked_rows(table_out, rows[0])
    t_top[...] = dot(tops, lanes[...])
    t_low[...] = dot(lows, lanes[...])
    mask = first_mask[0:1]
    for p in range(WINDOWS):
        blended = blend(scores[p], v[p], lambda h: expanded_bias(t_top, t_low, p, h) + mask)
        write_window(cells, 2 * p, dot(moved(query_choice[1], blended), proj[...]))
    for quarter, target in ((2, sent_lon), (3, sent_both), (1, sent_lat)):
        result = first_quarter(quarter, inputs, cells, gains, fc1, fc2, keep)
        out[(quarter - 1) * TOKENS : quarter * TOKENS] = result
        target[...] = pack_piece(result)


def bias_kernel(table, second_mask, columns, rows, inputs, cells, gains, fc1, fc2, keep, bias_out, near, z_even, z_odd):
    near[...] = first_quarter(0, inputs, cells, gains, fc1, fc2, keep)
    tops, lows = picked_rows(table, rows[1])
    z_even[...] = dot(tops, columns[0])
    z_odd[...] = dot(lows, columns[1])
    for p in range(WINDOWS):
        for h in range(HEADS):
            whole = selected_bias(z_even, z_odd, p, h) + second_mask[1 if p == WINDOWS - 1 else 0]
            bias_out[p, h * TOKENS : (h + 1) * TOKENS] = whole.astype(BF16)


def write_normed(cells, quarter, piece, gains):
    normed = layer_norm(piece.astype(F32), gains[1, 0:1]).astype(BF16)
    write_quarter(cells, 1 - ROW_HALF[quarter], window_half(quarter), normed.astype(F32))


def ready_kernel(near, from_lon, from_both, gains, cells):
    write_normed(cells, 0, near[...], gains)
    write_normed(cells, 2, unpack_piece(from_lon[...]), gains)
    write_normed(cells, 3, unpack_piece(from_both[...]), gains)


def second_kernel(given, from_lat, bias, gains, qkv_weight, proj, query_choice, own, sent_lat, sent_lon, sent_both, cells, results):
    cells[...] = given[...]
    write_normed(cells, 1, unpack_piece(from_lat[...]), gains)
    for p in range(WINDOWS):
        normed = read_window(cells, 2 * p + 1).astype(BF16)
        q, k, v = project(normed, qkv_weight[...], query_choice)

        def bias_of(h):
            return bias[p, h * TOKENS : (h + 1) * TOKENS].astype(F32) - SHIFT

        blended = blend(score(q, k), v, bias_of)
        write_window(results, 2 * p + 1, dot(moved(query_choice[1], blended), proj[...]))
    pieces = [read_quarter(results, 1 - ROW_HALF[k], window_half(k)).astype(BF16) for k in range(4)]
    own[...] = pieces[0]
    sent_lat[...] = pack_piece(pieces[1])
    sent_lon[...] = pack_piece(pieces[2])
    sent_both[...] = pack_piece(pieces[3])


def own_kernel(keep, near, own, gains, fc1, fc2, result):
    middle = near[...].astype(F32) + own[...].astype(F32)
    result[...] = feed_forward(middle, gains[1, 1:2], fc1[...], fc2[...], keep[1][:, :1] > 0)


def add_kernel(far, from_lon, from_both, middle):
    for at, piece in enumerate((from_lon, from_both)):
        inputs = far[(at + 1) * TOKENS : (at + 2) * TOKENS].astype(F32)
        middle[at] = inputs + unpack_piece(piece[...]).astype(F32)


def last_kernel(keep, far, done, middle, from_lat, gains, fc1, fc2, merge_gain, merge_weight, merged):
    results = [done[...].astype(F32)]
    upper = far[:TOKENS].astype(F32) + unpack_piece(from_lat[...]).astype(F32)
    for quarter, whole in ((1, upper), (2, middle[0]), (3, middle[1])):
        flags = keep[ROW_HALF[quarter]][:, :1] > 0
        results.append(feed_forward(whole, gains[1, 1:2], fc1[...], fc2[...], flags).astype(F32))
    odd = lax.rem(lax.axis_index("lat"), 2) == 1
    groups = {}
    for qr, (first, second) in enumerate(((1, 3), (0, 2))):
        turned_round = odd if qr == 1 else jnp.logical_not(odd)
        right = jnp.where(turned_round, results[second], results[first])
        left = jnp.where(turned_round, results[first], results[second])
        for qc, result in enumerate((left, right)):
            for r in range(3):
                for c in range(6):
                    at = (c * 3 + r) * LEVELS
                    groups[3 * qr + r, 6 * qc + c] = result[at : at + LEVELS]
    parts = [
        jnp.concatenate([groups[2 * r + dr, 2 * c + dc] for r in range(3) for c in range(6)], axis=0)
        for dr in range(2)
        for dc in range(2)
    ]
    average = sum(jnp.sum(part, axis=-1, keepdims=True) for part in parts) / (4 * C)
    parts = [part - average for part in parts]
    spread = sum(jnp.sum(part * part, axis=-1, keepdims=True) for part in parts) / (4 * C)
    scale = lax.rsqrt(spread + 1e-05)
    total = jnp.zeros((TOKENS, 2 * C), F32)
    for d, part in enumerate(parts):
        normed = (part * scale * merge_gain[d : d + 1]).astype(BF16)
        total = total + dot(normed, merge_weight[d * C : (d + 1) * C])
    merged[...] = total.astype(BF16)


VMEM_SPEC = pl.BlockSpec(memory_space=pltpu.VMEM)
SMEM_SPEC = pl.BlockSpec(memory_space=pltpu.SMEM)


def call(kernel, name, micros, outs, scratch, *operands, in_specs=None, aliases=None):
    return pl.pallas_call(
        kernel,
        name=name,
        out_shape=outs,
        in_specs=in_specs or [VMEM_SPEC] * len(operands),
        out_specs=jax.tree.map(lambda _: VMEM_SPEC, outs),
        scratch_shapes=scratch,
        input_output_aliases=aliases or {},
        cost_estimate=pl.CostEstimate(flops=int(micros * 1e9), bytes_accessed=2**20, transcendentals=0),
        compiler_params=pltpu.CompilerParams(vmem_limit_bytes=16 * 2**20),
    )(*operands)


def shape(*dims, dtype=BF16):
    return jax.ShapeDtypeStruct(dims, dtype)


def sent(block, rows, across, back=False):
    route = []
    for i in range(LATS):
        for j in range(LONS):
            to = (i + rows) % LATS
            owner = i if back else to
            step = (1 if owner % 2 == 1 else -1) * (-1 if back else 1)
            route.append((i * LONS + j, to * LONS + (j + across * step) % LONS))
    return lax.ppermute(block, ("lat", "lon"), route)


def turned(block, place):
    route = []
    for j in range(LONS):
        z, x, core = place(j // 8, j // 2 % 4, j % 2)
        route.append((j, z * 8 + x * 2 + core))
    return lax.ppermute(block, "lon", route)


def shards(state, lat_valid, norm_gains, qkv_weight, proj_weight, fc1_weight, fc2_weight, earth_bias, merge_gain, merge_weight):
    shard = earth_bias[:, 0]
    cells = pltpu.VMEM((2, CELLS, GROUP), F32)
    cell_rows = shape(2, CELLS, GROUP, dtype=F32)
    t_scratch = [pltpu.VMEM((768, KEYS), F32), pltpu.VMEM((768, KEYS), F32)]
    packed = shape(224, 128)

    def in_hbm(array):
        return pltpu.with_memory_space_constraint(array, pltpu.HBM)

    def like(arrays):
        return [shape(*array.shape, dtype=array.dtype) for array in arrays]

    hbm_spec = pl.BlockSpec(memory_space=pltpu.HBM)
    fc2_turned = jnp.swapaxes(fc2_weight, 1, 2)
    early = [
        shard[None],
        state.transpose(1, 2, 0, 3).reshape(CELLS, C),
        norm_gains,
        qkv_weight,
        jnp.stack([one_hot(query_order(), TOKENS), one_hot(natural_order(), TOKENS)]),
    ]
    late = [merge_weight, qkv_weight, proj_weight, fc1_weight, fc2_turned]
    layer = [shape(C, C), shape(C, HIDDEN), shape(C, HIDDEN)]
    other_half = turned(shard, lambda z, x, core: (1 - z, x, core))
    held_shard, x, gains, qkv0, query_choice, first_mask, second_mask, keep = call(
        functools.partial(sliced, fetch_kernel, {4: 0}),
        "fetch",
        1.4,
        like(early[:3])
        + [shape(C, 3 * C)]
        + like(early[4:])
        + [
            shape(8, KEYS, dtype=F32),
            shape(2, TOKENS, KEYS, dtype=F32),
            shape(2, TOKENS, GROUP, dtype=F32),
        ],
        [pltpu.SMEM((LATS * ROWS,), jnp.int32), pltpu.SemaphoreType.DMA((len(early) + 1,))],
        in_hbm(lat_valid),
        *[in_hbm(array) for array in early],
        in_specs=[hbm_spec] * (len(early) + 1),
    )
    halves = call(join_kernel, "halves", 0.2, shape(2, 2, WINDOWS, SHARD), [], held_shard, other_half[None])
    ring = [turned(halves, lambda z, x, core: (z, (x + hop) % 4, core)) for hop in range(1, 4)]
    scores, v, inputs, merge, qkv1, proj1, fc1_1, fc2_1 = call(
        functools.partial(sliced, before_kernel, {6: 1, 7: 1, 8: 1, 9: 1}),
        "before",
        2.5,
        [shape(WINDOWS, HEADS * TOKENS, KEYS, dtype=F32), shape(WINDOWS, KEYS, KEYS), cell_rows]
        + like([merge_weight])
        + [shape(C, 3 * C)]
        + layer,
        [pltpu.SemaphoreType.DMA((len(late),))],
        halves, x, gains, qkv0, query_choice,
        *[in_hbm(array) for array in late],
        in_specs=[VMEM_SPEC] * 5 + [hbm_spec] * len(late),
    )
    mine = call(join_kernel, "mine", 0.3, shape(8, 2, WINDOWS, SHARD), [], halves, *ring, v)
    theirs = turned(mine, lambda z, x, core: (z, x, 1 - core))
    proj0, fc1_0, fc2_0, lanes, rows, columns = call(
        functools.partial(sliced, prepare_kernel, {1: 0, 2: 0, 3: 0}),
        "prepare",
        1.2,
        layer + [shape(HALF, KEYS), shape(2, 256, 192), shape(2, HALF, 6 * GROUP)],
        [pltpu.SemaphoreType.DMA((3,))],
        mine, in_hbm(proj_weight), in_hbm(fc1_weight), in_hbm(fc2_turned),
        in_specs=[VMEM_SPEC] + [hbm_spec] * 3,
    )
    to_lat, to_lon, to_both, tables, far, attended = call(
        first_kernel,
        "first",
        4.5,
        [packed, packed, packed, shape(1152, KEYS), shape(3 * TOKENS, C), cell_rows],
        [pltpu.VMEM((1152, KEYS), F32)] + t_scratch,
        mine, theirs, scores, v, first_mask, keep, inputs, gains, query_choice, proj0, fc1_0, fc2_0, lanes, rows,
    )
    from_lat, from_lon, from_both = sent(to_lat, -1, 0), sent(to_lon, 0, 1), sent(to_both, -1, 1)
    bias, near = call(
        bias_kernel,
        "bias",
        0.2,
        [shape(WINDOWS, HEADS * TOKENS, KEYS), shape(TOKENS, C)],
        [pltpu.VMEM((768, 768), F32), pltpu.VMEM((768, 768), F32)],
        tables, second_mask, columns, rows, inputs, attended, gains, fc1_0, fc2_0, keep,
    )
    ready = call(ready_kernel, "ready", 0.4, cell_rows, [], near, from_lon, from_both, gains)
    own, to_lat, to_lon, to_both = call(
        second_kernel,
        "second",
        4.5,
        [shape(TOKENS, C), packed, packed, packed],
        [cells, cells],
        ready, from_lat, bias, gains, qkv1, proj1, query_choice,
    )
    from_lon, from_both, from_lat = sent(to_lon, 0, 1, True), sent(to_both, 1, 1, True), sent(to_lat, 1, 0, True)
    done = call(own_kernel, "own", 0.5, shape(TOKENS, C), [], keep, near, own, gains, fc1_1, fc2_1)
    middle = call(
        add_kernel, "add", 0.2, shape(2, TOKENS, C, dtype=F32), [], far, from_lon, from_both
    )
    merged = call(
        last_kernel,
        "last",
        2.0,
        shape(TOKENS, 2 * C),
        [],
        keep, far, done, middle, from_lat, gains, fc1_1, fc2_1, merge_gain.reshape(4, C), merge,
    )
    return merged.reshape(3, 6, LEVELS, 2 * C).transpose(2, 0, 1, 3)


def solution(mesh):
    return jax.shard_map(
        shards,
        mesh=mesh,
        in_specs=(
            P(None, "lat", "lon", None),
            P(),
            P(),
            P(),
            P(),
            P(),
            P(),
            P(None, "lat", None, "lon"),
            P(),
            P(),
        ),
        out_specs=P(None, "lat", "lon", None),
        check_vma=False,
    )
```

```python
import functools

import jax
import jax.numpy as jnp
import numpy as np
from jax import lax
from jax.experimental import pallas as pl
from jax.experimental.pallas import tpu as pltpu
from jax.sharding import PartitionSpec as P

BF16 = jnp.bfloat16
F32 = jnp.float32
C = 192
HEADS = 6
HEAD_SIZE = 32
HIDDEN = 768
LEVELS, ROWS, COLS = 8, 6, 12
WINDOWS = 4
TOKENS = 144
CELLS = 576
RUN = 24
SPAN = 23
HALF = 6 * SPAN
GROUP = 128
KEYS = 2 * GROUP
LATS, LONS = 8, 16
SHARD = 1242
SHIFT = 12.0
MASKED = -1e30


def one_hot(sources, width):
    sources = np.asarray(sources)
    matrix = np.zeros((len(sources), width), np.float32)
    rows = np.nonzero(sources >= 0)[0]
    matrix[rows, sources[rows]] = 1.0
    return jnp.asarray(matrix, BF16)


ROW_HALF = (1, 0, 1, 0)


def own_half(quarter):
    odd = lax.rem(lax.axis_index("lat"), 2)
    return (1 - odd, odd, odd, 1 - odd)[quarter]


def window_half(quarter):
    odd = lax.rem(lax.axis_index("lat"), 2)
    return (odd, odd, 1 - odd, 1 - odd)[quarter]


def query_order():
    return [level * 72 + c * 6 + r for c in range(COLS) for level in range(2) for r in range(ROWS)]


def natural_order():
    return [c * 12 + level * 6 + r for level in range(2) for c in range(COLS) for r in range(ROWS)]


def quarter_runs(qr, qc):
    starts = [qc * (6 * ROWS * LEVELS) + (c * ROWS + 3 * qr) * LEVELS for c in range(6)]
    return [pl.ds(pl.multiple_of(start, LEVELS), RUN) for start in starts]


def level_cells(level):
    return pl.ds(level, ROWS * COLS, stride=LEVELS)


def read_window(cells, first_level):
    parts = [
        jnp.concatenate([cells[0, level_cells(level % LEVELS)], cells[1, level_cells(level % LEVELS)]], axis=1)
        for level in (first_level, first_level + 1)
    ]
    return jnp.concatenate(parts, axis=0)[:, :C]


def write_window(cells, first_level, values):
    wide = jnp.concatenate([values, jnp.zeros((TOKENS, 2 * GROUP - C), F32)], axis=1)
    for offset in range(2):
        rows = wide[offset * 72 : (offset + 1) * 72]
        where = level_cells((first_level + offset) % LEVELS)
        cells[0, where] = rows[:, :GROUP]
        cells[1, where] = rows[:, GROUP:]


def read_quarter(cells, qr, qc):
    parts = [jnp.concatenate([cells[0, run, :], cells[1, run, :]], axis=1) for run in quarter_runs(qr, qc)]
    return jnp.concatenate(parts, axis=0)[:, :C]


def write_quarter(cells, qr, qc, values):
    wide = jnp.concatenate([values, jnp.zeros((TOKENS, 2 * GROUP - C), F32)], axis=1)
    for c, run in enumerate(quarter_runs(qr, qc)):
        cells[0, run, :] = wide[c * RUN : (c + 1) * RUN, :GROUP]
        cells[1, run, :] = wide[c * RUN : (c + 1) * RUN, GROUP:]


def layer_norm(values, scales):
    average = jnp.mean(values, axis=-1, keepdims=True)
    centred = values - average
    spread = jnp.mean(centred * centred, axis=-1, keepdims=True)
    return centred * lax.rsqrt(spread + 1e-05) * scales


def dot(a, b):
    return jnp.dot(a, b, preferred_element_type=F32)


def dot_transposed(a, b):
    return lax.dot_general(a, b, (((1,), (1,)), ((), ())), preferred_element_type=F32)


def moved(choice, rows):
    return dot(choice, rows).astype(BF16)


def head_lanes(head):
    lane = lax.broadcasted_iota(jnp.int32, (1, C), 1)
    return (lane >= head * HEAD_SIZE) & (lane < (head + 1) * HEAD_SIZE)


def project(normed, qkv_weight, orders):
    all_queries = dot(normed, qkv_weight[:, :C]).astype(BF16)
    all_keys = dot(normed, qkv_weight[:, C : 2 * C])
    all_values = dot(normed, qkv_weight[:, 2 * C :])
    pad = jnp.zeros((GROUP - 72, C), F32)
    ones = jnp.ones((KEYS, KEYS - C), BF16)

    def padded(part):
        return jnp.concatenate([part[:72], pad, part[72:], pad], axis=0).astype(BF16)

    results = []
    for p in range(WINDOWS):
        rows = slice(p * TOKENS, (p + 1) * TOKENS)
        values = jnp.concatenate([padded(all_values[rows]), ones], axis=1)
        results.append((moved(orders[0], all_queries[rows]), padded(all_keys[rows]), values))
    return results


def write_attended(cells, first_level, blended, orders, proj):
    natural = jnp.concatenate([moved(orders[1], part) for part in blended], axis=0)
    attended = dot(natural, proj)
    for p in range(WINDOWS):
        write_window(cells, 2 * p + first_level, attended[p * TOKENS : (p + 1) * TOKENS])


def score(queries, keys):
    stacked = jnp.concatenate(
        [jnp.where(head_lanes(h), queries, jnp.zeros((), BF16)) for h in range(HEADS)], axis=0
    )
    return dot_transposed(stacked, keys) * HEAD_SIZE ** (-0.5)


def blend(scores, values, bias_of):
    weights = []
    for h in range(HEADS):
        part = scores[h * TOKENS : (h + 1) * TOKENS] + bias_of(h)
        weights.append(jnp.exp(part).astype(BF16))
    blended = dot(jnp.concatenate(weights, axis=0), values)
    total = jnp.zeros((TOKENS, C), F32)
    result = jnp.zeros((TOKENS, C), F32)
    for h in range(HEADS):
        part = blended[h * TOKENS : (h + 1) * TOKENS]
        result = jnp.where(head_lanes(h), part[:, :C], result)
        total = jnp.where(head_lanes(h), part[:, C : C + 1], total)
    return (result / jnp.maximum(total, np.exp(-SHIFT))).astype(BF16)


def selected_bias(z_even, z_odd, window, head):
    rows = []
    for at in range(6):
        lanes = slice(at * GROUP, (at + 1) * GROUP)
        halves = []
        for key_level in range(2):
            first = head * 128 + (key_level * 4 + window) * 16
            top = z_even[first : first + 16, lanes]
            low = z_odd[first : first + 16, lanes]
            halves.append(jnp.concatenate([top[:8], top[8:] + low[:8], low[8:]], axis=0))
        rows.append(jnp.concatenate(halves, axis=1))
    return jnp.concatenate(rows, axis=0)


def window_lanes(tile, first):
    turn = (GROUP - first) % GROUP
    near = pltpu.roll(tile[:, :GROUP], turn, 1) if turn else tile[:, :GROUP]
    if first + 72 <= GROUP:
        return near
    lane = lax.broadcasted_iota(jnp.int32, (1, GROUP), 1)
    return jnp.where(lane < GROUP - first, near, pltpu.roll(tile[:, GROUP:], turn, 1))


def expanded_bias(t_top, t_low, window, head):
    halves = []
    for key_level in range(2):
        first = head * 128 + (key_level * 4 + window) * 16
        top_tile, low_tile = t_top[first : first + 16], t_low[first : first + 16]
        rows = []
        for column in range(0, 12, 2):
            top = window_lanes(top_tile, (11 - column) * ROWS)
            low = window_lanes(low_tile, (10 - column) * ROWS)
            rows += [top[:8], top[8:] + low[:8], low[8:]]
        halves.append(jnp.concatenate(rows, axis=0))
    return jnp.concatenate(halves, axis=1)


def picked_rows(table_ref, table_choice):
    tops, lows = [], []
    for h in range(HEADS):
        picked = moved(table_choice, table_ref[h * 192 : (h + 1) * 192, :HALF])
        tops.append(picked[:128])
        lows.append(picked[128:])
    return jnp.concatenate(tops, axis=0), jnp.concatenate(lows, axis=0)


def erf_gelu(values):
    return 0.5 * values * (1.0 + lax.erf(values * np.float32(np.sqrt(0.5))))


def feed_forward(middle, gain, fc1, fc2, keep):
    hidden = erf_gelu(dot(layer_norm(middle, gain).astype(BF16), fc1)).astype(BF16)
    return jnp.where(keep, middle + dot_transposed(hidden, fc2), 0.0).astype(BF16)


def finished(quarters, middle, gain, fc1, fc2, keep):
    flags = jnp.concatenate([keep[ROW_HALF[quarter]][:, :1] for quarter in quarters], axis=0) > 0
    return feed_forward(jnp.concatenate(middle, axis=0), gain, fc1[...], fc2[...], flags)


def pack_piece(piece):
    side = jnp.concatenate(
        [piece[:80, 128:], jnp.concatenate([piece[80:, 128:], piece[:16, 128:]], axis=0)], axis=1
    )
    return jnp.concatenate([piece[:, :128], side], axis=0)


def unpack_piece(packed):
    side = packed[TOKENS:]
    ends = jnp.concatenate([side[:, :64], side[: TOKENS - 80, 64:]], axis=0)
    return jnp.concatenate([packed[:TOKENS], ends], axis=1)


def prepare_masks(lat_valid, first_mask, second_mask, keep):
    lat = lax.axis_index("lat")

    def flag(row):
        return lat_valid[row] > 0

    lane = lax.broadcasted_iota(jnp.int32, (8, KEYS), 1)
    inner = lax.rem(lane, GROUP)
    key_row = jnp.where(inner < 72, lax.rem(inner, ROWS), -1)
    mask = jnp.full((8, KEYS), MASKED, F32)
    usable = jnp.full((8, KEYS), MASKED, F32)
    for r in range(ROWS):
        mask = jnp.where((key_row == r) & flag(lat * ROWS + r), -SHIFT, mask)
        rolled = lax.rem(lat * ROWS + 3 + r, LATS * ROWS)
        usable = jnp.where((key_row == r) & flag(rolled), 0.0, usable)
    first_mask[...] = mask
    a = lax.rem(lax.broadcasted_iota(jnp.int32, (TOKENS, 1), 0), 12)
    query_half = jnp.where(lax.rem(a, ROWS) >= 3, 1, 0)
    key_half = jnp.where(key_row[:1] >= 3, 1, 0)
    same_rows = (query_half == key_half) | (lat != LATS - 1)
    same_level = jnp.where(a >= ROWS, 1, 0) == jnp.where(lane[:1] >= GROUP, 1, 0)
    whole = jnp.where(same_rows, usable[:1], MASKED)
    second_mask[0] = whole
    second_mask[1] = jnp.where(same_level, whole, MASKED)
    for half in range(2):
        for r in range(3):
            value = jnp.where(flag(lat * ROWS + 3 * half + r), 1.0, 0.0)
            for c in range(6):
                at = (c * 3 + r) * LEVELS
                keep[half, at : at + LEVELS] = jnp.full((LEVELS, GROUP), value, F32)


def fetch(sources, held, sems):
    copies = [pltpu.make_async_copy(a, b, sems.at[n]) for n, (a, b) in enumerate(zip(sources, held))]
    for copy in copies:
        copy.start()
    return copies


def sliced(kernel, layers, *refs):
    kernel(*[ref.at[layers[at]] if at in layers else ref for at, ref in enumerate(refs)])


def fetch_kernel(*refs):
    sources, held, (first_mask, second_mask, keep, flags, sems) = refs[:6], refs[6:11], refs[11:]
    copies = fetch(sources, (flags,) + tuple(held), sems)
    copies[0].wait()
    prepare_masks(flags, first_mask, second_mask, keep)
    for copy in copies[1:]:
        copy.wait()


def choose(row_keys, lane_keys):
    return jnp.where(row_keys == lane_keys, 1.0, 0.0).astype(BF16)


def prepare_kernel(mine, proj, fc1, fc2, *refs):
    copies = fetch((proj, fc1, fc2), refs[:3], refs[-1])
    lanes, rows, columns = refs[3:6]

    def place(shape, axis):
        return lax.broadcasted_iota(jnp.int32, shape, axis)

    at = place((HALF, 1), 0)
    row, position = at // SPAN, lax.rem(at, SPAN)
    lanes[...] = choose(position * ROWS + row, place((HALF, KEYS), 1))
    at = place((256, 1), 0)
    a = lax.rem(at, 16) - 4 * (at // 128)
    source = (a * 2 + lax.rem(at // 64, 2)) * 8 + lax.rem(at // 16, 4)
    for block in range(2):
        rows[block] = choose(jnp.where((a >= 0) & (a < 12), source + 4 * block, -1), place((256, 192), 1))
    lane = place((1, 6 * GROUP), 1)
    inner = lax.rem(lane, GROUP)
    for parity in range(2):
        met = inner // ROWS - (lane // GROUP * 2 + parity) + 11
        wanted = jnp.where(inner < 72, met * ROWS + lax.rem(inner, ROWS), -1)
        columns[parity] = choose(position * ROWS + row, wanted)
    for copy in copies:
        copy.wait()


def join_kernel(*refs):
    at = 0
    for ref in refs[:-1]:
        if ref.shape[1:] == refs[-1].shape[1:]:
            refs[-1][at : at + ref.shape[0]] = ref[...]
            at += ref.shape[0]


def before_kernel(halves, x, gains, qkv_weight, query_choice, *refs):
    sources, (scores_out, v_out, cells), held, sems = refs[:2], refs[2:5], refs[5:7], refs[7]
    copies = fetch(sources, held, sems)
    wide = jnp.concatenate([x[...].astype(F32), jnp.zeros((CELLS, 2 * GROUP - C), F32)], axis=1)
    for r in range(ROWS):
        for c in range(COLS):
            group = wide[(r * COLS + c) * LEVELS : (r * COLS + c + 1) * LEVELS]
            at = (c * ROWS + r) * LEVELS
            cells[0, at : at + LEVELS] = group[:, :GROUP]
            cells[1, at : at + LEVELS] = group[:, GROUP:]
    windows = jnp.concatenate([read_window(cells, 2 * p) for p in range(WINDOWS)], axis=0)
    normed = layer_norm(windows, gains[0, 0:1]).astype(BF16)
    for p, (q, k, v) in enumerate(project(normed, qkv_weight[...], query_choice)):
        v_out[p] = v
        scores_out[p] = score(q, k)
    for copy in copies:
        copy.wait()


def first_quarters(quarters, inputs, cells, gains, fc1, fc2, keep):
    middle = []
    for quarter in quarters:
        qr, qc = ROW_HALF[quarter], own_half(quarter)
        middle.append(read_quarter(inputs, qr, qc) + read_quarter(cells, qr, qc).astype(BF16).astype(F32))
    return finished(quarters, middle, gains[0, 1:2], fc1, fc2, keep)


def first_kernel(mine, theirs, scores, v, first_mask, keep, inputs, gains, query_choice, proj, fc1, fc2, lanes, rows, sent_lat, sent_lon, sent_both, table_out, out, cells, table_f32, t_top, t_low):
    me = lax.axis_index("lon")
    for g in range(LONS):
        slot = lax.rem(me // 2 - g // 2 + 8, 4) * 2 + jnp.where(me // 8 == g // 8, 0, 1)
        shard = jnp.where(lax.rem(me, 2) == g % 2, mine[slot], theirs[slot]).astype(F32)
        piece = jnp.concatenate([shard[0], shard[1]], axis=0)
        for n in range(9):
            at = (g * 9 + n) * 8
            table_f32[at : at + 8, :HALF] = piece[:, n * HALF : (n + 1) * HALF]
    table_out[:, :HALF] = table_f32[:, :HALF].astype(BF16)
    tops, lows = picked_rows(table_out, rows[0])
    t_top[...] = dot(tops, lanes[...])
    t_low[...] = dot(lows, lanes[...])
    mask = first_mask[0:1]
    blended = [blend(scores[p], v[p], lambda h: expanded_bias(t_top, t_low, p, h) + mask) for p in range(WINDOWS)]
    write_attended(cells, 0, blended, query_choice, proj[...])
    results = first_quarters((1, 2, 3), inputs, cells, gains, fc1, fc2, keep)
    out[...] = results
    for at, target in enumerate((sent_lat, sent_lon, sent_both)):
        target[...] = pack_piece(results[at * TOKENS : (at + 1) * TOKENS])


def bias_kernel(table, second_mask, columns, rows, inputs, cells, gains, fc1, fc2, keep, bias_out, near, z_even, z_odd):
    near[...] = first_quarters((0,), inputs, cells, gains, fc1, fc2, keep)
    tops, lows = picked_rows(table, rows[1])
    z_even[...] = dot(tops, columns[0])
    z_odd[...] = dot(lows, columns[1])
    for p in range(WINDOWS):
        for h in range(HEADS):
            whole = selected_bias(z_even, z_odd, p, h) + second_mask[1 if p == WINDOWS - 1 else 0]
            bias_out[p, h * TOKENS : (h + 1) * TOKENS] = whole.astype(BF16)


def write_normed(cells, quarter, piece, gains):
    normed = layer_norm(piece.astype(F32), gains[1, 0:1]).astype(BF16)
    write_quarter(cells, 1 - ROW_HALF[quarter], window_half(quarter), normed.astype(F32))


def ready_kernel(near, from_lon, from_both, gains, cells):
    write_normed(cells, 0, near[...], gains)
    write_normed(cells, 2, unpack_piece(from_lon[...]), gains)
    write_normed(cells, 3, unpack_piece(from_both[...]), gains)


def second_kernel(given, from_lat, bias, gains, qkv_weight, proj, query_choice, own, sent_lat, sent_lon, sent_both, cells, results):
    cells[...] = given[...]
    write_normed(cells, 1, unpack_piece(from_lat[...]), gains)
    normed = jnp.concatenate([read_window(cells, 2 * p + 1) for p in range(WINDOWS)], axis=0).astype(BF16)
    blended = []
    for p, (q, k, v) in enumerate(project(normed, qkv_weight[...], query_choice)):

        def bias_of(h):
            return bias[p, h * TOKENS : (h + 1) * TOKENS].astype(F32) - SHIFT

        blended.append(blend(score(q, k), v, bias_of))
    write_attended(results, 1, blended, query_choice, proj[...])
    pieces = [read_quarter(results, 1 - ROW_HALF[k], window_half(k)).astype(BF16) for k in range(4)]
    own[...] = pieces[0]
    sent_lat[...] = pack_piece(pieces[1])
    sent_lon[...] = pack_piece(pieces[2])
    sent_both[...] = pack_piece(pieces[3])


def own_kernel(fc1, fc2, merge, keep, near, own, gains, result, *refs):
    copies = fetch((fc1, fc2, merge), refs[:3], refs[3])
    middle = near[...].astype(F32) + own[...].astype(F32)
    for copy in copies:
        copy.wait()
    result[...] = feed_forward(middle, gains[1, 1:2], refs[0][...], refs[1][...], keep[1][:, :1] > 0)


def add_kernel(far, from_lon, from_both, middle):
    for at, piece in enumerate((from_lon, from_both)):
        inputs = far[(at + 1) * TOKENS : (at + 2) * TOKENS].astype(F32)
        middle[at] = inputs + unpack_piece(piece[...]).astype(F32)


def last_kernel(keep, far, done, middle, from_lat, gains, fc1, fc2, merge_gain, merge_weight, merged):
    upper = far[:TOKENS].astype(F32) + unpack_piece(from_lat[...]).astype(F32)
    fresh = finished((1, 2, 3), [upper, middle[0], middle[1]], gains[1, 1:2], fc1, fc2, keep).astype(F32)
    results = [done[...].astype(F32)] + [fresh[at * TOKENS : (at + 1) * TOKENS] for at in range(3)]
    odd = lax.rem(lax.axis_index("lat"), 2) == 1
    groups = {}
    for qr, (first, second) in enumerate(((1, 3), (0, 2))):
        turned_round = odd if qr == 1 else jnp.logical_not(odd)
        right = jnp.where(turned_round, results[second], results[first])
        left = jnp.where(turned_round, results[first], results[second])
        for qc, result in enumerate((left, right)):
            for r in range(3):
                for c in range(6):
                    at = (c * 3 + r) * LEVELS
                    groups[3 * qr + r, 6 * qc + c] = result[at : at + LEVELS]
    parts = [
        jnp.concatenate([groups[2 * r + dr, 2 * c + dc] for r in range(3) for c in range(6)], axis=0)
        for dr in range(2)
        for dc in range(2)
    ]
    average = sum(jnp.sum(part, axis=-1, keepdims=True) for part in parts) / (4 * C)
    parts = [part - average for part in parts]
    spread = sum(jnp.sum(part * part, axis=-1, keepdims=True) for part in parts) / (4 * C)
    scale = lax.rsqrt(spread + 1e-05)
    total = jnp.zeros((TOKENS, 2 * C), F32)
    for d, part in enumerate(parts):
        normed = (part * scale * merge_gain[d : d + 1]).astype(BF16)
        total = total + dot(normed, merge_weight[d * C : (d + 1) * C])
    merged[...] = total.astype(BF16)


VMEM_SPEC = pl.BlockSpec(memory_space=pltpu.VMEM)
SMEM_SPEC = pl.BlockSpec(memory_space=pltpu.SMEM)


def call(kernel, name, micros, outs, scratch, *operands, in_specs=None, aliases=None):
    return pl.pallas_call(
        kernel,
        name=name,
        out_shape=outs,
        in_specs=in_specs or [VMEM_SPEC] * len(operands),
        out_specs=jax.tree.map(lambda _: VMEM_SPEC, outs),
        scratch_shapes=scratch,
        input_output_aliases=aliases or {},
        cost_estimate=pl.CostEstimate(flops=int(micros * 1e9), bytes_accessed=2**20, transcendentals=0),
        compiler_params=pltpu.CompilerParams(vmem_limit_bytes=16 * 2**20),
    )(*operands)


def shape(*dims, dtype=BF16):
    return jax.ShapeDtypeStruct(dims, dtype)


def sent(block, rows, across, back=False):
    route = []
    for i in range(LATS):
        for j in range(LONS):
            to = (i + rows) % LATS
            owner = i if back else to
            step = (1 if owner % 2 == 1 else -1) * (-1 if back else 1)
            route.append((i * LONS + j, to * LONS + (j + across * step) % LONS))
    return lax.ppermute(block, ("lat", "lon"), route)


def turned(block, place):
    route = []
    for j in range(LONS):
        z, x, core = place(j // 8, j // 2 % 4, j % 2)
        route.append((j, z * 8 + x * 2 + core))
    return lax.ppermute(block, "lon", route)


def shards(state, lat_valid, norm_gains, qkv_weight, proj_weight, fc1_weight, fc2_weight, earth_bias, merge_gain, merge_weight):
    shard = earth_bias[:, 0]
    cells = pltpu.VMEM((2, CELLS, GROUP), F32)
    cell_rows = shape(2, CELLS, GROUP, dtype=F32)
    t_scratch = [pltpu.VMEM((768, KEYS), F32), pltpu.VMEM((768, KEYS), F32)]
    packed = shape(224, 128)

    def in_hbm(array):
        return pltpu.with_memory_space_constraint(array, pltpu.HBM)

    def like(arrays):
        return [shape(*array.shape, dtype=array.dtype) for array in arrays]

    hbm_spec = pl.BlockSpec(memory_space=pltpu.HBM)
    fc2_turned = jnp.swapaxes(fc2_weight, 1, 2)
    early = [
        shard[None],
        state.transpose(1, 2, 0, 3).reshape(CELLS, C),
        norm_gains,
        qkv_weight,
        jnp.stack([one_hot(query_order(), TOKENS), one_hot(natural_order(), TOKENS)]),
    ]
    late = [qkv_weight, proj_weight]
    layer = [shape(C, C), shape(C, HIDDEN), shape(C, HIDDEN)]
    other_half = turned(shard, lambda z, x, core: (1 - z, x, core))
    held_shard, x, gains, qkv0, query_choice, first_mask, second_mask, keep = call(
        functools.partial(sliced, fetch_kernel, {4: 0}),
        "fetch",
        1.4,
        like(early[:3])
        + [shape(C, 3 * C)]
        + like(early[4:])
        + [
            shape(8, KEYS, dtype=F32),
            shape(2, TOKENS, KEYS, dtype=F32),
            shape(2, TOKENS, GROUP, dtype=F32),
        ],
        [pltpu.SMEM((LATS * ROWS,), jnp.int32), pltpu.SemaphoreType.DMA((len(early) + 1,))],
        in_hbm(lat_valid),
        *[in_hbm(array) for array in early],
        in_specs=[hbm_spec] * (len(early) + 1),
    )
    halves = call(join_kernel, "halves", 0.2, shape(2, 2, WINDOWS, SHARD), [], held_shard, other_half[None])
    ring = [turned(halves, lambda z, x, core: (z, (x + hop) % 4, core)) for hop in range(1, 4)]
    scores, v, inputs, qkv1, proj1 = call(
        functools.partial(sliced, before_kernel, {5: 1, 6: 1}),
        "before",
        2.5,
        [shape(WINDOWS, HEADS * TOKENS, KEYS, dtype=F32), shape(WINDOWS, KEYS, KEYS), cell_rows]
        + [shape(C, 3 * C), shape(C, C)],
        [pltpu.SemaphoreType.DMA((len(late),))],
        halves, x, gains, qkv0, query_choice,
        *[in_hbm(array) for array in late],
        in_specs=[VMEM_SPEC] * 5 + [hbm_spec] * len(late),
    )
    mine = call(join_kernel, "mine", 0.3, shape(8, 2, WINDOWS, SHARD), [], halves, *ring, v)
    theirs = turned(mine, lambda z, x, core: (z, x, 1 - core))
    proj0, fc1_0, fc2_0, lanes, rows, columns = call(
        functools.partial(sliced, prepare_kernel, {1: 0, 2: 0, 3: 0}),
        "prepare",
        1.2,
        layer + [shape(HALF, KEYS), shape(2, 256, 192), shape(2, HALF, 6 * GROUP)],
        [pltpu.SemaphoreType.DMA((3,))],
        mine, in_hbm(proj_weight), in_hbm(fc1_weight), in_hbm(fc2_turned),
        in_specs=[VMEM_SPEC] + [hbm_spec] * 3,
    )
    to_lat, to_lon, to_both, tables, far, attended = call(
        first_kernel,
        "first",
        4.5,
        [packed, packed, packed, shape(1152, KEYS), shape(3 * TOKENS, C), cell_rows],
        [pltpu.VMEM((1152, KEYS), F32)] + t_scratch,
        mine, theirs, scores, v, first_mask, keep, inputs, gains, query_choice, proj0, fc1_0, fc2_0, lanes, rows,
    )
    from_lat, from_lon, from_both = sent(to_lat, -1, 0), sent(to_lon, 0, 1), sent(to_both, -1, 1)
    bias, near = call(
        bias_kernel,
        "bias",
        0.2,
        [shape(WINDOWS, HEADS * TOKENS, KEYS), shape(TOKENS, C)],
        [pltpu.VMEM((768, 768), F32), pltpu.VMEM((768, 768), F32)],
        tables, second_mask, columns, rows, inputs, attended, gains, fc1_0, fc2_0, keep,
    )
    ready = call(ready_kernel, "ready", 0.4, cell_rows, [], near, from_lon, from_both, gains)
    own, to_lat, to_lon, to_both = call(
        second_kernel,
        "second",
        4.5,
        [shape(TOKENS, C), packed, packed, packed],
        [cells, cells],
        ready, from_lat, bias, gains, qkv1, proj1, query_choice,
    )
    from_lon, from_both, from_lat = sent(to_lon, 0, 1, True), sent(to_both, 1, 1, True), sent(to_lat, 1, 0, True)
    done, fc1_1, fc2_1, merge = call(
        functools.partial(sliced, own_kernel, {0: 1, 1: 1}),
        "own",
        0.5,
        [shape(TOKENS, C)] + layer[1:] + like([merge_weight]),
        [pltpu.SemaphoreType.DMA((3,))],
        in_hbm(fc1_weight), in_hbm(fc2_turned), in_hbm(merge_weight), keep, near, own, gains,
        in_specs=[hbm_spec] * 3 + [VMEM_SPEC] * 4,
    )
    middle = call(
        add_kernel, "add", 0.2, shape(2, TOKENS, C, dtype=F32), [], far, from_lon, from_both
    )
    merged = call(
        last_kernel,
        "last",
        2.0,
        shape(TOKENS, 2 * C),
        [],
        keep, far, done, middle, from_lat, gains, fc1_1, fc2_1, merge_gain.reshape(4, C), merge,
    )
    return merged.reshape(3, 6, LEVELS, 2 * C).transpose(2, 0, 1, 3)


def solution(mesh):
    return jax.shard_map(
        shards,
        mesh=mesh,
        in_specs=(
            P(None, "lat", "lon", None),
            P(),
            P(),
            P(),
            P(),
            P(),
            P(),
            P(None, "lat", None, "lon"),
            P(),
            P(),
        ),
        out_specs=P(None, "lat", "lon", None),
        check_vma=False,
    )
```

```python
import functools

import jax
import jax.numpy as jnp
import numpy as np
from jax import lax
from jax.experimental import pallas as pl
from jax.experimental.pallas import tpu as pltpu
from jax.sharding import PartitionSpec as P

BF16 = jnp.bfloat16
F32 = jnp.float32
C = 192
HEADS = 6
HEAD_SIZE = 32
HIDDEN = 768
LEVELS, ROWS, COLS = 8, 6, 12
WINDOWS = 4
TOKENS = 144
CELLS = 576
RUN = 24
SPAN = 23
HALF = 6 * SPAN
GROUP = 128
KEYS = 2 * GROUP
LATS, LONS = 8, 16
SHARD = 1242
SHIFT = 12.0
MASKED = -1e30


def one_hot(sources, width):
    sources = np.asarray(sources)
    matrix = np.zeros((len(sources), width), np.float32)
    rows = np.nonzero(sources >= 0)[0]
    matrix[rows, sources[rows]] = 1.0
    return jnp.asarray(matrix, BF16)


ROW_HALF = (1, 0, 1, 0)


def own_half(quarter):
    odd = lax.rem(lax.axis_index("lat"), 2)
    return (1 - odd, odd, odd, 1 - odd)[quarter]


def window_half(quarter):
    odd = lax.rem(lax.axis_index("lat"), 2)
    return (odd, odd, 1 - odd, 1 - odd)[quarter]


def query_order():
    return [level * 72 + c * 6 + r for c in range(COLS) for level in range(2) for r in range(ROWS)]


def natural_order():
    return [c * 12 + level * 6 + r for level in range(2) for c in range(COLS) for r in range(ROWS)]


def quarter_runs(qr, qc):
    starts = [qc * (6 * ROWS * LEVELS) + (c * ROWS + 3 * qr) * LEVELS for c in range(6)]
    return [pl.ds(pl.multiple_of(start, LEVELS), RUN) for start in starts]


def level_cells(level):
    return pl.ds(level, ROWS * COLS, stride=LEVELS)


def read_window(cells, first_level):
    parts = [
        jnp.concatenate([cells[0, level_cells(level % LEVELS)], cells[1, level_cells(level % LEVELS)]], axis=1)
        for level in (first_level, first_level + 1)
    ]
    return jnp.concatenate(parts, axis=0)[:, :C]


def write_window(cells, first_level, values):
    wide = jnp.concatenate([values, jnp.zeros((TOKENS, 2 * GROUP - C), F32)], axis=1)
    for offset in range(2):
        rows = wide[offset * 72 : (offset + 1) * 72]
        where = level_cells((first_level + offset) % LEVELS)
        cells[0, where] = rows[:, :GROUP]
        cells[1, where] = rows[:, GROUP:]


def read_quarter(cells, qr, qc):
    parts = [jnp.concatenate([cells[0, run, :], cells[1, run, :]], axis=1) for run in quarter_runs(qr, qc)]
    return jnp.concatenate(parts, axis=0)[:, :C]


def write_quarter(cells, qr, qc, values):
    wide = jnp.concatenate([values, jnp.zeros((TOKENS, 2 * GROUP - C), F32)], axis=1)
    for c, run in enumerate(quarter_runs(qr, qc)):
        cells[0, run, :] = wide[c * RUN : (c + 1) * RUN, :GROUP]
        cells[1, run, :] = wide[c * RUN : (c + 1) * RUN, GROUP:]


def layer_norm(values, scales):
    average = jnp.mean(values, axis=-1, keepdims=True)
    centred = values - average
    spread = jnp.mean(centred * centred, axis=-1, keepdims=True)
    return centred * lax.rsqrt(spread + 1e-05) * scales


def dot(a, b):
    return jnp.dot(a, b, preferred_element_type=F32)


def dot_transposed(a, b):
    return lax.dot_general(a, b, (((1,), (1,)), ((), ())), preferred_element_type=F32)


def moved(choice, rows):
    return dot(choice, rows).astype(BF16)


def head_lanes(head):
    lane = lax.broadcasted_iota(jnp.int32, (1, C), 1)
    return (lane >= head * HEAD_SIZE) & (lane < (head + 1) * HEAD_SIZE)


def project(normed, qkv_weight, orders):
    all_queries = dot(normed, qkv_weight[:, :C]).astype(BF16)
    all_keys = dot(normed, qkv_weight[:, C : 2 * C])
    all_values = dot(normed, qkv_weight[:, 2 * C :])
    pad = jnp.zeros((GROUP - 72, C), F32)
    ones = jnp.ones((KEYS, KEYS - C), BF16)

    def padded(part):
        return jnp.concatenate([part[:72], pad, part[72:], pad], axis=0).astype(BF16)

    results = []
    for p in range(WINDOWS):
        rows = slice(p * TOKENS, (p + 1) * TOKENS)
        values = jnp.concatenate([padded(all_values[rows]), ones], axis=1)
        results.append((moved(orders[0], all_queries[rows]), padded(all_keys[rows]), values))
    return results


def write_attended(cells, first_level, blended, orders, proj):
    natural = jnp.concatenate([moved(orders[1], part) for part in blended], axis=0)
    attended = dot(natural, proj)
    for p in range(WINDOWS):
        write_window(cells, 2 * p + first_level, attended[p * TOKENS : (p + 1) * TOKENS])


def score(queries, keys):
    stacked = jnp.concatenate(
        [jnp.where(head_lanes(h), queries, jnp.zeros((), BF16)) for h in range(HEADS)], axis=0
    )
    return dot_transposed(stacked, keys) * HEAD_SIZE ** (-0.5)


def blend(scores, values, bias_of):
    weights = []
    for h in range(HEADS):
        part = scores[h * TOKENS : (h + 1) * TOKENS] + bias_of(h)
        weights.append(jnp.exp(part).astype(BF16))
    blended = dot(jnp.concatenate(weights, axis=0), values)
    total = jnp.zeros((TOKENS, C), F32)
    result = jnp.zeros((TOKENS, C), F32)
    for h in range(HEADS):
        part = blended[h * TOKENS : (h + 1) * TOKENS]
        result = jnp.where(head_lanes(h), part[:, :C], result)
        total = jnp.where(head_lanes(h), part[:, C : C + 1], total)
    return (result / jnp.maximum(total, np.exp(-SHIFT))).astype(BF16)


def selected_bias(z_even, z_odd, window, head):
    rows = []
    for at in range(6):
        lanes = slice(at * GROUP, (at + 1) * GROUP)
        halves = []
        for key_level in range(2):
            first = head * 128 + (key_level * 4 + window) * 16
            top = z_even[first : first + 16, lanes]
            low = z_odd[first : first + 16, lanes]
            halves.append(jnp.concatenate([top[:8], top[8:] + low[:8], low[8:]], axis=0))
        rows.append(jnp.concatenate(halves, axis=1))
    return jnp.concatenate(rows, axis=0)


def window_lanes(tile, first):
    turn = (GROUP - first) % GROUP
    near = pltpu.roll(tile[:, :GROUP], turn, 1) if turn else tile[:, :GROUP]
    if first + 72 <= GROUP:
        return near
    lane = lax.broadcasted_iota(jnp.int32, (1, GROUP), 1)
    return jnp.where(lane < GROUP - first, near, pltpu.roll(tile[:, GROUP:], turn, 1))


def expanded_bias(t_top, t_low, window, head):
    halves = []
    for key_level in range(2):
        first = head * 128 + (key_level * 4 + window) * 16
        top_tile, low_tile = t_top[first : first + 16], t_low[first : first + 16]
        rows = []
        for column in range(0, 12, 2):
            top = window_lanes(top_tile, (11 - column) * ROWS).astype(F32)
            low = window_lanes(low_tile, (10 - column) * ROWS).astype(F32)
            rows += [top[:8], top[8:] + low[:8], low[8:]]
        halves.append(jnp.concatenate(rows, axis=0))
    return jnp.concatenate(halves, axis=1)


def picked_rows(table_ref, table_choice):
    tops, lows = [], []
    for h in range(HEADS):
        picked = moved(table_choice, table_ref[h * 192 : (h + 1) * 192, :HALF])
        tops.append(picked[:128])
        lows.append(picked[128:])
    return jnp.concatenate(tops, axis=0), jnp.concatenate(lows, axis=0)


def erf_gelu(values):
    return 0.5 * values * (1.0 + lax.erf(values * np.float32(np.sqrt(0.5))))


def feed_forward(middle, gain, fc1, fc2, keep):
    hidden = erf_gelu(dot(layer_norm(middle, gain).astype(BF16), fc1)).astype(BF16)
    return jnp.where(keep, middle + dot_transposed(hidden, fc2), 0.0).astype(BF16)


def finished(quarters, middle, gain, fc1, fc2, keep):
    flags = jnp.concatenate([keep[ROW_HALF[quarter]][:, :1] for quarter in quarters], axis=0) > 0
    return feed_forward(jnp.concatenate(middle, axis=0), gain, fc1[...], fc2[...], flags)


def pack_piece(piece):
    side = jnp.concatenate(
        [piece[:80, 128:], jnp.concatenate([piece[80:, 128:], piece[:16, 128:]], axis=0)], axis=1
    )
    return jnp.concatenate([piece[:, :128], side], axis=0)


def unpack_piece(packed):
    side = packed[TOKENS:]
    ends = jnp.concatenate([side[:, :64], side[: TOKENS - 80, 64:]], axis=0)
    return jnp.concatenate([packed[:TOKENS], ends], axis=1)


def prepare_masks(lat_valid, first_mask, second_mask, keep):
    lat = lax.axis_index("lat")

    def flag(row):
        return lat_valid[row] > 0

    lane = lax.broadcasted_iota(jnp.int32, (8, KEYS), 1)
    inner = lax.rem(lane, GROUP)
    key_row = jnp.where(inner < 72, lax.rem(inner, ROWS), -1)
    mask = jnp.full((8, KEYS), MASKED, F32)
    usable = jnp.full((8, KEYS), MASKED, F32)
    for r in range(ROWS):
        mask = jnp.where((key_row == r) & flag(lat * ROWS + r), -SHIFT, mask)
        rolled = lax.rem(lat * ROWS + 3 + r, LATS * ROWS)
        usable = jnp.where((key_row == r) & flag(rolled), 0.0, usable)
    first_mask[...] = mask
    a = lax.rem(lax.broadcasted_iota(jnp.int32, (TOKENS, 1), 0), 12)
    query_half = jnp.where(lax.rem(a, ROWS) >= 3, 1, 0)
    key_half = jnp.where(key_row[:1] >= 3, 1, 0)
    same_rows = (query_half == key_half) | (lat != LATS - 1)
    same_level = jnp.where(a >= ROWS, 1, 0) == jnp.where(lane[:1] >= GROUP, 1, 0)
    whole = jnp.where(same_rows, usable[:1], MASKED)
    second_mask[0] = whole
    second_mask[1] = jnp.where(same_level, whole, MASKED)
    for half in range(2):
        for r in range(3):
            value = jnp.where(flag(lat * ROWS + 3 * half + r), 1.0, 0.0)
            for c in range(6):
                at = (c * 3 + r) * LEVELS
                keep[half, at : at + LEVELS] = jnp.full((LEVELS, GROUP), value, F32)


def fetch(sources, held, sems):
    copies = [pltpu.make_async_copy(a, b, sems.at[n]) for n, (a, b) in enumerate(zip(sources, held))]
    for copy in copies:
        copy.start()
    return copies


def sliced(kernel, layers, *refs):
    kernel(*[ref.at[layers[at]] if at in layers else ref for at, ref in enumerate(refs)])


def fetch_kernel(*refs):
    sources, held, (first_mask, second_mask, keep, flags, sems) = refs[:6], refs[6:11], refs[11:]
    copies = fetch(sources, (flags,) + tuple(held), sems)
    copies[0].wait()
    prepare_masks(flags, first_mask, second_mask, keep)
    for copy in copies[1:]:
        copy.wait()


def choose(row_keys, lane_keys):
    return jnp.where(row_keys == lane_keys, 1.0, 0.0).astype(BF16)


def prepare_kernel(mine, proj, fc1, fc2, *refs):
    copies = fetch((proj, fc1, fc2), refs[:3], refs[-1])
    lanes, rows, columns = refs[3:6]

    def place(shape, axis):
        return lax.broadcasted_iota(jnp.int32, shape, axis)

    at = place((HALF, 1), 0)
    row, position = at // SPAN, lax.rem(at, SPAN)
    lanes[...] = choose(position * ROWS + row, place((HALF, KEYS), 1))
    at = place((256, 1), 0)
    a = lax.rem(at, 16) - 4 * (at // 128)
    source = (a * 2 + lax.rem(at // 64, 2)) * 8 + lax.rem(at // 16, 4)
    for block in range(2):
        rows[block] = choose(jnp.where((a >= 0) & (a < 12), source + 4 * block, -1), place((256, 192), 1))
    lane = place((1, 6 * GROUP), 1)
    inner = lax.rem(lane, GROUP)
    for parity in range(2):
        met = inner // ROWS - (lane // GROUP * 2 + parity) + 11
        wanted = jnp.where(inner < 72, met * ROWS + lax.rem(inner, ROWS), -1)
        columns[parity] = choose(position * ROWS + row, wanted)
    for copy in copies:
        copy.wait()


def join_kernel(*refs):
    at = 0
    for ref in refs[:-1]:
        if ref.shape[1:] == refs[-1].shape[1:]:
            refs[-1][at : at + ref.shape[0]] = ref[...]
            at += ref.shape[0]


def before_kernel(halves, x, gains, qkv_weight, query_choice, *refs):
    sources, (scores_out, v_out, cells), held, sems = refs[:2], refs[2:5], refs[5:7], refs[7]
    copies = fetch(sources, held, sems)
    wide = jnp.concatenate([x[...].astype(F32), jnp.zeros((CELLS, 2 * GROUP - C), F32)], axis=1)
    for r in range(ROWS):
        for c in range(COLS):
            group = wide[(r * COLS + c) * LEVELS : (r * COLS + c + 1) * LEVELS]
            at = (c * ROWS + r) * LEVELS
            cells[0, at : at + LEVELS] = group[:, :GROUP]
            cells[1, at : at + LEVELS] = group[:, GROUP:]
    windows = jnp.concatenate([read_window(cells, 2 * p) for p in range(WINDOWS)], axis=0)
    normed = layer_norm(windows, gains[0, 0:1]).astype(BF16)
    for p, (q, k, v) in enumerate(project(normed, qkv_weight[...], query_choice)):
        v_out[p] = v
        scores_out[p] = score(q, k)
    for copy in copies:
        copy.wait()


def first_quarters(quarters, inputs, cells, gains, fc1, fc2, keep):
    middle = []
    for quarter in quarters:
        qr, qc = ROW_HALF[quarter], own_half(quarter)
        middle.append(read_quarter(inputs, qr, qc) + read_quarter(cells, qr, qc).astype(BF16).astype(F32))
    return finished(quarters, middle, gains[0, 1:2], fc1, fc2, keep)


def first_kernel(mine, theirs, scores, v, first_mask, keep, inputs, gains, query_choice, proj, fc1, fc2, lanes, rows, sent_lat, sent_lon, sent_both, table_out, out, cells, table_f32, t_top, t_low):
    me = lax.axis_index("lon")
    for g in range(LONS):
        slot = lax.rem(me // 2 - g // 2 + 8, 4) * 2 + jnp.where(me // 8 == g // 8, 0, 1)
        shard = jnp.where(lax.rem(me, 2) == g % 2, mine[slot], theirs[slot]).astype(F32)
        piece = jnp.concatenate([shard[0], shard[1]], axis=0)
        for n in range(9):
            at = (g * 9 + n) * 8
            table_f32[at : at + 8, :HALF] = piece[:, n * HALF : (n + 1) * HALF]
    table_out[:, :HALF] = table_f32[:, :HALF].astype(BF16)
    tops, lows = picked_rows(table_out, rows[0])
    t_top[...] = dot(tops, lanes[...]).astype(BF16)
    t_low[...] = dot(lows, lanes[...]).astype(BF16)
    mask = first_mask[0:1]
    blended = [blend(scores[p], v[p], lambda h: expanded_bias(t_top, t_low, p, h) + mask) for p in range(WINDOWS)]
    write_attended(cells, 0, blended, query_choice, proj[...])
    results = first_quarters((1, 2, 3), inputs, cells, gains, fc1, fc2, keep)
    out[...] = results
    for at, target in enumerate((sent_lat, sent_lon, sent_both)):
        target[...] = pack_piece(results[at * TOKENS : (at + 1) * TOKENS])


def bias_kernel(table, second_mask, columns, rows, inputs, cells, gains, fc1, fc2, keep, bias_out, near, z_even, z_odd):
    near[...] = first_quarters((0,), inputs, cells, gains, fc1, fc2, keep)
    tops, lows = picked_rows(table, rows[1])
    z_even[...] = dot(tops, columns[0])
    z_odd[...] = dot(lows, columns[1])
    for p in range(WINDOWS):
        for h in range(HEADS):
            whole = selected_bias(z_even, z_odd, p, h) + second_mask[1 if p == WINDOWS - 1 else 0]
            bias_out[p, h * TOKENS : (h + 1) * TOKENS] = whole.astype(BF16)


def write_normed(cells, quarter, piece, gains):
    normed = layer_norm(piece.astype(F32), gains[1, 0:1]).astype(BF16)
    write_quarter(cells, 1 - ROW_HALF[quarter], window_half(quarter), normed.astype(F32))


def ready_kernel(near, from_lon, from_both, gains, cells):
    write_normed(cells, 0, near[...], gains)
    write_normed(cells, 2, unpack_piece(from_lon[...]), gains)
    write_normed(cells, 3, unpack_piece(from_both[...]), gains)


def second_kernel(given, from_lat, bias, gains, qkv_weight, proj, query_choice, own, sent_lat, sent_lon, sent_both, cells, results):
    cells[...] = given[...]
    write_normed(cells, 1, unpack_piece(from_lat[...]), gains)
    normed = jnp.concatenate([read_window(cells, 2 * p + 1) for p in range(WINDOWS)], axis=0).astype(BF16)
    blended = []
    for p, (q, k, v) in enumerate(project(normed, qkv_weight[...], query_choice)):

        def bias_of(h):
            return bias[p, h * TOKENS : (h + 1) * TOKENS].astype(F32) - SHIFT

        blended.append(blend(score(q, k), v, bias_of))
    write_attended(results, 1, blended, query_choice, proj[...])
    pieces = [read_quarter(results, 1 - ROW_HALF[k], window_half(k)).astype(BF16) for k in range(4)]
    own[...] = pieces[0]
    sent_lat[...] = pack_piece(pieces[1])
    sent_lon[...] = pack_piece(pieces[2])
    sent_both[...] = pack_piece(pieces[3])


def own_kernel(fc1, fc2, merge, keep, near, own, gains, result, *refs):
    copies = fetch((fc1, fc2, merge), refs[:3], refs[3])
    middle = near[...].astype(F32) + own[...].astype(F32)
    for copy in copies:
        copy.wait()
    result[...] = feed_forward(middle, gains[1, 1:2], refs[0][...], refs[1][...], keep[1][:, :1] > 0)


def add_kernel(far, from_lon, from_both, middle):
    for at, piece in enumerate((from_lon, from_both)):
        inputs = far[(at + 1) * TOKENS : (at + 2) * TOKENS].astype(F32)
        middle[at] = inputs + unpack_piece(piece[...]).astype(F32)


def last_kernel(keep, far, done, middle, from_lat, gains, fc1, fc2, merge_gain, merge_weight, merged):
    upper = far[:TOKENS].astype(F32) + unpack_piece(from_lat[...]).astype(F32)
    fresh = finished((1, 2, 3), [upper, middle[0], middle[1]], gains[1, 1:2], fc1, fc2, keep).astype(F32)
    results = [done[...].astype(F32)] + [fresh[at * TOKENS : (at + 1) * TOKENS] for at in range(3)]
    odd = lax.rem(lax.axis_index("lat"), 2) == 1
    groups = {}
    for qr, (first, second) in enumerate(((1, 3), (0, 2))):
        turned_round = odd if qr == 1 else jnp.logical_not(odd)
        right = jnp.where(turned_round, results[second], results[first])
        left = jnp.where(turned_round, results[first], results[second])
        for qc, result in enumerate((left, right)):
            for r in range(3):
                for c in range(6):
                    at = (c * 3 + r) * LEVELS
                    groups[3 * qr + r, 6 * qc + c] = result[at : at + LEVELS]
    parts = [
        jnp.concatenate([groups[2 * r + dr, 2 * c + dc] for r in range(3) for c in range(6)], axis=0)
        for dr in range(2)
        for dc in range(2)
    ]
    average = sum(jnp.sum(part, axis=-1, keepdims=True) for part in parts) / (4 * C)
    parts = [part - average for part in parts]
    spread = sum(jnp.sum(part * part, axis=-1, keepdims=True) for part in parts) / (4 * C)
    scale = lax.rsqrt(spread + 1e-05)
    total = jnp.zeros((TOKENS, 2 * C), F32)
    for d, part in enumerate(parts):
        normed = (part * scale * merge_gain[d : d + 1]).astype(BF16)
        total = total + dot(normed, merge_weight[d * C : (d + 1) * C])
    merged[...] = total.astype(BF16)


VMEM_SPEC = pl.BlockSpec(memory_space=pltpu.VMEM)
SMEM_SPEC = pl.BlockSpec(memory_space=pltpu.SMEM)


def call(kernel, name, micros, outs, scratch, *operands, in_specs=None, aliases=None):
    return pl.pallas_call(
        kernel,
        name=name,
        out_shape=outs,
        in_specs=in_specs or [VMEM_SPEC] * len(operands),
        out_specs=jax.tree.map(lambda _: VMEM_SPEC, outs),
        scratch_shapes=scratch,
        input_output_aliases=aliases or {},
        cost_estimate=pl.CostEstimate(flops=int(micros * 1e9), bytes_accessed=2**20, transcendentals=0),
        compiler_params=pltpu.CompilerParams(vmem_limit_bytes=16 * 2**20),
    )(*operands)


def shape(*dims, dtype=BF16):
    return jax.ShapeDtypeStruct(dims, dtype)


def sent(block, rows, across, back=False):
    route = []
    for i in range(LATS):
        for j in range(LONS):
            to = (i + rows) % LATS
            owner = i if back else to
            step = (1 if owner % 2 == 1 else -1) * (-1 if back else 1)
            route.append((i * LONS + j, to * LONS + (j + across * step) % LONS))
    return lax.ppermute(block, ("lat", "lon"), route)


def turned(block, place):
    route = []
    for j in range(LONS):
        z, x, core = place(j // 8, j // 2 % 4, j % 2)
        route.append((j, z * 8 + x * 2 + core))
    return lax.ppermute(block, "lon", route)


def shards(state, lat_valid, norm_gains, qkv_weight, proj_weight, fc1_weight, fc2_weight, earth_bias, merge_gain, merge_weight):
    shard = earth_bias[:, 0]
    cells = pltpu.VMEM((2, CELLS, GROUP), F32)
    cell_rows = shape(2, CELLS, GROUP, dtype=F32)
    t_scratch = [pltpu.VMEM((768, KEYS), BF16), pltpu.VMEM((768, KEYS), BF16)]
    packed = shape(224, 128)

    def in_hbm(array):
        return pltpu.with_memory_space_constraint(array, pltpu.HBM)

    def like(arrays):
        return [shape(*array.shape, dtype=array.dtype) for array in arrays]

    hbm_spec = pl.BlockSpec(memory_space=pltpu.HBM)
    fc2_turned = jnp.swapaxes(fc2_weight, 1, 2)
    early = [
        shard[None],
        state.transpose(1, 2, 0, 3).reshape(CELLS, C),
        norm_gains,
        qkv_weight,
        jnp.stack([one_hot(query_order(), TOKENS), one_hot(natural_order(), TOKENS)]),
    ]
    late = [qkv_weight, proj_weight]
    layer = [shape(C, C), shape(C, HIDDEN), shape(C, HIDDEN)]
    other_half = turned(shard, lambda z, x, core: (1 - z, x, core))
    held_shard, x, gains, qkv0, query_choice, first_mask, second_mask, keep = call(
        functools.partial(sliced, fetch_kernel, {4: 0}),
        "fetch",
        1.4,
        like(early[:3])
        + [shape(C, 3 * C)]
        + like(early[4:])
        + [
            shape(8, KEYS, dtype=F32),
            shape(2, TOKENS, KEYS, dtype=F32),
            shape(2, TOKENS, GROUP, dtype=F32),
        ],
        [pltpu.SMEM((LATS * ROWS,), jnp.int32), pltpu.SemaphoreType.DMA((len(early) + 1,))],
        in_hbm(lat_valid),
        *[in_hbm(array) for array in early],
        in_specs=[hbm_spec] * (len(early) + 1),
    )
    halves = call(join_kernel, "halves", 0.2, shape(2, 2, WINDOWS, SHARD), [], held_shard, other_half[None])
    ring = [turned(halves, lambda z, x, core: (z, (x + hop) % 4, core)) for hop in range(1, 4)]
    scores, v, inputs, qkv1, proj1 = call(
        functools.partial(sliced, before_kernel, {5: 1, 6: 1}),
        "before",
        2.5,
        [shape(WINDOWS, HEADS * TOKENS, KEYS, dtype=F32), shape(WINDOWS, KEYS, KEYS), cell_rows]
        + [shape(C, 3 * C), shape(C, C)],
        [pltpu.SemaphoreType.DMA((len(late),))],
        halves, x, gains, qkv0, query_choice,
        *[in_hbm(array) for array in late],
        in_specs=[VMEM_SPEC] * 5 + [hbm_spec] * len(late),
    )
    mine = call(join_kernel, "mine", 0.3, shape(8, 2, WINDOWS, SHARD), [], halves, *ring, v)
    theirs = turned(mine, lambda z, x, core: (z, x, 1 - core))
    proj0, fc1_0, fc2_0, lanes, rows, columns = call(
        functools.partial(sliced, prepare_kernel, {1: 0, 2: 0, 3: 0}),
        "prepare",
        1.2,
        layer + [shape(HALF, KEYS), shape(2, 256, 192), shape(2, HALF, 6 * GROUP)],
        [pltpu.SemaphoreType.DMA((3,))],
        mine, in_hbm(proj_weight), in_hbm(fc1_weight), in_hbm(fc2_turned),
        in_specs=[VMEM_SPEC] + [hbm_spec] * 3,
    )
    to_lat, to_lon, to_both, tables, far, attended = call(
        first_kernel,
        "first",
        4.5,
        [packed, packed, packed, shape(1152, KEYS), shape(3 * TOKENS, C), cell_rows],
        [pltpu.VMEM((1152, KEYS), F32)] + t_scratch,
        mine, theirs, scores, v, first_mask, keep, inputs, gains, query_choice, proj0, fc1_0, fc2_0, lanes, rows,
    )
    from_lat, from_lon, from_both = sent(to_lat, -1, 0), sent(to_lon, 0, 1), sent(to_both, -1, 1)
    bias, near = call(
        bias_kernel,
        "bias",
        0.2,
        [shape(WINDOWS, HEADS * TOKENS, KEYS), shape(TOKENS, C)],
        [pltpu.VMEM((768, 768), F32), pltpu.VMEM((768, 768), F32)],
        tables, second_mask, columns, rows, inputs, attended, gains, fc1_0, fc2_0, keep,
    )
    ready = call(ready_kernel, "ready", 0.4, cell_rows, [], near, from_lon, from_both, gains)
    own, to_lat, to_lon, to_both = call(
        second_kernel,
        "second",
        4.5,
        [shape(TOKENS, C), packed, packed, packed],
        [cells, cells],
        ready, from_lat, bias, gains, qkv1, proj1, query_choice,
    )
    from_lon, from_both, from_lat = sent(to_lon, 0, 1, True), sent(to_both, 1, 1, True), sent(to_lat, 1, 0, True)
    done, fc1_1, fc2_1, merge = call(
        functools.partial(sliced, own_kernel, {0: 1, 1: 1}),
        "own",
        0.5,
        [shape(TOKENS, C)] + layer[1:] + like([merge_weight]),
        [pltpu.SemaphoreType.DMA((3,))],
        in_hbm(fc1_weight), in_hbm(fc2_turned), in_hbm(merge_weight), keep, near, own, gains,
        in_specs=[hbm_spec] * 3 + [VMEM_SPEC] * 4,
    )
    middle = call(
        add_kernel, "add", 0.2, shape(2, TOKENS, C, dtype=F32), [], far, from_lon, from_both
    )
    merged = call(
        last_kernel,
        "last",
        2.0,
        shape(TOKENS, 2 * C),
        [],
        keep, far, done, middle, from_lat, gains, fc1_1, fc2_1, merge_gain.reshape(4, C), merge,
    )
    return merged.reshape(3, 6, LEVELS, 2 * C).transpose(2, 0, 1, 3)


def solution(mesh):
    return jax.shard_map(
        shards,
        mesh=mesh,
        in_specs=(
            P(None, "lat", "lon", None),
            P(),
            P(),
            P(),
            P(),
            P(),
            P(),
            P(None, "lat", None, "lon"),
            P(),
            P(),
        ),
        out_specs=P(None, "lat", "lon", None),
        check_vma=False,
    )
```

```python
import functools

import jax
import jax.numpy as jnp
import numpy as np
from jax import lax
from jax.experimental import pallas as pl
from jax.experimental.pallas import tpu as pltpu
from jax.sharding import PartitionSpec as P

BF16 = jnp.bfloat16
F32 = jnp.float32
C = 192
HEADS = 6
HEAD_SIZE = 32
HIDDEN = 768
LEVELS, ROWS, COLS = 8, 6, 12
WINDOWS = 4
TOKENS = 144
CELLS = 576
RUN = 24
SPAN = 23
HALF = 6 * SPAN
GROUP = 128
KEYS = 2 * GROUP
LATS, LONS = 8, 16
SHARD = 1242
SHIFT = 12.0
MASKED = -1e30


def one_hot(sources, width):
    sources = np.asarray(sources)
    matrix = np.zeros((len(sources), width), np.float32)
    rows = np.nonzero(sources >= 0)[0]
    matrix[rows, sources[rows]] = 1.0
    return jnp.asarray(matrix, BF16)


ROW_HALF = (1, 0, 1, 0)


def own_half(quarter):
    odd = lax.rem(lax.axis_index("lat"), 2)
    return (1 - odd, odd, odd, 1 - odd)[quarter]


def window_half(quarter):
    odd = lax.rem(lax.axis_index("lat"), 2)
    return (odd, odd, 1 - odd, 1 - odd)[quarter]


def query_order():
    return [level * 72 + c * 6 + r for c in range(COLS) for level in range(2) for r in range(ROWS)]


def natural_order():
    return [c * 12 + level * 6 + r for level in range(2) for c in range(COLS) for r in range(ROWS)]


def quarter_runs(qr, qc):
    starts = [qc * (6 * ROWS * LEVELS) + (c * ROWS + 3 * qr) * LEVELS for c in range(6)]
    return [pl.ds(pl.multiple_of(start, LEVELS), RUN) for start in starts]


def level_cells(level):
    return pl.ds(level, ROWS * COLS, stride=LEVELS)


def read_window(cells, first_level):
    parts = [
        jnp.concatenate([cells[0, level_cells(level % LEVELS)], cells[1, level_cells(level % LEVELS)]], axis=1)
        for level in (first_level, first_level + 1)
    ]
    return jnp.concatenate(parts, axis=0)[:, :C]


def write_window(cells, first_level, values):
    wide = jnp.concatenate([values, jnp.zeros((TOKENS, 2 * GROUP - C), F32)], axis=1)
    for offset in range(2):
        rows = wide[offset * 72 : (offset + 1) * 72]
        where = level_cells((first_level + offset) % LEVELS)
        cells[0, where] = rows[:, :GROUP]
        cells[1, where] = rows[:, GROUP:]


def read_quarter(cells, qr, qc):
    parts = [jnp.concatenate([cells[0, run, :], cells[1, run, :]], axis=1) for run in quarter_runs(qr, qc)]
    return jnp.concatenate(parts, axis=0)[:, :C]


def write_quarter(cells, qr, qc, values):
    wide = jnp.concatenate([values, jnp.zeros((TOKENS, 2 * GROUP - C), F32)], axis=1)
    for c, run in enumerate(quarter_runs(qr, qc)):
        cells[0, run, :] = wide[c * RUN : (c + 1) * RUN, :GROUP]
        cells[1, run, :] = wide[c * RUN : (c + 1) * RUN, GROUP:]


def layer_norm(values, scales):
    average = jnp.mean(values, axis=-1, keepdims=True)
    centred = values - average
    spread = jnp.mean(centred * centred, axis=-1, keepdims=True)
    return centred * lax.rsqrt(spread + 1e-05) * scales


def dot(a, b):
    return jnp.dot(a, b, preferred_element_type=F32)


def dot_transposed(a, b):
    return lax.dot_general(a, b, (((1,), (1,)), ((), ())), preferred_element_type=F32)


def moved(choice, rows):
    return dot(choice, rows).astype(BF16)


def head_lanes(head):
    lane = lax.broadcasted_iota(jnp.int32, (1, C), 1)
    return (lane >= head * HEAD_SIZE) & (lane < (head + 1) * HEAD_SIZE)


def project(normed, qkv_weight, orders):
    all_queries = dot(normed, qkv_weight[:, :C]).astype(BF16)
    all_keys = dot(normed, qkv_weight[:, C : 2 * C])
    all_values = dot(normed, qkv_weight[:, 2 * C :])
    pad = jnp.zeros((GROUP - 72, C), F32)
    ones = jnp.ones((KEYS, KEYS - C), BF16)

    def padded(part):
        return jnp.concatenate([part[:72], pad, part[72:], pad], axis=0).astype(BF16)

    results = []
    for p in range(WINDOWS):
        rows = slice(p * TOKENS, (p + 1) * TOKENS)
        values = jnp.concatenate([padded(all_values[rows]), ones], axis=1)
        results.append((moved(orders[0], all_queries[rows]), padded(all_keys[rows]), values))
    return results


def write_attended(cells, first_level, blended, orders, proj):
    natural = jnp.concatenate([moved(orders[1], part) for part in blended], axis=0)
    attended = dot(natural, proj)
    for p in range(WINDOWS):
        write_window(cells, 2 * p + first_level, attended[p * TOKENS : (p + 1) * TOKENS])


def score(queries, keys):
    stacked = jnp.concatenate(
        [jnp.where(head_lanes(h), queries, jnp.zeros((), BF16)) for h in range(HEADS)], axis=0
    )
    return dot_transposed(stacked, keys) * HEAD_SIZE ** (-0.5)


def blend(scores, values, bias_of):
    weights = []
    for h in range(HEADS):
        part = scores[h * TOKENS : (h + 1) * TOKENS] + bias_of(h)
        weights.append(jnp.exp(part).astype(BF16))
    blended = dot(jnp.concatenate(weights, axis=0), values)
    total = jnp.zeros((TOKENS, C), F32)
    result = jnp.zeros((TOKENS, C), F32)
    for h in range(HEADS):
        part = blended[h * TOKENS : (h + 1) * TOKENS]
        result = jnp.where(head_lanes(h), part[:, :C], result)
        total = jnp.where(head_lanes(h), part[:, C : C + 1], total)
    return (result / jnp.maximum(total, np.exp(-SHIFT))).astype(BF16)


def selected_bias(z_even, z_odd, window, head):
    rows = []
    for at in range(6):
        lanes = slice(at * GROUP, (at + 1) * GROUP)
        halves = []
        for key_level in range(2):
            first = head * 128 + (key_level * 4 + window) * 16
            top = z_even[first : first + 16, lanes]
            low = z_odd[first : first + 16, lanes]
            halves.append(jnp.concatenate([top[:8], top[8:] + low[:8], low[8:]], axis=0))
        rows.append(jnp.concatenate(halves, axis=1))
    return jnp.concatenate(rows, axis=0)


def window_lanes(tile, first):
    turn = (GROUP - first) % GROUP
    near = pltpu.roll(tile[:, :GROUP], turn, 1) if turn else tile[:, :GROUP]
    if first + 72 <= GROUP:
        return near
    lane = lax.broadcasted_iota(jnp.int32, (1, GROUP), 1)
    return jnp.where(lane < GROUP - first, near, pltpu.roll(tile[:, GROUP:], turn, 1))


def expanded_bias(t_top, t_low, window, head):
    halves = []
    for key_level in range(2):
        first = head * 128 + (key_level * 4 + window) * 16
        top_tile, low_tile = t_top[first : first + 16], t_low[first : first + 16]
        rows = []
        for column in range(0, 12, 2):
            top = window_lanes(top_tile, (11 - column) * ROWS).astype(F32)
            low = window_lanes(low_tile, (10 - column) * ROWS).astype(F32)
            rows += [top[:8], top[8:] + low[:8], low[8:]]
        halves.append(jnp.concatenate(rows, axis=0))
    return jnp.concatenate(halves, axis=1)


def picked_rows(table_ref, table_choice):
    tops, lows = [], []
    for h in range(HEADS):
        picked = moved(table_choice, table_ref[h * 192 : (h + 1) * 192, :HALF])
        tops.append(picked[:128])
        lows.append(picked[128:])
    return jnp.concatenate(tops, axis=0), jnp.concatenate(lows, axis=0)


def erf_gelu(values):
    return 0.5 * values * (1.0 + lax.erf(values * np.float32(np.sqrt(0.5))))


def feed_forward(middle, gain, fc1, fc2, keep):
    hidden = erf_gelu(dot(layer_norm(middle, gain).astype(BF16), fc1)).astype(BF16)
    return jnp.where(keep, middle + dot_transposed(hidden, fc2), 0.0).astype(BF16)


def finished(quarters, middle, gain, fc1, fc2, keep):
    flags = jnp.concatenate([keep[ROW_HALF[quarter]][:, :1] for quarter in quarters], axis=0) > 0
    return feed_forward(jnp.concatenate(middle, axis=0), gain, fc1[...], fc2[...], flags)


def pack_piece(piece):
    side = jnp.concatenate(
        [piece[:80, 128:], jnp.concatenate([piece[80:, 128:], piece[:16, 128:]], axis=0)], axis=1
    )
    return jnp.concatenate([piece[:, :128], side], axis=0)


def unpack_piece(packed):
    side = packed[TOKENS:]
    ends = jnp.concatenate([side[:, :64], side[: TOKENS - 80, 64:]], axis=0)
    return jnp.concatenate([packed[:TOKENS], ends], axis=1)


def prepare_masks(lat_valid, first_mask, second_mask, keep):
    lat = lax.axis_index("lat")

    def flag(row):
        return lat_valid[row] > 0

    lane = lax.broadcasted_iota(jnp.int32, (8, KEYS), 1)
    inner = lax.rem(lane, GROUP)
    key_row = jnp.where(inner < 72, lax.rem(inner, ROWS), -1)
    mask = jnp.full((8, KEYS), MASKED, F32)
    usable = jnp.full((8, KEYS), MASKED, F32)
    for r in range(ROWS):
        mask = jnp.where((key_row == r) & flag(lat * ROWS + r), -SHIFT, mask)
        rolled = lax.rem(lat * ROWS + 3 + r, LATS * ROWS)
        usable = jnp.where((key_row == r) & flag(rolled), 0.0, usable)
    first_mask[...] = mask
    a = lax.rem(lax.broadcasted_iota(jnp.int32, (TOKENS, 1), 0), 12)
    query_half = jnp.where(lax.rem(a, ROWS) >= 3, 1, 0)
    key_half = jnp.where(key_row[:1] >= 3, 1, 0)
    same_rows = (query_half == key_half) | (lat != LATS - 1)
    same_level = jnp.where(a >= ROWS, 1, 0) == jnp.where(lane[:1] >= GROUP, 1, 0)
    whole = jnp.where(same_rows, usable[:1], MASKED)
    second_mask[0] = whole
    second_mask[1] = jnp.where(same_level, whole, MASKED)
    for half in range(2):
        for r in range(3):
            value = jnp.where(flag(lat * ROWS + 3 * half + r), 1.0, 0.0)
            for c in range(6):
                at = (c * 3 + r) * LEVELS
                keep[half, at : at + LEVELS] = jnp.full((LEVELS, GROUP), value, F32)


def fetch(sources, held, sems):
    copies = [pltpu.make_async_copy(a, b, sems.at[n]) for n, (a, b) in enumerate(zip(sources, held))]
    for copy in copies:
        copy.start()
    return copies


def sliced(kernel, layers, *refs):
    kernel(*[ref.at[layers[at]] if at in layers else ref for at, ref in enumerate(refs)])


def fetch_kernel(*refs):
    sources, held, (first_mask, second_mask, keep, flags, sems) = refs[:6], refs[6:11], refs[11:]
    copies = fetch(sources, (flags,) + tuple(held), sems)
    copies[0].wait()
    prepare_masks(flags, first_mask, second_mask, keep)
    for copy in copies[1:]:
        copy.wait()


def choose(row_keys, lane_keys):
    return jnp.where(row_keys == lane_keys, 1.0, 0.0).astype(BF16)


def prepare_kernel(mine, proj, fc1, fc2, *refs):
    copies = fetch((proj, fc1, fc2), refs[:3], refs[-1])
    lanes, rows, columns = refs[3:6]

    def place(shape, axis):
        return lax.broadcasted_iota(jnp.int32, shape, axis)

    at = place((HALF, 1), 0)
    row, position = at // SPAN, lax.rem(at, SPAN)
    lanes[...] = choose(position * ROWS + row, place((HALF, KEYS), 1))
    at = place((256, 1), 0)
    a = lax.rem(at, 16) - 4 * (at // 128)
    source = (a * 2 + lax.rem(at // 64, 2)) * 8 + lax.rem(at // 16, 4)
    for block in range(2):
        rows[block] = choose(jnp.where((a >= 0) & (a < 12), source + 4 * block, -1), place((256, 192), 1))
    lane = place((1, 6 * GROUP), 1)
    inner = lax.rem(lane, GROUP)
    for parity in range(2):
        met = inner // ROWS - (lane // GROUP * 2 + parity) + 11
        wanted = jnp.where(inner < 72, met * ROWS + lax.rem(inner, ROWS), -1)
        columns[parity] = choose(position * ROWS + row, wanted)
    for copy in copies:
        copy.wait()


def join_kernel(*refs):
    at = 0
    for ref in refs[:-1]:
        if ref.shape[1:] == refs[-1].shape[1:]:
            refs[-1][at : at + ref.shape[0]] = ref[...]
            at += ref.shape[0]


def before_kernel(halves, x, gains, qkv_weight, query_choice, *refs):
    sources, (scores_out, v_out, cells), held, sems = refs[:2], refs[2:5], refs[5:7], refs[7]
    copies = fetch(sources, held, sems)
    wide = jnp.concatenate([x[...].astype(F32), jnp.zeros((CELLS, 2 * GROUP - C), F32)], axis=1)
    for r in range(ROWS):
        for c in range(COLS):
            group = wide[(r * COLS + c) * LEVELS : (r * COLS + c + 1) * LEVELS]
            at = (c * ROWS + r) * LEVELS
            cells[0, at : at + LEVELS] = group[:, :GROUP]
            cells[1, at : at + LEVELS] = group[:, GROUP:]
    windows = jnp.concatenate([read_window(cells, 2 * p) for p in range(WINDOWS)], axis=0)
    normed = layer_norm(windows, gains[0, 0:1]).astype(BF16)
    for p, (q, k, v) in enumerate(project(normed, qkv_weight[...], query_choice)):
        v_out[p] = v
        scores_out[p] = score(q, k)
    for copy in copies:
        copy.wait()


def first_quarters(quarters, inputs, cells, gains, fc1, fc2, keep):
    middle = []
    for quarter in quarters:
        qr, qc = ROW_HALF[quarter], own_half(quarter)
        middle.append(read_quarter(inputs, qr, qc) + read_quarter(cells, qr, qc).astype(BF16).astype(F32))
    return finished(quarters, middle, gains[0, 1:2], fc1, fc2, keep)


def first_kernel(mine, theirs, scores, v, first_mask, keep, inputs, gains, query_choice, proj, fc1, fc2, lanes, rows, sent_lat, sent_lon, sent_both, table_out, out, cells, table_f32, t_top, t_low):
    me = lax.axis_index("lon")
    for core, shards_of in ((lax.rem(me, 2), mine), (1 - lax.rem(me, 2), theirs)):
        for slot in range(LONS // 2):
            z = jnp.where(me >= 8, 1, 0) if slot % 2 == 0 else jnp.where(me >= 8, 0, 1)
            g = z * 8 + lax.rem(me // 2 - slot // 2 + 8, 4) * 2 + core
            shard = shards_of[slot].astype(F32)
            piece = jnp.concatenate([shard[0], shard[1]], axis=0)
            for n in range(9):
                rows_at = pl.ds(pl.multiple_of(g * 72 + n * 8, 8), 8)
                table_f32[rows_at, :HALF] = piece[:, n * HALF : (n + 1) * HALF]
    table_out[:, :HALF] = table_f32[:, :HALF].astype(BF16)
    tops, lows = picked_rows(table_out, rows[0])
    t_top[...] = dot(tops, lanes[...]).astype(BF16)
    t_low[...] = dot(lows, lanes[...]).astype(BF16)
    mask = first_mask[0:1]
    blended = [blend(scores[p], v[p], lambda h: expanded_bias(t_top, t_low, p, h) + mask) for p in range(WINDOWS)]
    write_attended(cells, 0, blended, query_choice, proj[...])
    results = first_quarters((1, 2, 3), inputs, cells, gains, fc1, fc2, keep)
    out[...] = results
    for at, target in enumerate((sent_lat, sent_lon, sent_both)):
        target[...] = pack_piece(results[at * TOKENS : (at + 1) * TOKENS])


def bias_kernel(table, second_mask, columns, rows, inputs, cells, gains, fc1, fc2, keep, bias_out, near, z_even, z_odd):
    near[...] = first_quarters((0,), inputs, cells, gains, fc1, fc2, keep)
    tops, lows = picked_rows(table, rows[1])
    z_even[...] = dot(tops, columns[0])
    z_odd[...] = dot(lows, columns[1])
    for p in range(WINDOWS):
        for h in range(HEADS):
            whole = selected_bias(z_even, z_odd, p, h) + second_mask[1 if p == WINDOWS - 1 else 0]
            bias_out[p, h * TOKENS : (h + 1) * TOKENS] = whole.astype(BF16)


def write_normed(cells, quarter, piece, gains):
    normed = layer_norm(piece.astype(F32), gains[1, 0:1]).astype(BF16)
    write_quarter(cells, 1 - ROW_HALF[quarter], window_half(quarter), normed.astype(F32))


def ready_kernel(near, from_lon, from_both, gains, cells):
    write_normed(cells, 0, near[...], gains)
    write_normed(cells, 2, unpack_piece(from_lon[...]), gains)
    write_normed(cells, 3, unpack_piece(from_both[...]), gains)


def second_kernel(given, from_lat, bias, gains, qkv_weight, proj, query_choice, own, sent_lat, sent_lon, sent_both, cells, results):
    cells[...] = given[...]
    write_normed(cells, 1, unpack_piece(from_lat[...]), gains)
    normed = jnp.concatenate([read_window(cells, 2 * p + 1) for p in range(WINDOWS)], axis=0).astype(BF16)
    blended = []
    for p, (q, k, v) in enumerate(project(normed, qkv_weight[...], query_choice)):

        def bias_of(h):
            return bias[p, h * TOKENS : (h + 1) * TOKENS].astype(F32) - SHIFT

        blended.append(blend(score(q, k), v, bias_of))
    write_attended(results, 1, blended, query_choice, proj[...])
    pieces = [read_quarter(results, 1 - ROW_HALF[k], window_half(k)).astype(BF16) for k in range(4)]
    own[...] = pieces[0]
    sent_lat[...] = pack_piece(pieces[1])
    sent_lon[...] = pack_piece(pieces[2])
    sent_both[...] = pack_piece(pieces[3])


def own_kernel(fc1, fc2, merge, keep, near, own, gains, result, *refs):
    copies = fetch((fc1, fc2, merge), refs[:3], refs[3])
    middle = near[...].astype(F32) + own[...].astype(F32)
    for copy in copies:
        copy.wait()
    result[...] = feed_forward(middle, gains[1, 1:2], refs[0][...], refs[1][...], keep[1][:, :1] > 0)


def add_kernel(far, from_lon, from_both, middle):
    for at, piece in enumerate((from_lon, from_both)):
        inputs = far[(at + 1) * TOKENS : (at + 2) * TOKENS].astype(F32)
        middle[at] = inputs + unpack_piece(piece[...]).astype(F32)


def last_kernel(keep, far, done, middle, from_lat, gains, fc1, fc2, merge_gain, merge_weight, merged):
    upper = far[:TOKENS].astype(F32) + unpack_piece(from_lat[...]).astype(F32)
    fresh = finished((1, 2, 3), [upper, middle[0], middle[1]], gains[1, 1:2], fc1, fc2, keep).astype(F32)
    results = [done[...].astype(F32)] + [fresh[at * TOKENS : (at + 1) * TOKENS] for at in range(3)]
    odd = lax.rem(lax.axis_index("lat"), 2) == 1
    groups = {}
    for qr, (first, second) in enumerate(((1, 3), (0, 2))):
        turned_round = odd if qr == 1 else jnp.logical_not(odd)
        right = jnp.where(turned_round, results[second], results[first])
        left = jnp.where(turned_round, results[first], results[second])
        for qc, result in enumerate((left, right)):
            for r in range(3):
                for c in range(6):
                    at = (c * 3 + r) * LEVELS
                    groups[3 * qr + r, 6 * qc + c] = result[at : at + LEVELS]
    parts = [
        jnp.concatenate([groups[2 * r + dr, 2 * c + dc] for r in range(3) for c in range(6)], axis=0)
        for dr in range(2)
        for dc in range(2)
    ]
    average = sum(jnp.sum(part, axis=-1, keepdims=True) for part in parts) / (4 * C)
    parts = [part - average for part in parts]
    spread = sum(jnp.sum(part * part, axis=-1, keepdims=True) for part in parts) / (4 * C)
    scale = lax.rsqrt(spread + 1e-05)
    total = jnp.zeros((TOKENS, 2 * C), F32)
    for d, part in enumerate(parts):
        normed = (part * scale * merge_gain[d : d + 1]).astype(BF16)
        total = total + dot(normed, merge_weight[d * C : (d + 1) * C])
    merged[...] = total.astype(BF16)


VMEM_SPEC = pl.BlockSpec(memory_space=pltpu.VMEM)
SMEM_SPEC = pl.BlockSpec(memory_space=pltpu.SMEM)


def call(kernel, name, micros, outs, scratch, *operands, in_specs=None, aliases=None):
    return pl.pallas_call(
        kernel,
        name=name,
        out_shape=outs,
        in_specs=in_specs or [VMEM_SPEC] * len(operands),
        out_specs=jax.tree.map(lambda _: VMEM_SPEC, outs),
        scratch_shapes=scratch,
        input_output_aliases=aliases or {},
        cost_estimate=pl.CostEstimate(flops=int(micros * 1e9), bytes_accessed=2**20, transcendentals=0),
        compiler_params=pltpu.CompilerParams(vmem_limit_bytes=16 * 2**20),
    )(*operands)


def shape(*dims, dtype=BF16):
    return jax.ShapeDtypeStruct(dims, dtype)


def sent(block, rows, across, back=False):
    route = []
    for i in range(LATS):
        for j in range(LONS):
            to = (i + rows) % LATS
            owner = i if back else to
            step = (1 if owner % 2 == 1 else -1) * (-1 if back else 1)
            route.append((i * LONS + j, to * LONS + (j + across * step) % LONS))
    return lax.ppermute(block, ("lat", "lon"), route)


def turned(block, place):
    route = []
    for j in range(LONS):
        z, x, core = place(j // 8, j // 2 % 4, j % 2)
        route.append((j, z * 8 + x * 2 + core))
    return lax.ppermute(block, "lon", route)


def shards(state, lat_valid, norm_gains, qkv_weight, proj_weight, fc1_weight, fc2_weight, earth_bias, merge_gain, merge_weight):
    shard = earth_bias[:, 0]
    cells = pltpu.VMEM((2, CELLS, GROUP), F32)
    cell_rows = shape(2, CELLS, GROUP, dtype=F32)
    t_scratch = [pltpu.VMEM((768, KEYS), BF16), pltpu.VMEM((768, KEYS), BF16)]
    packed = shape(224, 128)

    def in_hbm(array):
        return pltpu.with_memory_space_constraint(array, pltpu.HBM)

    def like(arrays):
        return [shape(*array.shape, dtype=array.dtype) for array in arrays]

    hbm_spec = pl.BlockSpec(memory_space=pltpu.HBM)
    fc2_turned = jnp.swapaxes(fc2_weight, 1, 2)
    early = [
        shard[None],
        state.transpose(1, 2, 0, 3).reshape(CELLS, C),
        norm_gains,
        qkv_weight,
        jnp.stack([one_hot(query_order(), TOKENS), one_hot(natural_order(), TOKENS)]),
    ]
    late = [qkv_weight, proj_weight]
    layer = [shape(C, C), shape(C, HIDDEN), shape(C, HIDDEN)]
    other_half = turned(shard, lambda z, x, core: (1 - z, x, core))
    held_shard, x, gains, qkv0, query_choice, first_mask, second_mask, keep = call(
        functools.partial(sliced, fetch_kernel, {4: 0}),
        "fetch",
        1.4,
        like(early[:3])
        + [shape(C, 3 * C)]
        + like(early[4:])
        + [
            shape(8, KEYS, dtype=F32),
            shape(2, TOKENS, KEYS, dtype=F32),
            shape(2, TOKENS, GROUP, dtype=F32),
        ],
        [pltpu.SMEM((LATS * ROWS,), jnp.int32), pltpu.SemaphoreType.DMA((len(early) + 1,))],
        in_hbm(lat_valid),
        *[in_hbm(array) for array in early],
        in_specs=[hbm_spec] * (len(early) + 1),
    )
    halves = call(join_kernel, "halves", 0.2, shape(2, 2, WINDOWS, SHARD), [], held_shard, other_half[None])
    ring = {hop: turned(halves, lambda z, x, core: (z, (x + hop) % 4, core)) for hop in (2, 1, 3)}
    scores, v, inputs, qkv1, proj1 = call(
        functools.partial(sliced, before_kernel, {5: 1, 6: 1}),
        "before",
        2.5,
        [shape(WINDOWS, HEADS * TOKENS, KEYS, dtype=F32), shape(WINDOWS, KEYS, KEYS), cell_rows]
        + [shape(C, 3 * C), shape(C, C)],
        [pltpu.SemaphoreType.DMA((len(late),))],
        halves, x, gains, qkv0, query_choice,
        *[in_hbm(array) for array in late],
        in_specs=[VMEM_SPEC] * 5 + [hbm_spec] * len(late),
    )
    mine = call(join_kernel, "mine", 0.3, shape(8, 2, WINDOWS, SHARD), [], halves, ring[1], ring[2], ring[3], v)
    theirs = turned(mine, lambda z, x, core: (z, x, 1 - core))
    proj0, fc1_0, fc2_0, lanes, rows, columns = call(
        functools.partial(sliced, prepare_kernel, {1: 0, 2: 0, 3: 0}),
        "prepare",
        1.2,
        layer + [shape(HALF, KEYS), shape(2, 256, 192), shape(2, HALF, 6 * GROUP)],
        [pltpu.SemaphoreType.DMA((3,))],
        mine, in_hbm(proj_weight), in_hbm(fc1_weight), in_hbm(fc2_turned),
        in_specs=[VMEM_SPEC] + [hbm_spec] * 3,
    )
    to_lat, to_lon, to_both, tables, far, attended = call(
        first_kernel,
        "first",
        4.5,
        [packed, packed, packed, shape(1152, KEYS), shape(3 * TOKENS, C), cell_rows],
        [pltpu.VMEM((1152, KEYS), F32)] + t_scratch,
        mine, theirs, scores, v, first_mask, keep, inputs, gains, query_choice, proj0, fc1_0, fc2_0, lanes, rows,
    )
    from_lat, from_lon, from_both = sent(to_lat, -1, 0), sent(to_lon, 0, 1), sent(to_both, -1, 1)
    bias, near = call(
        bias_kernel,
        "bias",
        0.2,
        [shape(WINDOWS, HEADS * TOKENS, KEYS), shape(TOKENS, C)],
        [pltpu.VMEM((768, 768), F32), pltpu.VMEM((768, 768), F32)],
        tables, second_mask, columns, rows, inputs, attended, gains, fc1_0, fc2_0, keep,
    )
    ready = call(ready_kernel, "ready", 0.4, cell_rows, [], near, from_lon, from_both, gains)
    own, to_lat, to_lon, to_both = call(
        second_kernel,
        "second",
        4.5,
        [shape(TOKENS, C), packed, packed, packed],
        [cells, cells],
        ready, from_lat, bias, gains, qkv1, proj1, query_choice,
    )
    from_lon, from_both, from_lat = sent(to_lon, 0, 1, True), sent(to_both, 1, 1, True), sent(to_lat, 1, 0, True)
    done, fc1_1, fc2_1, merge = call(
        functools.partial(sliced, own_kernel, {0: 1, 1: 1}),
        "own",
        0.5,
        [shape(TOKENS, C)] + layer[1:] + like([merge_weight]),
        [pltpu.SemaphoreType.DMA((3,))],
        in_hbm(fc1_weight), in_hbm(fc2_turned), in_hbm(merge_weight), keep, near, own, gains,
        in_specs=[hbm_spec] * 3 + [VMEM_SPEC] * 4,
    )
    middle = call(
        add_kernel, "add", 0.2, shape(2, TOKENS, C, dtype=F32), [], far, from_lon, from_both
    )
    merged = call(
        last_kernel,
        "last",
        2.0,
        shape(TOKENS, 2 * C),
        [],
        keep, far, done, middle, from_lat, gains, fc1_1, fc2_1, merge_gain.reshape(4, C), merge,
    )
    return merged.reshape(3, 6, LEVELS, 2 * C).transpose(2, 0, 1, 3)


def solution(mesh):
    return jax.shard_map(
        shards,
        mesh=mesh,
        in_specs=(
            P(None, "lat", "lon", None),
            P(),
            P(),
            P(),
            P(),
            P(),
            P(),
            P(None, "lat", None, "lon"),
            P(),
            P(),
        ),
        out_specs=P(None, "lat", "lon", None),
        check_vma=False,
    )
```

```python
import functools

import jax
import jax.numpy as jnp
import numpy as np
from jax import lax
from jax.experimental import pallas as pl
from jax.experimental.pallas import tpu as pltpu
from jax.sharding import PartitionSpec as P

BF16 = jnp.bfloat16
F32 = jnp.float32
C = 192
HEADS = 6
HEAD_SIZE = 32
HIDDEN = 768
LEVELS, ROWS, COLS = 8, 6, 12
WINDOWS = 4
TOKENS = 144
CELLS = 576
RUN = 24
SPAN = 23
HALF = 6 * SPAN
GROUP = 128
KEYS = 2 * GROUP
LATS, LONS = 8, 16
SHARD = 1242
SHIFT = 12.0
MASKED = -1e30


def one_hot(sources, width):
    sources = np.asarray(sources)
    matrix = np.zeros((len(sources), width), np.float32)
    rows = np.nonzero(sources >= 0)[0]
    matrix[rows, sources[rows]] = 1.0
    return jnp.asarray(matrix, BF16)


ROW_HALF = (1, 0, 1, 0)


def own_half(quarter):
    odd = lax.rem(lax.axis_index("lat"), 2)
    return (1 - odd, odd, odd, 1 - odd)[quarter]


def window_half(quarter):
    odd = lax.rem(lax.axis_index("lat"), 2)
    return (odd, odd, 1 - odd, 1 - odd)[quarter]


def query_order():
    return [level * 72 + c * 6 + r for c in range(COLS) for level in range(2) for r in range(ROWS)]


def natural_order():
    return [c * 12 + level * 6 + r for level in range(2) for c in range(COLS) for r in range(ROWS)]


def quarter_runs(qr, qc):
    starts = [qc * (6 * ROWS * LEVELS) + (c * ROWS + 3 * qr) * LEVELS for c in range(6)]
    return [pl.ds(pl.multiple_of(start, LEVELS), RUN) for start in starts]


def level_cells(level):
    return pl.ds(level, ROWS * COLS, stride=LEVELS)


def read_window(cells, first_level):
    parts = [
        jnp.concatenate([cells[0, level_cells(level % LEVELS)], cells[1, level_cells(level % LEVELS)]], axis=1)
        for level in (first_level, first_level + 1)
    ]
    return jnp.concatenate(parts, axis=0)[:, :C]


def write_window(cells, first_level, values):
    wide = jnp.concatenate([values, jnp.zeros((TOKENS, 2 * GROUP - C), F32)], axis=1)
    for offset in range(2):
        rows = wide[offset * 72 : (offset + 1) * 72]
        where = level_cells((first_level + offset) % LEVELS)
        cells[0, where] = rows[:, :GROUP]
        cells[1, where] = rows[:, GROUP:]


def read_quarter(cells, qr, qc):
    parts = [jnp.concatenate([cells[0, run, :], cells[1, run, :]], axis=1) for run in quarter_runs(qr, qc)]
    return jnp.concatenate(parts, axis=0)[:, :C]


def write_quarter(cells, qr, qc, values):
    wide = jnp.concatenate([values, jnp.zeros((TOKENS, 2 * GROUP - C), F32)], axis=1)
    for c, run in enumerate(quarter_runs(qr, qc)):
        cells[0, run, :] = wide[c * RUN : (c + 1) * RUN, :GROUP]
        cells[1, run, :] = wide[c * RUN : (c + 1) * RUN, GROUP:]


def layer_norm(values, scales):
    average = jnp.mean(values, axis=-1, keepdims=True)
    centred = values - average
    spread = jnp.mean(centred * centred, axis=-1, keepdims=True)
    return centred * lax.rsqrt(spread + 1e-05) * scales


def dot(a, b):
    return jnp.dot(a, b, preferred_element_type=F32)


def dot_transposed(a, b):
    return lax.dot_general(a, b, (((1,), (1,)), ((), ())), preferred_element_type=F32)


def moved(choice, rows):
    return dot(choice, rows).astype(BF16)


def head_lanes(head):
    lane = lax.broadcasted_iota(jnp.int32, (1, C), 1)
    return (lane >= head * HEAD_SIZE) & (lane < (head + 1) * HEAD_SIZE)


def project(normed, qkv_weight, orders):
    all_queries = dot(normed, qkv_weight[:, :C]).astype(BF16)
    all_keys = dot(normed, qkv_weight[:, C : 2 * C])
    all_values = dot(normed, qkv_weight[:, 2 * C :])
    pad = jnp.zeros((GROUP - 72, C), F32)
    ones = jnp.ones((KEYS, KEYS - C), BF16)

    def padded(part):
        return jnp.concatenate([part[:72], pad, part[72:], pad], axis=0).astype(BF16)

    results = []
    for p in range(WINDOWS):
        rows = slice(p * TOKENS, (p + 1) * TOKENS)
        values = jnp.concatenate([padded(all_values[rows]), ones], axis=1)
        results.append((moved(orders[0], all_queries[rows]), padded(all_keys[rows]), values))
    return results


def write_attended(cells, first_level, blended, orders, proj):
    natural = jnp.concatenate([moved(orders[1], part) for part in blended], axis=0)
    attended = dot(natural, proj)
    for p in range(WINDOWS):
        write_window(cells, 2 * p + first_level, attended[p * TOKENS : (p + 1) * TOKENS])


def score(queries, keys):
    stacked = jnp.concatenate(
        [jnp.where(head_lanes(h), queries, jnp.zeros((), BF16)) for h in range(HEADS)], axis=0
    )
    return dot_transposed(stacked, keys) * HEAD_SIZE ** (-0.5)


def blend(scores, values, bias_of):
    weights = []
    for h in range(HEADS):
        part = scores[h * TOKENS : (h + 1) * TOKENS] + bias_of(h)
        weights.append(jnp.exp(part).astype(BF16))
    blended = dot(jnp.concatenate(weights, axis=0), values)
    total = jnp.zeros((TOKENS, C), F32)
    result = jnp.zeros((TOKENS, C), F32)
    for h in range(HEADS):
        part = blended[h * TOKENS : (h + 1) * TOKENS]
        result = jnp.where(head_lanes(h), part[:, :C], result)
        total = jnp.where(head_lanes(h), part[:, C : C + 1], total)
    return (result / jnp.maximum(total, np.exp(-SHIFT))).astype(BF16)


def selected_bias(z_even, z_odd, window, head):
    rows = []
    for at in range(6):
        lanes = slice(at * GROUP, (at + 1) * GROUP)
        halves = []
        for key_level in range(2):
            first = head * 128 + (key_level * 4 + window) * 16
            top = z_even[first : first + 16, lanes]
            low = z_odd[first : first + 16, lanes]
            halves.append(jnp.concatenate([top[:8], top[8:] + low[:8], low[8:]], axis=0))
        rows.append(jnp.concatenate(halves, axis=1))
    return jnp.concatenate(rows, axis=0)


def window_lanes(tile, first):
    turn = (GROUP - first) % GROUP
    near = pltpu.roll(tile[:, :GROUP], turn, 1) if turn else tile[:, :GROUP]
    if first + 72 <= GROUP:
        return near
    lane = lax.broadcasted_iota(jnp.int32, (1, GROUP), 1)
    return jnp.where(lane < GROUP - first, near, pltpu.roll(tile[:, GROUP:], turn, 1))


def expanded_bias(t_top, t_low, window, head):
    halves = []
    for key_level in range(2):
        first = head * 128 + (key_level * 4 + window) * 16
        top_tile, low_tile = t_top[first : first + 16], t_low[first : first + 16]
        rows = []
        for column in range(0, 12, 2):
            top = window_lanes(top_tile, (11 - column) * ROWS).astype(F32)
            low = window_lanes(low_tile, (10 - column) * ROWS).astype(F32)
            rows += [top[:8], top[8:] + low[:8], low[8:]]
        halves.append(jnp.concatenate(rows, axis=0))
    return jnp.concatenate(halves, axis=1)


def picked_rows(table_ref, table_choice):
    tops, lows = [], []
    for h in range(HEADS):
        picked = moved(table_choice, table_ref[h * 192 : (h + 1) * 192, :HALF])
        tops.append(picked[:128])
        lows.append(picked[128:])
    return jnp.concatenate(tops, axis=0), jnp.concatenate(lows, axis=0)


def erf_gelu(values):
    return 0.5 * values * (1.0 + lax.erf(values * np.float32(np.sqrt(0.5))))


def feed_forward(middle, gain, fc1, fc2, keep):
    hidden = erf_gelu(dot(layer_norm(middle, gain).astype(BF16), fc1)).astype(BF16)
    return jnp.where(keep, middle + dot_transposed(hidden, fc2), 0.0).astype(BF16)


def finished(quarters, middle, gain, fc1, fc2, keep):
    flags = jnp.concatenate([keep[ROW_HALF[quarter]][:, :1] for quarter in quarters], axis=0) > 0
    return feed_forward(jnp.concatenate(middle, axis=0), gain, fc1[...], fc2[...], flags)


def pack_piece(piece):
    side = jnp.concatenate(
        [piece[:80, 128:], jnp.concatenate([piece[80:, 128:], piece[:16, 128:]], axis=0)], axis=1
    )
    return jnp.concatenate([piece[:, :128], side], axis=0)


def unpack_piece(packed):
    side = packed[TOKENS:]
    ends = jnp.concatenate([side[:, :64], side[: TOKENS - 80, 64:]], axis=0)
    return jnp.concatenate([packed[:TOKENS], ends], axis=1)


def prepare_masks(lat_valid, first_mask, second_mask, keep):
    lat = lax.axis_index("lat")

    def flag(row):
        return lat_valid[row] > 0

    lane = lax.broadcasted_iota(jnp.int32, (8, KEYS), 1)
    inner = lax.rem(lane, GROUP)
    key_row = jnp.where(inner < 72, lax.rem(inner, ROWS), -1)
    mask = jnp.full((8, KEYS), MASKED, F32)
    usable = jnp.full((8, KEYS), MASKED, F32)
    for r in range(ROWS):
        mask = jnp.where((key_row == r) & flag(lat * ROWS + r), -SHIFT, mask)
        rolled = lax.rem(lat * ROWS + 3 + r, LATS * ROWS)
        usable = jnp.where((key_row == r) & flag(rolled), 0.0, usable)
    first_mask[...] = mask
    a = lax.rem(lax.broadcasted_iota(jnp.int32, (TOKENS, 1), 0), 12)
    query_half = jnp.where(lax.rem(a, ROWS) >= 3, 1, 0)
    key_half = jnp.where(key_row[:1] >= 3, 1, 0)
    same_rows = (query_half == key_half) | (lat != LATS - 1)
    same_level = jnp.where(a >= ROWS, 1, 0) == jnp.where(lane[:1] >= GROUP, 1, 0)
    whole = jnp.where(same_rows, usable[:1], MASKED)
    second_mask[0] = whole
    second_mask[1] = jnp.where(same_level, whole, MASKED)
    for half in range(2):
        for r in range(3):
            value = jnp.where(flag(lat * ROWS + 3 * half + r), 1.0, 0.0)
            for c in range(6):
                at = (c * 3 + r) * LEVELS
                keep[half, at : at + LEVELS] = jnp.full((LEVELS, GROUP), value, F32)


def fetch(sources, held, sems):
    copies = [pltpu.make_async_copy(a, b, sems.at[n]) for n, (a, b) in enumerate(zip(sources, held))]
    for copy in copies:
        copy.start()
    return copies


def sliced(kernel, layers, *refs):
    kernel(*[ref.at[layers[at]] if at in layers else ref for at, ref in enumerate(refs)])


def fetch_kernel(*refs):
    sources, held, (first_mask, second_mask, keep, flags, sems) = refs[:6], refs[6:11], refs[11:]
    copies = fetch(sources, (flags,) + tuple(held), sems)
    copies[0].wait()
    prepare_masks(flags, first_mask, second_mask, keep)
    for copy in copies[1:]:
        copy.wait()


def choose(row_keys, lane_keys):
    return jnp.where(row_keys == lane_keys, 1.0, 0.0).astype(BF16)


def prepare_kernel(mine, proj, fc1, fc2, *refs):
    copies = fetch((proj, fc1, fc2), refs[:3], refs[-1])
    lanes, rows, columns = refs[3:6]

    def place(shape, axis):
        return lax.broadcasted_iota(jnp.int32, shape, axis)

    at = place((HALF, 1), 0)
    row, position = at // SPAN, lax.rem(at, SPAN)
    lanes[...] = choose(position * ROWS + row, place((HALF, KEYS), 1))
    at = place((256, 1), 0)
    a = lax.rem(at, 16) - 4 * (at // 128)
    source = (a * 2 + lax.rem(at // 64, 2)) * 8 + lax.rem(at // 16, 4)
    for block in range(2):
        rows[block] = choose(jnp.where((a >= 0) & (a < 12), source + 4 * block, -1), place((256, 192), 1))
    lane = place((1, 6 * GROUP), 1)
    inner = lax.rem(lane, GROUP)
    for parity in range(2):
        met = inner // ROWS - (lane // GROUP * 2 + parity) + 11
        wanted = jnp.where(inner < 72, met * ROWS + lax.rem(inner, ROWS), -1)
        columns[parity] = choose(position * ROWS + row, wanted)
    for copy in copies:
        copy.wait()


def join_kernel(*refs):
    at = 0
    for ref in refs[:-1]:
        if ref.shape[1:] == refs[-1].shape[1:]:
            refs[-1][at : at + ref.shape[0]] = ref[...]
            at += ref.shape[0]


def before_kernel(halves, x, gains, qkv_weight, query_choice, *refs):
    sources, (scores_out, v_out, cells), held, sems = refs[:2], refs[2:5], refs[5:7], refs[7]
    copies = fetch(sources, held, sems)
    wide = jnp.concatenate([x[...].astype(F32), jnp.zeros((CELLS, 2 * GROUP - C), F32)], axis=1)
    for r in range(ROWS):
        for c in range(COLS):
            group = wide[(r * COLS + c) * LEVELS : (r * COLS + c + 1) * LEVELS]
            at = (c * ROWS + r) * LEVELS
            cells[0, at : at + LEVELS] = group[:, :GROUP]
            cells[1, at : at + LEVELS] = group[:, GROUP:]
    windows = jnp.concatenate([read_window(cells, 2 * p) for p in range(WINDOWS)], axis=0)
    normed = layer_norm(windows, gains[0, 0:1]).astype(BF16)
    for p, (q, k, v) in enumerate(project(normed, qkv_weight[...], query_choice)):
        v_out[p] = v
        scores_out[p] = score(q, k)
    for copy in copies:
        copy.wait()


def first_quarters(quarters, inputs, cells, gains, fc1, fc2, keep):
    middle = []
    for quarter in quarters:
        qr, qc = ROW_HALF[quarter], own_half(quarter)
        middle.append(read_quarter(inputs, qr, qc) + read_quarter(cells, qr, qc).astype(BF16).astype(F32))
    return finished(quarters, middle, gains[0, 1:2], fc1, fc2, keep)


def first_kernel(mine, theirs, scores, v, first_mask, keep, inputs, gains, query_choice, proj, fc1, fc2, lanes, rows, sent_lat, sent_lon, sent_both, table_out, out, cells, table_f32, t_top, t_low):
    me = lax.axis_index("lon")
    for g in range(LONS):
        hops = lax.rem(me // 2 - g // 2 + 8, 4)
        slot = jnp.where(hops == 1, 2, jnp.where(hops == 2, 1, hops)) * 2 + jnp.where(me // 8 == g // 8, 0, 1)
        shard = jnp.where(lax.rem(me, 2) == g % 2, mine[slot], theirs[slot]).astype(F32)
        piece = jnp.concatenate([shard[0], shard[1]], axis=0)
        for n in range(9):
            at = (g * 9 + n) * 8
            table_f32[at : at + 8, :HALF] = piece[:, n * HALF : (n + 1) * HALF]
    table_out[:, :HALF] = table_f32[:, :HALF].astype(BF16)
    tops, lows = picked_rows(table_out, rows[0])
    t_top[...] = dot(tops, lanes[...]).astype(BF16)
    t_low[...] = dot(lows, lanes[...]).astype(BF16)
    mask = first_mask[0:1]
    blended = [blend(scores[p], v[p], lambda h: expanded_bias(t_top, t_low, p, h) + mask) for p in range(WINDOWS)]
    write_attended(cells, 0, blended, query_choice, proj[...])
    results = first_quarters((1, 2, 3), inputs, cells, gains, fc1, fc2, keep)
    out[...] = results
    for at, target in enumerate((sent_lat, sent_lon, sent_both)):
        target[...] = pack_piece(results[at * TOKENS : (at + 1) * TOKENS])


def bias_kernel(table, second_mask, columns, rows, inputs, cells, gains, fc1, fc2, keep, bias_out, near, z_even, z_odd):
    near[...] = first_quarters((0,), inputs, cells, gains, fc1, fc2, keep)
    tops, lows = picked_rows(table, rows[1])
    z_even[...] = dot(tops, columns[0])
    z_odd[...] = dot(lows, columns[1])
    for p in range(WINDOWS):
        for h in range(HEADS):
            whole = selected_bias(z_even, z_odd, p, h) + second_mask[1 if p == WINDOWS - 1 else 0]
            bias_out[p, h * TOKENS : (h + 1) * TOKENS] = whole.astype(BF16)


def write_normed(cells, quarter, piece, gains):
    normed = layer_norm(piece.astype(F32), gains[1, 0:1]).astype(BF16)
    write_quarter(cells, 1 - ROW_HALF[quarter], window_half(quarter), normed.astype(F32))


def ready_kernel(near, from_lon, from_both, gains, cells):
    write_normed(cells, 0, near[...], gains)
    write_normed(cells, 2, unpack_piece(from_lon[...]), gains)
    write_normed(cells, 3, unpack_piece(from_both[...]), gains)


def second_kernel(given, from_lat, bias, gains, qkv_weight, proj, query_choice, own, sent_lat, sent_lon, sent_both, cells, results):
    cells[...] = given[...]
    write_normed(cells, 1, unpack_piece(from_lat[...]), gains)
    normed = jnp.concatenate([read_window(cells, 2 * p + 1) for p in range(WINDOWS)], axis=0).astype(BF16)
    blended = []
    for p, (q, k, v) in enumerate(project(normed, qkv_weight[...], query_choice)):

        def bias_of(h):
            return bias[p, h * TOKENS : (h + 1) * TOKENS].astype(F32) - SHIFT

        blended.append(blend(score(q, k), v, bias_of))
    write_attended(results, 1, blended, query_choice, proj[...])
    pieces = [read_quarter(results, 1 - ROW_HALF[k], window_half(k)).astype(BF16) for k in range(4)]
    own[...] = pieces[0]
    sent_lat[...] = pack_piece(pieces[1])
    sent_lon[...] = pack_piece(pieces[2])
    sent_both[...] = pack_piece(pieces[3])


def own_kernel(fc1, fc2, merge, keep, near, own, gains, result, *refs):
    copies = fetch((fc1, fc2, merge), refs[:3], refs[3])
    middle = near[...].astype(F32) + own[...].astype(F32)
    for copy in copies:
        copy.wait()
    result[...] = feed_forward(middle, gains[1, 1:2], refs[0][...], refs[1][...], keep[1][:, :1] > 0)


def add_kernel(far, from_lon, from_both, middle):
    for at, piece in enumerate((from_lon, from_both)):
        inputs = far[(at + 1) * TOKENS : (at + 2) * TOKENS].astype(F32)
        middle[at] = inputs + unpack_piece(piece[...]).astype(F32)


def last_kernel(keep, far, done, middle, from_lat, gains, fc1, fc2, merge_gain, merge_weight, merged):
    upper = far[:TOKENS].astype(F32) + unpack_piece(from_lat[...]).astype(F32)
    fresh = finished((1, 2, 3), [upper, middle[0], middle[1]], gains[1, 1:2], fc1, fc2, keep).astype(F32)
    results = [done[...].astype(F32)] + [fresh[at * TOKENS : (at + 1) * TOKENS] for at in range(3)]
    odd = lax.rem(lax.axis_index("lat"), 2) == 1
    groups = {}
    for qr, (first, second) in enumerate(((1, 3), (0, 2))):
        turned_round = odd if qr == 1 else jnp.logical_not(odd)
        right = jnp.where(turned_round, results[second], results[first])
        left = jnp.where(turned_round, results[first], results[second])
        for qc, result in enumerate((left, right)):
            for r in range(3):
                for c in range(6):
                    at = (c * 3 + r) * LEVELS
                    groups[3 * qr + r, 6 * qc + c] = result[at : at + LEVELS]
    parts = [
        jnp.concatenate([groups[2 * r + dr, 2 * c + dc] for r in range(3) for c in range(6)], axis=0)
        for dr in range(2)
        for dc in range(2)
    ]
    average = sum(jnp.sum(part, axis=-1, keepdims=True) for part in parts) / (4 * C)
    parts = [part - average for part in parts]
    spread = sum(jnp.sum(part * part, axis=-1, keepdims=True) for part in parts) / (4 * C)
    scale = lax.rsqrt(spread + 1e-05)
    total = jnp.zeros((TOKENS, 2 * C), F32)
    for d, part in enumerate(parts):
        normed = (part * scale * merge_gain[d : d + 1]).astype(BF16)
        total = total + dot(normed, merge_weight[d * C : (d + 1) * C])
    merged[...] = total.astype(BF16)


VMEM_SPEC = pl.BlockSpec(memory_space=pltpu.VMEM)
SMEM_SPEC = pl.BlockSpec(memory_space=pltpu.SMEM)


def call(kernel, name, micros, outs, scratch, *operands, in_specs=None, aliases=None):
    return pl.pallas_call(
        kernel,
        name=name,
        out_shape=outs,
        in_specs=in_specs or [VMEM_SPEC] * len(operands),
        out_specs=jax.tree.map(lambda _: VMEM_SPEC, outs),
        scratch_shapes=scratch,
        input_output_aliases=aliases or {},
        cost_estimate=pl.CostEstimate(flops=int(micros * 1e9), bytes_accessed=2**20, transcendentals=0),
        compiler_params=pltpu.CompilerParams(vmem_limit_bytes=16 * 2**20),
    )(*operands)


def shape(*dims, dtype=BF16):
    return jax.ShapeDtypeStruct(dims, dtype)


def sent(block, rows, across, back=False):
    route = []
    for i in range(LATS):
        for j in range(LONS):
            to = (i + rows) % LATS
            owner = i if back else to
            step = (1 if owner % 2 == 1 else -1) * (-1 if back else 1)
            route.append((i * LONS + j, to * LONS + (j + across * step) % LONS))
    return lax.ppermute(block, ("lat", "lon"), route)


def turned(block, place):
    route = []
    for j in range(LONS):
        z, x, core = place(j // 8, j // 2 % 4, j % 2)
        route.append((j, z * 8 + x * 2 + core))
    return lax.ppermute(block, "lon", route)


def shards(state, lat_valid, norm_gains, qkv_weight, proj_weight, fc1_weight, fc2_weight, earth_bias, merge_gain, merge_weight):
    shard = earth_bias[:, 0]
    cells = pltpu.VMEM((2, CELLS, GROUP), F32)
    cell_rows = shape(2, CELLS, GROUP, dtype=F32)
    t_scratch = [pltpu.VMEM((768, KEYS), BF16), pltpu.VMEM((768, KEYS), BF16)]
    packed = shape(224, 128)

    def in_hbm(array):
        return pltpu.with_memory_space_constraint(array, pltpu.HBM)

    def like(arrays):
        return [shape(*array.shape, dtype=array.dtype) for array in arrays]

    hbm_spec = pl.BlockSpec(memory_space=pltpu.HBM)
    fc2_turned = jnp.swapaxes(fc2_weight, 1, 2)
    early = [
        shard[None],
        state.transpose(1, 2, 0, 3).reshape(CELLS, C),
        norm_gains,
        qkv_weight,
        jnp.stack([one_hot(query_order(), TOKENS), one_hot(natural_order(), TOKENS)]),
    ]
    late = [qkv_weight, proj_weight]
    layer = [shape(C, C), shape(C, HIDDEN), shape(C, HIDDEN)]
    other_half = turned(shard, lambda z, x, core: (1 - z, x, core))
    held_shard, x, gains, qkv0, query_choice, first_mask, second_mask, keep = call(
        functools.partial(sliced, fetch_kernel, {4: 0}),
        "fetch",
        1.4,
        like(early[:3])
        + [shape(C, 3 * C)]
        + like(early[4:])
        + [
            shape(8, KEYS, dtype=F32),
            shape(2, TOKENS, KEYS, dtype=F32),
            shape(2, TOKENS, GROUP, dtype=F32),
        ],
        [pltpu.SMEM((LATS * ROWS,), jnp.int32), pltpu.SemaphoreType.DMA((len(early) + 1,))],
        in_hbm(lat_valid),
        *[in_hbm(array) for array in early],
        in_specs=[hbm_spec] * (len(early) + 1),
    )
    halves = call(join_kernel, "halves", 0.2, shape(2, 2, WINDOWS, SHARD), [], held_shard, other_half[None])
    ring = [turned(halves, lambda z, x, core: (z, (x + hop) % 4, core)) for hop in range(1, 4)]
    scores, v, inputs, qkv1, proj1 = call(
        functools.partial(sliced, before_kernel, {5: 1, 6: 1}),
        "before",
        2.5,
        [shape(WINDOWS, HEADS * TOKENS, KEYS, dtype=F32), shape(WINDOWS, KEYS, KEYS), cell_rows]
        + [shape(C, 3 * C), shape(C, C)],
        [pltpu.SemaphoreType.DMA((len(late),))],
        halves, x, gains, qkv0, query_choice,
        *[in_hbm(array) for array in late],
        in_specs=[VMEM_SPEC] * 5 + [hbm_spec] * len(late),
    )
    mine = call(join_kernel, "mine", 0.3, shape(8, 2, WINDOWS, SHARD), [], halves, ring[1], ring[0], ring[2], v)
    theirs = turned(mine, lambda z, x, core: (z, x, 1 - core))
    proj0, fc1_0, fc2_0, lanes, rows, columns = call(
        functools.partial(sliced, prepare_kernel, {1: 0, 2: 0, 3: 0}),
        "prepare",
        1.2,
        layer + [shape(HALF, KEYS), shape(2, 256, 192), shape(2, HALF, 6 * GROUP)],
        [pltpu.SemaphoreType.DMA((3,))],
        mine, in_hbm(proj_weight), in_hbm(fc1_weight), in_hbm(fc2_turned),
        in_specs=[VMEM_SPEC] + [hbm_spec] * 3,
    )
    to_lat, to_lon, to_both, tables, far, attended = call(
        first_kernel,
        "first",
        4.5,
        [packed, packed, packed, shape(1152, KEYS), shape(3 * TOKENS, C), cell_rows],
        [pltpu.VMEM((1152, KEYS), F32)] + t_scratch,
        mine, theirs, scores, v, first_mask, keep, inputs, gains, query_choice, proj0, fc1_0, fc2_0, lanes, rows,
    )
    from_lat, from_lon, from_both = sent(to_lat, -1, 0), sent(to_lon, 0, 1), sent(to_both, -1, 1)
    bias, near = call(
        bias_kernel,
        "bias",
        0.2,
        [shape(WINDOWS, HEADS * TOKENS, KEYS), shape(TOKENS, C)],
        [pltpu.VMEM((768, 768), F32), pltpu.VMEM((768, 768), F32)],
        tables, second_mask, columns, rows, inputs, attended, gains, fc1_0, fc2_0, keep,
    )
    ready = call(ready_kernel, "ready", 0.4, cell_rows, [], near, from_lon, from_both, gains)
    own, to_lat, to_lon, to_both = call(
        second_kernel,
        "second",
        4.5,
        [shape(TOKENS, C), packed, packed, packed],
        [cells, cells],
        ready, from_lat, bias, gains, qkv1, proj1, query_choice,
    )
    from_lon, from_both, from_lat = sent(to_lon, 0, 1, True), sent(to_both, 1, 1, True), sent(to_lat, 1, 0, True)
    done, fc1_1, fc2_1, merge = call(
        functools.partial(sliced, own_kernel, {0: 1, 1: 1}),
        "own",
        0.5,
        [shape(TOKENS, C)] + layer[1:] + like([merge_weight]),
        [pltpu.SemaphoreType.DMA((3,))],
        in_hbm(fc1_weight), in_hbm(fc2_turned), in_hbm(merge_weight), keep, near, own, gains,
        in_specs=[hbm_spec] * 3 + [VMEM_SPEC] * 4,
    )
    middle = call(
        add_kernel, "add", 0.2, shape(2, TOKENS, C, dtype=F32), [], far, from_lon, from_both
    )
    merged = call(
        last_kernel,
        "last",
        2.0,
        shape(TOKENS, 2 * C),
        [],
        keep, far, done, middle, from_lat, gains, fc1_1, fc2_1, merge_gain.reshape(4, C), merge,
    )
    return merged.reshape(3, 6, LEVELS, 2 * C).transpose(2, 0, 1, 3)


def solution(mesh):
    return jax.shard_map(
        shards,
        mesh=mesh,
        in_specs=(
            P(None, "lat", "lon", None),
            P(),
            P(),
            P(),
            P(),
            P(),
            P(),
            P(None, "lat", None, "lon"),
            P(),
            P(),
        ),
        out_specs=P(None, "lat", "lon", None),
        check_vma=False,
    )
```

```python
import functools

import jax
import jax.numpy as jnp
import numpy as np
from jax import lax
from jax.experimental import pallas as pl
from jax.experimental.pallas import tpu as pltpu
from jax.sharding import PartitionSpec as P

BF16 = jnp.bfloat16
F32 = jnp.float32
C = 192
HEADS = 6
HEAD_SIZE = 32
HIDDEN = 768
LEVELS, ROWS, COLS = 8, 6, 12
WINDOWS = 4
TOKENS = 144
CELLS = 576
RUN = 24
SPAN = 23
HALF = 6 * SPAN
GROUP = 128
KEYS = 2 * GROUP
LATS, LONS = 8, 16
SHARD = 1242
SHIFT = 12.0
MASKED = -1e30


def one_hot(sources, width):
    sources = np.asarray(sources)
    matrix = np.zeros((len(sources), width), np.float32)
    rows = np.nonzero(sources >= 0)[0]
    matrix[rows, sources[rows]] = 1.0
    return jnp.asarray(matrix, BF16)


ROW_HALF = (1, 0, 1, 0)


def own_half(quarter):
    odd = lax.rem(lax.axis_index("lat"), 2)
    return (1 - odd, odd, odd, 1 - odd)[quarter]


def window_half(quarter):
    odd = lax.rem(lax.axis_index("lat"), 2)
    return (odd, odd, 1 - odd, 1 - odd)[quarter]


def query_order():
    return [level * 72 + c * 6 + r for c in range(COLS) for level in range(2) for r in range(ROWS)]


def natural_order():
    return [c * 12 + level * 6 + r for level in range(2) for c in range(COLS) for r in range(ROWS)]


def quarter_runs(qr, qc):
    starts = [qc * (6 * ROWS * LEVELS) + (c * ROWS + 3 * qr) * LEVELS for c in range(6)]
    return [pl.ds(pl.multiple_of(start, LEVELS), RUN) for start in starts]


def level_cells(level):
    return pl.ds(level, ROWS * COLS, stride=LEVELS)


def read_window(cells, first_level):
    parts = [
        jnp.concatenate([cells[0, level_cells(level % LEVELS)], cells[1, level_cells(level % LEVELS)]], axis=1)
        for level in (first_level, first_level + 1)
    ]
    return jnp.concatenate(parts, axis=0)[:, :C]


def write_window(cells, first_level, values):
    wide = jnp.concatenate([values, jnp.zeros((TOKENS, 2 * GROUP - C), F32)], axis=1)
    for offset in range(2):
        rows = wide[offset * 72 : (offset + 1) * 72]
        where = level_cells((first_level + offset) % LEVELS)
        cells[0, where] = rows[:, :GROUP]
        cells[1, where] = rows[:, GROUP:]


def read_quarter(cells, qr, qc):
    parts = [jnp.concatenate([cells[0, run, :], cells[1, run, :]], axis=1) for run in quarter_runs(qr, qc)]
    return jnp.concatenate(parts, axis=0)[:, :C]


def write_quarter(cells, qr, qc, values):
    wide = jnp.concatenate([values, jnp.zeros((TOKENS, 2 * GROUP - C), F32)], axis=1)
    for c, run in enumerate(quarter_runs(qr, qc)):
        cells[0, run, :] = wide[c * RUN : (c + 1) * RUN, :GROUP]
        cells[1, run, :] = wide[c * RUN : (c + 1) * RUN, GROUP:]


def layer_norm(values, scales):
    average = jnp.mean(values, axis=-1, keepdims=True)
    centred = values - average
    spread = jnp.mean(centred * centred, axis=-1, keepdims=True)
    return centred * lax.rsqrt(spread + 1e-05) * scales


def dot(a, b):
    return jnp.dot(a, b, preferred_element_type=F32)


def dot_transposed(a, b):
    return lax.dot_general(a, b, (((1,), (1,)), ((), ())), preferred_element_type=F32)


def moved(choice, rows):
    return dot(choice, rows).astype(BF16)


def head_lanes(head):
    lane = lax.broadcasted_iota(jnp.int32, (1, C), 1)
    return (lane >= head * HEAD_SIZE) & (lane < (head + 1) * HEAD_SIZE)


def project(normed, qkv_weight, orders):
    all_queries = dot(normed, qkv_weight[:, :C]).astype(BF16)
    all_keys = dot(normed, qkv_weight[:, C : 2 * C])
    all_values = dot(normed, qkv_weight[:, 2 * C :])
    pad = jnp.zeros((GROUP - 72, C), F32)
    ones = jnp.ones((KEYS, KEYS - C), BF16)

    def padded(part):
        return jnp.concatenate([part[:72], pad, part[72:], pad], axis=0).astype(BF16)

    results = []
    for p in range(WINDOWS):
        rows = slice(p * TOKENS, (p + 1) * TOKENS)
        values = jnp.concatenate([padded(all_values[rows]), ones], axis=1)
        results.append((moved(orders[0], all_queries[rows]), padded(all_keys[rows]), values))
    return results


def write_attended(cells, first_level, blended, orders, proj):
    natural = jnp.concatenate([moved(orders[1], part) for part in blended], axis=0)
    attended = dot(natural, proj)
    for p in range(WINDOWS):
        write_window(cells, 2 * p + first_level, attended[p * TOKENS : (p + 1) * TOKENS])


def score(queries, keys):
    stacked = jnp.concatenate(
        [jnp.where(head_lanes(h), queries, jnp.zeros((), BF16)) for h in range(HEADS)], axis=0
    )
    return dot_transposed(stacked, keys) * HEAD_SIZE ** (-0.5)


def blend(scores, values, bias_of):
    weights = []
    for h in range(HEADS):
        part = scores[h * TOKENS : (h + 1) * TOKENS] + bias_of(h)
        weights.append(jnp.exp(part).astype(BF16))
    blended = dot(jnp.concatenate(weights, axis=0), values)
    total = jnp.zeros((TOKENS, C), F32)
    result = jnp.zeros((TOKENS, C), F32)
    for h in range(HEADS):
        part = blended[h * TOKENS : (h + 1) * TOKENS]
        result = jnp.where(head_lanes(h), part[:, :C], result)
        total = jnp.where(head_lanes(h), part[:, C : C + 1], total)
    return (result / jnp.maximum(total, np.exp(-SHIFT))).astype(BF16)


def selected_bias(z_even, z_odd, window, head):
    rows = []
    for at in range(6):
        lanes = slice(at * GROUP, (at + 1) * GROUP)
        halves = []
        for key_level in range(2):
            first = head * 128 + (key_level * 4 + window) * 16
            top = z_even[first : first + 16, lanes]
            low = z_odd[first : first + 16, lanes]
            halves.append(jnp.concatenate([top[:8], top[8:] + low[:8], low[8:]], axis=0))
        rows.append(jnp.concatenate(halves, axis=1))
    return jnp.concatenate(rows, axis=0)


def window_lanes(tile, first):
    turn = (GROUP - first) % GROUP
    near = pltpu.roll(tile[:, :GROUP], turn, 1) if turn else tile[:, :GROUP]
    if first + 72 <= GROUP:
        return near
    lane = lax.broadcasted_iota(jnp.int32, (1, GROUP), 1)
    return jnp.where(lane < GROUP - first, near, pltpu.roll(tile[:, GROUP:], turn, 1))


def expanded_bias(t_top, t_low, window, head):
    halves = []
    for key_level in range(2):
        first = head * 128 + (key_level * 4 + window) * 16
        top_tile, low_tile = t_top[first : first + 16], t_low[first : first + 16]
        rows = []
        for column in range(0, 12, 2):
            top = window_lanes(top_tile, (11 - column) * ROWS).astype(F32)
            low = window_lanes(low_tile, (10 - column) * ROWS).astype(F32)
            rows += [top[:8], top[8:] + low[:8], low[8:]]
        halves.append(jnp.concatenate(rows, axis=0))
    return jnp.concatenate(halves, axis=1)


def picked_rows(table_ref, table_choice):
    tops, lows = [], []
    for h in range(HEADS):
        picked = moved(table_choice, table_ref[h * 192 : (h + 1) * 192, :HALF])
        tops.append(picked[:128])
        lows.append(picked[128:])
    return jnp.concatenate(tops, axis=0), jnp.concatenate(lows, axis=0)


def erf_gelu(values):
    return 0.5 * values * (1.0 + lax.erf(values * np.float32(np.sqrt(0.5))))


def feed_forward(middle, gain, fc1, fc2, keep):
    hidden = erf_gelu(dot(layer_norm(middle, gain).astype(BF16), fc1)).astype(BF16)
    return jnp.where(keep, middle + dot_transposed(hidden, fc2), 0.0).astype(BF16)


def finished(quarters, middle, gain, fc1, fc2, keep):
    flags = jnp.concatenate([keep[ROW_HALF[quarter]][:, :1] for quarter in quarters], axis=0) > 0
    return feed_forward(jnp.concatenate(middle, axis=0), gain, fc1[...], fc2[...], flags)


def pack_piece(piece):
    side = jnp.concatenate(
        [piece[:80, 128:], jnp.concatenate([piece[80:, 128:], piece[:16, 128:]], axis=0)], axis=1
    )
    return jnp.concatenate([piece[:, :128], side], axis=0)


def unpack_piece(packed):
    side = packed[TOKENS:]
    ends = jnp.concatenate([side[:, :64], side[: TOKENS - 80, 64:]], axis=0)
    return jnp.concatenate([packed[:TOKENS], ends], axis=1)


def prepare_masks(lat_valid, first_mask, second_mask, keep):
    lat = lax.axis_index("lat")

    def flag(row):
        return lat_valid[row] > 0

    lane = lax.broadcasted_iota(jnp.int32, (8, KEYS), 1)
    inner = lax.rem(lane, GROUP)
    key_row = jnp.where(inner < 72, lax.rem(inner, ROWS), -1)
    mask = jnp.full((8, KEYS), MASKED, F32)
    usable = jnp.full((8, KEYS), MASKED, F32)
    for r in range(ROWS):
        mask = jnp.where((key_row == r) & flag(lat * ROWS + r), -SHIFT, mask)
        rolled = lax.rem(lat * ROWS + 3 + r, LATS * ROWS)
        usable = jnp.where((key_row == r) & flag(rolled), 0.0, usable)
    first_mask[...] = mask
    a = lax.rem(lax.broadcasted_iota(jnp.int32, (TOKENS, 1), 0), 12)
    query_half = jnp.where(lax.rem(a, ROWS) >= 3, 1, 0)
    key_half = jnp.where(key_row[:1] >= 3, 1, 0)
    same_rows = (query_half == key_half) | (lat != LATS - 1)
    same_level = jnp.where(a >= ROWS, 1, 0) == jnp.where(lane[:1] >= GROUP, 1, 0)
    whole = jnp.where(same_rows, usable[:1], MASKED)
    second_mask[0] = whole
    second_mask[1] = jnp.where(same_level, whole, MASKED)
    for half in range(2):
        for r in range(3):
            value = jnp.where(flag(lat * ROWS + 3 * half + r), 1.0, 0.0)
            for c in range(6):
                at = (c * 3 + r) * LEVELS
                keep[half, at : at + LEVELS] = jnp.full((LEVELS, GROUP), value, F32)


def fetch(sources, held, sems):
    copies = [pltpu.make_async_copy(a, b, sems.at[n]) for n, (a, b) in enumerate(zip(sources, held))]
    for copy in copies:
        copy.start()
    return copies


def sliced(kernel, layers, *refs):
    kernel(*[ref.at[layers[at]] if at in layers else ref for at, ref in enumerate(refs)])


def fetch_kernel(*refs):
    sources, held, (first_mask, second_mask, keep, flags, sems) = refs[:6], refs[6:11], refs[11:]
    copies = fetch(sources, (flags,) + tuple(held), sems)
    copies[0].wait()
    prepare_masks(flags, first_mask, second_mask, keep)
    for copy in copies[1:]:
        copy.wait()


def choose(row_keys, lane_keys):
    return jnp.where(row_keys == lane_keys, 1.0, 0.0).astype(BF16)


def prepare_kernel(mine, proj, fc1, fc2, *refs):
    copies = fetch((proj, fc1, fc2), refs[:3], refs[-1])
    lanes, rows, columns = refs[3:6]

    def place(shape, axis):
        return lax.broadcasted_iota(jnp.int32, shape, axis)

    at = place((HALF, 1), 0)
    row, position = at // SPAN, lax.rem(at, SPAN)
    lanes[...] = choose(position * ROWS + row, place((HALF, KEYS), 1))
    at = place((256, 1), 0)
    a = lax.rem(at, 16) - 4 * (at // 128)
    source = (a * 2 + lax.rem(at // 64, 2)) * 8 + lax.rem(at // 16, 4)
    for block in range(2):
        rows[block] = choose(jnp.where((a >= 0) & (a < 12), source + 4 * block, -1), place((256, 192), 1))
    lane = place((1, 6 * GROUP), 1)
    inner = lax.rem(lane, GROUP)
    for parity in range(2):
        met = inner // ROWS - (lane // GROUP * 2 + parity) + 11
        wanted = jnp.where(inner < 72, met * ROWS + lax.rem(inner, ROWS), -1)
        columns[parity] = choose(position * ROWS + row, wanted)
    for copy in copies:
        copy.wait()


def join_kernel(*refs):
    at = 0
    for ref in refs[:-1]:
        if ref.shape[1:] == refs[-1].shape[1:]:
            refs[-1][at : at + ref.shape[0]] = ref[...]
            at += ref.shape[0]


def before_kernel(halves, x, gains, qkv_weight, query_choice, *refs):
    sources, (scores_out, v_out, cells), held, sems = refs[:2], refs[2:5], refs[5:7], refs[7]
    copies = fetch(sources, held, sems)
    wide = jnp.concatenate([x[...].astype(F32), jnp.zeros((CELLS, 2 * GROUP - C), F32)], axis=1)
    for r in range(ROWS):
        for c in range(COLS):
            group = wide[(r * COLS + c) * LEVELS : (r * COLS + c + 1) * LEVELS]
            at = (c * ROWS + r) * LEVELS
            cells[0, at : at + LEVELS] = group[:, :GROUP]
            cells[1, at : at + LEVELS] = group[:, GROUP:]
    windows = jnp.concatenate([read_window(cells, 2 * p) for p in range(WINDOWS)], axis=0)
    normed = layer_norm(windows, gains[0, 0:1]).astype(BF16)
    for p, (q, k, v) in enumerate(project(normed, qkv_weight[...], query_choice)):
        v_out[p] = v
        scores_out[p] = score(q, k)
    for copy in copies:
        copy.wait()


def first_quarters(quarters, inputs, cells, gains, fc1, fc2, keep):
    middle = []
    for quarter in quarters:
        qr, qc = ROW_HALF[quarter], own_half(quarter)
        middle.append(read_quarter(inputs, qr, qc) + read_quarter(cells, qr, qc).astype(BF16).astype(F32))
    return finished(quarters, middle, gains[0, 1:2], fc1, fc2, keep)


def first_kernel(mine, theirs, scores, v, first_mask, keep, inputs, gains, query_choice, proj, fc1, fc2, lanes, rows, sent_lat, sent_lon, sent_both, table_out, out, cells, table_f32, t_top, t_low):
    me = lax.axis_index("lon")
    for g in range(LONS):
        slot = lax.rem(me // 2 - g // 2 + 8, 4) * 2 + jnp.where(me // 8 == g // 8, 0, 1)
        shard = jnp.where(lax.rem(me, 2) == g % 2, mine[slot], theirs[slot]).astype(F32)
        piece = jnp.concatenate([shard[0], shard[1]], axis=0)
        for n in range(9):
            at = (g * 9 + n) * 8
            table_f32[at : at + 8, :HALF] = piece[:, n * HALF : (n + 1) * HALF]
    table_out[:, :HALF] = table_f32[:, :HALF].astype(BF16)
    tops, lows = picked_rows(table_out, rows[0])
    t_top[...] = dot(tops, lanes[...]).astype(BF16)
    t_low[...] = dot(lows, lanes[...]).astype(BF16)
    mask = first_mask[0:1]
    blended = [blend(scores[p], v[p], lambda h: expanded_bias(t_top, t_low, p, h) + mask) for p in range(WINDOWS)]
    write_attended(cells, 0, blended, query_choice, proj[...])
    results = first_quarters((1, 2, 3), inputs, cells, gains, fc1, fc2, keep)
    out[...] = results
    for at, target in enumerate((sent_lat, sent_lon, sent_both)):
        target[...] = pack_piece(results[at * TOKENS : (at + 1) * TOKENS])


def bias_kernel(table, second_mask, columns, rows, inputs, cells, gains, fc1, fc2, keep, bias_out, near, z_even, z_odd):
    near[...] = first_quarters((0,), inputs, cells, gains, fc1, fc2, keep)
    tops, lows = picked_rows(table, rows[1])
    z_even[...] = dot(tops, columns[0])
    z_odd[...] = dot(lows, columns[1])
    for p in range(WINDOWS):
        for h in range(HEADS):
            whole = selected_bias(z_even, z_odd, p, h) + second_mask[1 if p == WINDOWS - 1 else 0]
            bias_out[p, h * TOKENS : (h + 1) * TOKENS] = whole.astype(BF16)


def write_normed(cells, quarter, piece, gains):
    normed = layer_norm(piece.astype(F32), gains[1, 0:1]).astype(BF16)
    write_quarter(cells, 1 - ROW_HALF[quarter], window_half(quarter), normed.astype(F32))


def ready_kernel(near, from_lon, from_both, gains, cells):
    write_normed(cells, 0, near[...], gains)
    write_normed(cells, 2, unpack_piece(from_lon[...]), gains)
    write_normed(cells, 3, unpack_piece(from_both[...]), gains)


def second_kernel(given, from_lat, bias, gains, qkv_weight, proj, query_choice, own, sent_lat, sent_lon, sent_both, cells, results):
    cells[...] = given[...]
    write_normed(cells, 1, unpack_piece(from_lat[...]), gains)
    normed = jnp.concatenate([read_window(cells, 2 * p + 1) for p in range(WINDOWS)], axis=0).astype(BF16)
    blended = []
    for p, (q, k, v) in enumerate(project(normed, qkv_weight[...], query_choice)):

        def bias_of(h):
            return bias[p, h * TOKENS : (h + 1) * TOKENS].astype(F32) - SHIFT

        blended.append(blend(score(q, k), v, bias_of))
    write_attended(results, 1, blended, query_choice, proj[...])
    pieces = [read_quarter(results, 1 - ROW_HALF[k], window_half(k)).astype(BF16) for k in range(4)]
    own[...] = pieces[0]
    sent_lat[...] = pack_piece(pieces[1])
    sent_lon[...] = pack_piece(pieces[2])
    sent_both[...] = pack_piece(pieces[3])


def own_kernel(fc1, fc2, merge, keep, near, own, gains, result, *refs):
    copies = fetch((fc1, fc2, merge), refs[:3], refs[3])
    middle = near[...].astype(F32) + own[...].astype(F32)
    for copy in copies:
        copy.wait()
    result[...] = feed_forward(middle, gains[1, 1:2], refs[0][...], refs[1][...], keep[1][:, :1] > 0)


def add_kernel(far, from_both, from_lon, middle):
    for at, piece in enumerate((from_lon, from_both)):
        inputs = far[(at + 1) * TOKENS : (at + 2) * TOKENS].astype(F32)
        middle[at] = inputs + unpack_piece(piece[...]).astype(F32)


def last_kernel(keep, far, done, middle, from_lat, gains, fc1, fc2, merge_gain, merge_weight, merged):
    upper = far[:TOKENS].astype(F32) + unpack_piece(from_lat[...]).astype(F32)
    fresh = finished((1, 2, 3), [upper, middle[0], middle[1]], gains[1, 1:2], fc1, fc2, keep).astype(F32)
    results = [done[...].astype(F32)] + [fresh[at * TOKENS : (at + 1) * TOKENS] for at in range(3)]
    odd = lax.rem(lax.axis_index("lat"), 2) == 1
    groups = {}
    for qr, (first, second) in enumerate(((1, 3), (0, 2))):
        turned_round = odd if qr == 1 else jnp.logical_not(odd)
        right = jnp.where(turned_round, results[second], results[first])
        left = jnp.where(turned_round, results[first], results[second])
        for qc, result in enumerate((left, right)):
            for r in range(3):
                for c in range(6):
                    at = (c * 3 + r) * LEVELS
                    groups[3 * qr + r, 6 * qc + c] = result[at : at + LEVELS]
    parts = [
        jnp.concatenate([groups[2 * r + dr, 2 * c + dc] for r in range(3) for c in range(6)], axis=0)
        for dr in range(2)
        for dc in range(2)
    ]
    average = sum(jnp.sum(part, axis=-1, keepdims=True) for part in parts) / (4 * C)
    parts = [part - average for part in parts]
    spread = sum(jnp.sum(part * part, axis=-1, keepdims=True) for part in parts) / (4 * C)
    scale = lax.rsqrt(spread + 1e-05)
    total = jnp.zeros((TOKENS, 2 * C), F32)
    for d, part in enumerate(parts):
        normed = (part * scale * merge_gain[d : d + 1]).astype(BF16)
        total = total + dot(normed, merge_weight[d * C : (d + 1) * C])
    merged[...] = total.astype(BF16)


VMEM_SPEC = pl.BlockSpec(memory_space=pltpu.VMEM)
SMEM_SPEC = pl.BlockSpec(memory_space=pltpu.SMEM)


def call(kernel, name, micros, outs, scratch, *operands, in_specs=None, aliases=None):
    return pl.pallas_call(
        kernel,
        name=name,
        out_shape=outs,
        in_specs=in_specs or [VMEM_SPEC] * len(operands),
        out_specs=jax.tree.map(lambda _: VMEM_SPEC, outs),
        scratch_shapes=scratch,
        input_output_aliases=aliases or {},
        cost_estimate=pl.CostEstimate(flops=int(micros * 1e9), bytes_accessed=2**20, transcendentals=0),
        compiler_params=pltpu.CompilerParams(vmem_limit_bytes=16 * 2**20),
    )(*operands)


def shape(*dims, dtype=BF16):
    return jax.ShapeDtypeStruct(dims, dtype)


def sent(block, rows, across, back=False):
    route = []
    for i in range(LATS):
        for j in range(LONS):
            to = (i + rows) % LATS
            owner = i if back else to
            step = (1 if owner % 2 == 1 else -1) * (-1 if back else 1)
            route.append((i * LONS + j, to * LONS + (j + across * step) % LONS))
    return lax.ppermute(block, ("lat", "lon"), route)


def turned(block, place):
    route = []
    for j in range(LONS):
        z, x, core = place(j // 8, j // 2 % 4, j % 2)
        route.append((j, z * 8 + x * 2 + core))
    return lax.ppermute(block, "lon", route)


def shards(state, lat_valid, norm_gains, qkv_weight, proj_weight, fc1_weight, fc2_weight, earth_bias, merge_gain, merge_weight):
    shard = earth_bias[:, 0]
    cells = pltpu.VMEM((2, CELLS, GROUP), F32)
    cell_rows = shape(2, CELLS, GROUP, dtype=F32)
    t_scratch = [pltpu.VMEM((768, KEYS), BF16), pltpu.VMEM((768, KEYS), BF16)]
    packed = shape(224, 128)

    def in_hbm(array):
        return pltpu.with_memory_space_constraint(array, pltpu.HBM)

    def like(arrays):
        return [shape(*array.shape, dtype=array.dtype) for array in arrays]

    hbm_spec = pl.BlockSpec(memory_space=pltpu.HBM)
    fc2_turned = jnp.swapaxes(fc2_weight, 1, 2)
    early = [
        shard[None],
        state.transpose(1, 2, 0, 3).reshape(CELLS, C),
        norm_gains,
        qkv_weight,
        jnp.stack([one_hot(query_order(), TOKENS), one_hot(natural_order(), TOKENS)]),
    ]
    late = [qkv_weight, proj_weight]
    layer = [shape(C, C), shape(C, HIDDEN), shape(C, HIDDEN)]
    other_half = turned(shard, lambda z, x, core: (1 - z, x, core))
    held_shard, x, gains, qkv0, query_choice, first_mask, second_mask, keep = call(
        functools.partial(sliced, fetch_kernel, {4: 0}),
        "fetch",
        1.4,
        like(early[:3])
        + [shape(C, 3 * C)]
        + like(early[4:])
        + [
            shape(8, KEYS, dtype=F32),
            shape(2, TOKENS, KEYS, dtype=F32),
            shape(2, TOKENS, GROUP, dtype=F32),
        ],
        [pltpu.SMEM((LATS * ROWS,), jnp.int32), pltpu.SemaphoreType.DMA((len(early) + 1,))],
        in_hbm(lat_valid),
        *[in_hbm(array) for array in early],
        in_specs=[hbm_spec] * (len(early) + 1),
    )
    halves = call(join_kernel, "halves", 0.2, shape(2, 2, WINDOWS, SHARD), [], held_shard, other_half[None])
    ring = [turned(halves, lambda z, x, core: (z, (x + hop) % 4, core)) for hop in range(1, 4)]
    scores, v, inputs, qkv1, proj1 = call(
        functools.partial(sliced, before_kernel, {5: 1, 6: 1}),
        "before",
        2.5,
        [shape(WINDOWS, HEADS * TOKENS, KEYS, dtype=F32), shape(WINDOWS, KEYS, KEYS), cell_rows]
        + [shape(C, 3 * C), shape(C, C)],
        [pltpu.SemaphoreType.DMA((len(late),))],
        halves, x, gains, qkv0, query_choice,
        *[in_hbm(array) for array in late],
        in_specs=[VMEM_SPEC] * 5 + [hbm_spec] * len(late),
    )
    mine = call(join_kernel, "mine", 0.3, shape(8, 2, WINDOWS, SHARD), [], halves, *ring, v)
    theirs = turned(mine, lambda z, x, core: (z, x, 1 - core))
    proj0, fc1_0, fc2_0, lanes, rows, columns = call(
        functools.partial(sliced, prepare_kernel, {1: 0, 2: 0, 3: 0}),
        "prepare",
        1.2,
        layer + [shape(HALF, KEYS), shape(2, 256, 192), shape(2, HALF, 6 * GROUP)],
        [pltpu.SemaphoreType.DMA((3,))],
        mine, in_hbm(proj_weight), in_hbm(fc1_weight), in_hbm(fc2_turned),
        in_specs=[VMEM_SPEC] + [hbm_spec] * 3,
    )
    to_lat, to_lon, to_both, tables, far, attended = call(
        first_kernel,
        "first",
        4.5,
        [packed, packed, packed, shape(1152, KEYS), shape(3 * TOKENS, C), cell_rows],
        [pltpu.VMEM((1152, KEYS), F32)] + t_scratch,
        mine, theirs, scores, v, first_mask, keep, inputs, gains, query_choice, proj0, fc1_0, fc2_0, lanes, rows,
    )
    from_lat, from_lon, from_both = sent(to_lat, -1, 0), sent(to_lon, 0, 1), sent(to_both, -1, 1)
    bias, near = call(
        bias_kernel,
        "bias",
        0.2,
        [shape(WINDOWS, HEADS * TOKENS, KEYS), shape(TOKENS, C)],
        [pltpu.VMEM((768, 768), F32), pltpu.VMEM((768, 768), F32)],
        tables, second_mask, columns, rows, inputs, attended, gains, fc1_0, fc2_0, keep,
    )
    ready = call(ready_kernel, "ready", 0.4, cell_rows, [], near, from_lon, from_both, gains)
    own, to_lat, to_lon, to_both = call(
        second_kernel,
        "second",
        4.5,
        [shape(TOKENS, C), packed, packed, packed],
        [cells, cells],
        ready, from_lat, bias, gains, qkv1, proj1, query_choice,
    )
    from_lon, from_both, from_lat = sent(to_lon, 0, 1, True), sent(to_both, 1, 1, True), sent(to_lat, 1, 0, True)
    done, fc1_1, fc2_1, merge = call(
        functools.partial(sliced, own_kernel, {0: 1, 1: 1}),
        "own",
        0.5,
        [shape(TOKENS, C)] + layer[1:] + like([merge_weight]),
        [pltpu.SemaphoreType.DMA((3,))],
        in_hbm(fc1_weight), in_hbm(fc2_turned), in_hbm(merge_weight), keep, near, own, gains,
        in_specs=[hbm_spec] * 3 + [VMEM_SPEC] * 4,
    )
    middle = call(
        add_kernel, "add", 0.2, shape(2, TOKENS, C, dtype=F32), [], far, from_both, from_lon
    )
    merged = call(
        last_kernel,
        "last",
        2.0,
        shape(TOKENS, 2 * C),
        [],
        keep, far, done, middle, from_lat, gains, fc1_1, fc2_1, merge_gain.reshape(4, C), merge,
    )
    return merged.reshape(3, 6, LEVELS, 2 * C).transpose(2, 0, 1, 3)


def solution(mesh):
    return jax.shard_map(
        shards,
        mesh=mesh,
        in_specs=(
            P(None, "lat", "lon", None),
            P(),
            P(),
            P(),
            P(),
            P(),
            P(),
            P(None, "lat", None, "lon"),
            P(),
            P(),
        ),
        out_specs=P(None, "lat", "lon", None),
        check_vma=False,
    )
```

```python
import functools

import jax
import jax.numpy as jnp
import numpy as np
from jax import lax
from jax.experimental import pallas as pl
from jax.experimental.pallas import tpu as pltpu
from jax.sharding import PartitionSpec as P

BF16 = jnp.bfloat16
F32 = jnp.float32
C = 192
HEADS = 6
HEAD_SIZE = 32
HIDDEN = 768
LEVELS, ROWS, COLS = 8, 6, 12
WINDOWS = 4
TOKENS = 144
CELLS = 576
RUN = 24
SPAN = 23
HALF = 6 * SPAN
GROUP = 128
KEYS = 2 * GROUP
LATS, LONS = 8, 16
SHARD = 1242
SHIFT = 12.0
MASKED = -1e30


def one_hot(sources, width):
    sources = np.asarray(sources)
    matrix = np.zeros((len(sources), width), np.float32)
    rows = np.nonzero(sources >= 0)[0]
    matrix[rows, sources[rows]] = 1.0
    return jnp.asarray(matrix, BF16)


ROW_HALF = (1, 0, 1, 0)


def own_half(quarter):
    odd = lax.rem(lax.axis_index("lat"), 2)
    return (1 - odd, odd, odd, 1 - odd)[quarter]


def window_half(quarter):
    odd = lax.rem(lax.axis_index("lat"), 2)
    return (odd, odd, 1 - odd, 1 - odd)[quarter]


def query_order():
    return [level * 72 + c * 6 + r for c in range(COLS) for level in range(2) for r in range(ROWS)]


def natural_order():
    return [c * 12 + level * 6 + r for level in range(2) for c in range(COLS) for r in range(ROWS)]


def quarter_runs(qr, qc):
    starts = [qc * (6 * ROWS * LEVELS) + (c * ROWS + 3 * qr) * LEVELS for c in range(6)]
    return [pl.ds(pl.multiple_of(start, LEVELS), RUN) for start in starts]


def level_cells(level):
    return pl.ds(level, ROWS * COLS, stride=LEVELS)


def read_window(cells, first_level):
    parts = [
        jnp.concatenate([cells[0, level_cells(level % LEVELS)], cells[1, level_cells(level % LEVELS)]], axis=1)
        for level in (first_level, first_level + 1)
    ]
    return jnp.concatenate(parts, axis=0)[:, :C]


def write_window(cells, first_level, values):
    wide = jnp.concatenate([values, jnp.zeros((TOKENS, 2 * GROUP - C), F32)], axis=1)
    for offset in range(2):
        rows = wide[offset * 72 : (offset + 1) * 72]
        where = level_cells((first_level + offset) % LEVELS)
        cells[0, where] = rows[:, :GROUP]
        cells[1, where] = rows[:, GROUP:]


def read_quarter(cells, qr, qc):
    parts = [jnp.concatenate([cells[0, run, :], cells[1, run, :]], axis=1) for run in quarter_runs(qr, qc)]
    return jnp.concatenate(parts, axis=0)[:, :C]


def write_quarter(cells, qr, qc, values):
    wide = jnp.concatenate([values, jnp.zeros((TOKENS, 2 * GROUP - C), F32)], axis=1)
    for c, run in enumerate(quarter_runs(qr, qc)):
        cells[0, run, :] = wide[c * RUN : (c + 1) * RUN, :GROUP]
        cells[1, run, :] = wide[c * RUN : (c + 1) * RUN, GROUP:]


def layer_norm(values, scales):
    average = jnp.mean(values, axis=-1, keepdims=True)
    centred = values - average
    spread = jnp.mean(centred * centred, axis=-1, keepdims=True)
    return centred * lax.rsqrt(spread + 1e-05) * scales


def dot(a, b):
    return jnp.dot(a, b, preferred_element_type=F32)


def dot_transposed(a, b):
    return lax.dot_general(a, b, (((1,), (1,)), ((), ())), preferred_element_type=F32)


def moved(choice, rows):
    return dot(choice, rows).astype(BF16)


def head_lanes(head):
    lane = lax.broadcasted_iota(jnp.int32, (1, C), 1)
    return (lane >= head * HEAD_SIZE) & (lane < (head + 1) * HEAD_SIZE)


def project(normed, qkv_weight, orders):
    all_queries = dot(normed, qkv_weight[:, :C]).astype(BF16)
    all_keys = dot(normed, qkv_weight[:, C : 2 * C])
    all_values = dot(normed, qkv_weight[:, 2 * C :])
    pad = jnp.zeros((GROUP - 72, C), F32)
    ones = jnp.ones((KEYS, KEYS - C), BF16)

    def padded(part):
        return jnp.concatenate([part[:72], pad, part[72:], pad], axis=0).astype(BF16)

    results = []
    for p in range(WINDOWS):
        rows = slice(p * TOKENS, (p + 1) * TOKENS)
        values = jnp.concatenate([padded(all_values[rows]), ones], axis=1)
        results.append((moved(orders[0], all_queries[rows]), padded(all_keys[rows]), values))
    return results


def write_attended(cells, first_level, blended, orders, proj):
    natural = jnp.concatenate([moved(orders[1], part) for part in blended], axis=0)
    attended = dot(natural, proj)
    for p in range(WINDOWS):
        write_window(cells, 2 * p + first_level, attended[p * TOKENS : (p + 1) * TOKENS])


def score(queries, keys):
    stacked = jnp.concatenate(
        [jnp.where(head_lanes(h), queries, jnp.zeros((), BF16)) for h in range(HEADS)], axis=0
    )
    return dot_transposed(stacked, keys) * HEAD_SIZE ** (-0.5)


def blend(scores, values, bias_of):
    weights = []
    for h in range(HEADS):
        part = scores[h * TOKENS : (h + 1) * TOKENS] + bias_of(h)
        weights.append(jnp.exp(part).astype(BF16))
    blended = dot(jnp.concatenate(weights, axis=0), values)
    total = jnp.zeros((TOKENS, C), F32)
    result = jnp.zeros((TOKENS, C), F32)
    for h in range(HEADS):
        part = blended[h * TOKENS : (h + 1) * TOKENS]
        result = jnp.where(head_lanes(h), part[:, :C], result)
        total = jnp.where(head_lanes(h), part[:, C : C + 1], total)
    return (result / jnp.maximum(total, np.exp(-SHIFT))).astype(BF16)


def selected_bias(z_even, z_odd, window, head):
    rows = []
    for at in range(6):
        lanes = slice(at * GROUP, (at + 1) * GROUP)
        halves = []
        for key_level in range(2):
            first = head * 128 + (key_level * 4 + window) * 16
            top = z_even[first : first + 16, lanes]
            low = z_odd[first : first + 16, lanes]
            halves.append(jnp.concatenate([top[:8], top[8:] + low[:8], low[8:]], axis=0))
        rows.append(jnp.concatenate(halves, axis=1))
    return jnp.concatenate(rows, axis=0)


def window_lanes(tile, first):
    turn = (GROUP - first) % GROUP
    near = pltpu.roll(tile[:, :GROUP], turn, 1) if turn else tile[:, :GROUP]
    if first + 72 <= GROUP:
        return near
    lane = lax.broadcasted_iota(jnp.int32, (1, GROUP), 1)
    return jnp.where(lane < GROUP - first, near, pltpu.roll(tile[:, GROUP:], turn, 1))


def expanded_bias(t_top, t_low, window, head):
    halves = []
    for key_level in range(2):
        first = head * 128 + (key_level * 4 + window) * 16
        top_tile, low_tile = t_top[first : first + 16], t_low[first : first + 16]
        rows = []
        for column in range(0, 12, 2):
            top = window_lanes(top_tile, (11 - column) * ROWS).astype(F32)
            low = window_lanes(low_tile, (10 - column) * ROWS).astype(F32)
            rows += [top[:8], top[8:] + low[:8], low[8:]]
        halves.append(jnp.concatenate(rows, axis=0))
    return jnp.concatenate(halves, axis=1)


def picked_rows(table_ref, table_choice):
    tops, lows = [], []
    for h in range(HEADS):
        picked = moved(table_choice, table_ref[h * 192 : (h + 1) * 192, :HALF])
        tops.append(picked[:128])
        lows.append(picked[128:])
    return jnp.concatenate(tops, axis=0), jnp.concatenate(lows, axis=0)


def erf_gelu(values):
    return 0.5 * values * (1.0 + lax.erf(values * np.float32(np.sqrt(0.5))))


def feed_forward(middle, gain, fc1, fc2, keep):
    hidden = erf_gelu(dot(layer_norm(middle, gain).astype(BF16), fc1)).astype(BF16)
    return jnp.where(keep, middle + dot_transposed(hidden, fc2), 0.0).astype(BF16)


def finished(quarters, middle, gain, fc1, fc2, keep):
    flags = jnp.concatenate([keep[ROW_HALF[quarter]][:, :1] for quarter in quarters], axis=0) > 0
    return feed_forward(jnp.concatenate(middle, axis=0), gain, fc1[...], fc2[...], flags)


def pack_piece(piece):
    side = jnp.concatenate(
        [piece[:80, 128:], jnp.concatenate([piece[80:, 128:], piece[:16, 128:]], axis=0)], axis=1
    )
    return jnp.concatenate([piece[:, :128], side], axis=0)


def unpack_piece(packed):
    side = packed[TOKENS:]
    ends = jnp.concatenate([side[:, :64], side[: TOKENS - 80, 64:]], axis=0)
    return jnp.concatenate([packed[:TOKENS], ends], axis=1)


def prepare_masks(lat_valid, first_mask, second_mask, keep):
    lat = lax.axis_index("lat")

    def flag(row):
        return lat_valid[row] > 0

    lane = lax.broadcasted_iota(jnp.int32, (8, KEYS), 1)
    inner = lax.rem(lane, GROUP)
    key_row = jnp.where(inner < 72, lax.rem(inner, ROWS), -1)
    mask = jnp.full((8, KEYS), MASKED, F32)
    usable = jnp.full((8, KEYS), MASKED, F32)
    for r in range(ROWS):
        mask = jnp.where((key_row == r) & flag(lat * ROWS + r), -SHIFT, mask)
        rolled = lax.rem(lat * ROWS + 3 + r, LATS * ROWS)
        usable = jnp.where((key_row == r) & flag(rolled), 0.0, usable)
    first_mask[...] = mask
    a = lax.rem(lax.broadcasted_iota(jnp.int32, (TOKENS, 1), 0), 12)
    query_half = jnp.where(lax.rem(a, ROWS) >= 3, 1, 0)
    key_half = jnp.where(key_row[:1] >= 3, 1, 0)
    same_rows = (query_half == key_half) | (lat != LATS - 1)
    same_level = jnp.where(a >= ROWS, 1, 0) == jnp.where(lane[:1] >= GROUP, 1, 0)
    whole = jnp.where(same_rows, usable[:1], MASKED)
    second_mask[0] = whole
    second_mask[1] = jnp.where(same_level, whole, MASKED)
    for half in range(2):
        for r in range(3):
            value = jnp.where(flag(lat * ROWS + 3 * half + r), 1.0, 0.0)
            for c in range(6):
                at = (c * 3 + r) * LEVELS
                keep[half, at : at + LEVELS] = jnp.full((LEVELS, GROUP), value, F32)


def fetch(sources, held, sems):
    copies = [pltpu.make_async_copy(a, b, sems.at[n]) for n, (a, b) in enumerate(zip(sources, held))]
    for copy in copies:
        copy.start()
    return copies


def sliced(kernel, layers, *refs):
    kernel(*[ref.at[layers[at]] if at in layers else ref for at, ref in enumerate(refs)])


def fetch_kernel(*refs):
    sources, held, (first_mask, second_mask, keep, flags, sems) = refs[:6], refs[6:11], refs[11:]
    copies = fetch(sources, (flags,) + tuple(held), sems)
    copies[0].wait()
    prepare_masks(flags, first_mask, second_mask, keep)
    for copy in copies[1:]:
        copy.wait()


def choose(row_keys, lane_keys):
    return jnp.where(row_keys == lane_keys, 1.0, 0.0).astype(BF16)


def prepare_kernel(mine, proj, fc1, fc2, *refs):
    copies = fetch((proj, fc1, fc2), refs[:3], refs[-1])
    lanes, rows, columns = refs[3:6]

    def place(shape, axis):
        return lax.broadcasted_iota(jnp.int32, shape, axis)

    at = place((HALF, 1), 0)
    row, position = at // SPAN, lax.rem(at, SPAN)
    lanes[...] = choose(position * ROWS + row, place((HALF, KEYS), 1))
    at = place((256, 1), 0)
    a = lax.rem(at, 16) - 4 * (at // 128)
    source = (a * 2 + lax.rem(at // 64, 2)) * 8 + lax.rem(at // 16, 4)
    for block in range(2):
        rows[block] = choose(jnp.where((a >= 0) & (a < 12), source + 4 * block, -1), place((256, 192), 1))
    lane = place((1, 6 * GROUP), 1)
    inner = lax.rem(lane, GROUP)
    for parity in range(2):
        met = inner // ROWS - (lane // GROUP * 2 + parity) + 11
        wanted = jnp.where(inner < 72, met * ROWS + lax.rem(inner, ROWS), -1)
        columns[parity] = choose(position * ROWS + row, wanted)
    for copy in copies:
        copy.wait()


def join_kernel(*refs):
    at = 0
    for ref in refs[:-1]:
        if ref.shape[1:] == refs[-1].shape[1:]:
            refs[-1][at : at + ref.shape[0]] = ref[...]
            at += ref.shape[0]


def before_kernel(halves, x, gains, qkv_weight, query_choice, *refs):
    sources, (scores_out, v_out, cells), held, sems = refs[:2], refs[2:5], refs[5:7], refs[7]
    copies = fetch(sources, held, sems)
    wide = jnp.concatenate([x[...].astype(F32), jnp.zeros((CELLS, 2 * GROUP - C), F32)], axis=1)
    for r in range(ROWS):
        for c in range(COLS):
            group = wide[(r * COLS + c) * LEVELS : (r * COLS + c + 1) * LEVELS]
            at = (c * ROWS + r) * LEVELS
            cells[0, at : at + LEVELS] = group[:, :GROUP]
            cells[1, at : at + LEVELS] = group[:, GROUP:]
    windows = jnp.concatenate([read_window(cells, 2 * p) for p in range(WINDOWS)], axis=0)
    normed = layer_norm(windows, gains[0, 0:1]).astype(BF16)
    for p, (q, k, v) in enumerate(project(normed, qkv_weight[...], query_choice)):
        v_out[p] = v
        scores_out[p] = score(q, k)
    for copy in copies:
        copy.wait()


def first_quarters(quarters, inputs, cells, gains, fc1, fc2, keep):
    middle = []
    for quarter in quarters:
        qr, qc = ROW_HALF[quarter], own_half(quarter)
        middle.append(read_quarter(inputs, qr, qc) + read_quarter(cells, qr, qc).astype(BF16).astype(F32))
    return finished(quarters, middle, gains[0, 1:2], fc1, fc2, keep)


def first_kernel(mine, theirs, scores, v, first_mask, keep, inputs, gains, query_choice, proj, fc1, fc2, lanes, rows, sent_lat, sent_lon, sent_both, table_out, out, cells, table_f32, t_top, t_low):
    me = lax.axis_index("lon")
    for g in range(LONS):
        slot = lax.rem(me // 2 - g // 2 + 8, 4) * 2 + jnp.where(me // 8 == g // 8, 0, 1)
        shard = jnp.where(lax.rem(me, 2) == g % 2, mine[slot], theirs[slot]).astype(F32)
        piece = jnp.concatenate([shard[0], shard[1]], axis=0)
        for n in range(9):
            at = (g * 9 + n) * 8
            table_f32[at : at + 8, :HALF] = piece[:, n * HALF : (n + 1) * HALF]
    table_out[:, :HALF] = table_f32[:, :HALF].astype(BF16)
    tops, lows = picked_rows(table_out, rows[0])
    t_top[...] = dot(tops, lanes[...]).astype(BF16)
    t_low[...] = dot(lows, lanes[...]).astype(BF16)
    mask = first_mask[0:1]
    blended = [blend(scores[p], v[p], lambda h: expanded_bias(t_top, t_low, p, h) + mask) for p in range(WINDOWS)]
    write_attended(cells, 0, blended, query_choice, proj[...])
    results = first_quarters((1, 2, 3), inputs, cells, gains, fc1, fc2, keep)
    out[...] = results
    for at, target in enumerate((sent_lat, sent_lon, sent_both)):
        target[...] = pack_piece(results[at * TOKENS : (at + 1) * TOKENS])


def bias_kernel(table, second_mask, columns, rows, inputs, cells, gains, fc1, fc2, keep, bias_out, near, z_even, z_odd):
    near[...] = first_quarters((0,), inputs, cells, gains, fc1, fc2, keep)
    tops, lows = picked_rows(table, rows[1])
    z_even[...] = dot(tops, columns[0])
    z_odd[...] = dot(lows, columns[1])
    for p in range(WINDOWS):
        for h in range(HEADS):
            whole = selected_bias(z_even, z_odd, p, h) + second_mask[1 if p == WINDOWS - 1 else 0]
            bias_out[p, h * TOKENS : (h + 1) * TOKENS] = whole.astype(BF16)


def write_normed(cells, quarter, piece, gains):
    normed = layer_norm(piece.astype(F32), gains[1, 0:1]).astype(BF16)
    write_quarter(cells, 1 - ROW_HALF[quarter], window_half(quarter), normed.astype(F32))


def ready_kernel(near, from_both, from_lon, gains, cells):
    write_normed(cells, 0, near[...], gains)
    write_normed(cells, 2, unpack_piece(from_lon[...]), gains)
    write_normed(cells, 3, unpack_piece(from_both[...]), gains)


def second_kernel(given, from_lat, bias, gains, qkv_weight, proj, query_choice, own, sent_lat, sent_lon, sent_both, cells, results):
    cells[...] = given[...]
    write_normed(cells, 1, unpack_piece(from_lat[...]), gains)
    normed = jnp.concatenate([read_window(cells, 2 * p + 1) for p in range(WINDOWS)], axis=0).astype(BF16)
    blended = []
    for p, (q, k, v) in enumerate(project(normed, qkv_weight[...], query_choice)):

        def bias_of(h):
            return bias[p, h * TOKENS : (h + 1) * TOKENS].astype(F32) - SHIFT

        blended.append(blend(score(q, k), v, bias_of))
    write_attended(results, 1, blended, query_choice, proj[...])
    pieces = [read_quarter(results, 1 - ROW_HALF[k], window_half(k)).astype(BF16) for k in range(4)]
    own[...] = pieces[0]
    sent_lat[...] = pack_piece(pieces[1])
    sent_lon[...] = pack_piece(pieces[2])
    sent_both[...] = pack_piece(pieces[3])


def own_kernel(fc1, fc2, merge, keep, near, own, gains, result, *refs):
    copies = fetch((fc1, fc2, merge), refs[:3], refs[3])
    middle = near[...].astype(F32) + own[...].astype(F32)
    for copy in copies:
        copy.wait()
    result[...] = feed_forward(middle, gains[1, 1:2], refs[0][...], refs[1][...], keep[1][:, :1] > 0)


def add_kernel(far, from_both, from_lon, middle):
    for at, piece in enumerate((from_lon, from_both)):
        inputs = far[(at + 1) * TOKENS : (at + 2) * TOKENS].astype(F32)
        middle[at] = inputs + unpack_piece(piece[...]).astype(F32)


def last_kernel(keep, far, done, middle, from_lat, gains, fc1, fc2, merge_gain, merge_weight, merged):
    upper = far[:TOKENS].astype(F32) + unpack_piece(from_lat[...]).astype(F32)
    fresh = finished((1, 2, 3), [upper, middle[0], middle[1]], gains[1, 1:2], fc1, fc2, keep).astype(F32)
    results = [done[...].astype(F32)] + [fresh[at * TOKENS : (at + 1) * TOKENS] for at in range(3)]
    odd = lax.rem(lax.axis_index("lat"), 2) == 1
    groups = {}
    for qr, (first, second) in enumerate(((1, 3), (0, 2))):
        turned_round = odd if qr == 1 else jnp.logical_not(odd)
        right = jnp.where(turned_round, results[second], results[first])
        left = jnp.where(turned_round, results[first], results[second])
        for qc, result in enumerate((left, right)):
            for r in range(3):
                for c in range(6):
                    at = (c * 3 + r) * LEVELS
                    groups[3 * qr + r, 6 * qc + c] = result[at : at + LEVELS]
    parts = [
        jnp.concatenate([groups[2 * r + dr, 2 * c + dc] for r in range(3) for c in range(6)], axis=0)
        for dr in range(2)
        for dc in range(2)
    ]
    average = sum(jnp.sum(part, axis=-1, keepdims=True) for part in parts) / (4 * C)
    parts = [part - average for part in parts]
    spread = sum(jnp.sum(part * part, axis=-1, keepdims=True) for part in parts) / (4 * C)
    scale = lax.rsqrt(spread + 1e-05)
    total = jnp.zeros((TOKENS, 2 * C), F32)
    for d, part in enumerate(parts):
        normed = (part * scale * merge_gain[d : d + 1]).astype(BF16)
        total = total + dot(normed, merge_weight[d * C : (d + 1) * C])
    merged[...] = total.astype(BF16)


VMEM_SPEC = pl.BlockSpec(memory_space=pltpu.VMEM)
SMEM_SPEC = pl.BlockSpec(memory_space=pltpu.SMEM)


def call(kernel, name, micros, outs, scratch, *operands, in_specs=None, aliases=None):
    return pl.pallas_call(
        kernel,
        name=name,
        out_shape=outs,
        in_specs=in_specs or [VMEM_SPEC] * len(operands),
        out_specs=jax.tree.map(lambda _: VMEM_SPEC, outs),
        scratch_shapes=scratch,
        input_output_aliases=aliases or {},
        cost_estimate=pl.CostEstimate(flops=int(micros * 1e9), bytes_accessed=2**20, transcendentals=0),
        compiler_params=pltpu.CompilerParams(vmem_limit_bytes=16 * 2**20),
    )(*operands)


def shape(*dims, dtype=BF16):
    return jax.ShapeDtypeStruct(dims, dtype)


def sent(block, rows, across, back=False):
    route = []
    for i in range(LATS):
        for j in range(LONS):
            to = (i + rows) % LATS
            owner = i if back else to
            step = (1 if owner % 2 == 1 else -1) * (-1 if back else 1)
            route.append((i * LONS + j, to * LONS + (j + across * step) % LONS))
    return lax.ppermute(block, ("lat", "lon"), route)


def turned(block, place):
    route = []
    for j in range(LONS):
        z, x, core = place(j // 8, j // 2 % 4, j % 2)
        route.append((j, z * 8 + x * 2 + core))
    return lax.ppermute(block, "lon", route)


def shards(state, lat_valid, norm_gains, qkv_weight, proj_weight, fc1_weight, fc2_weight, earth_bias, merge_gain, merge_weight):
    shard = earth_bias[:, 0]
    cells = pltpu.VMEM((2, CELLS, GROUP), F32)
    cell_rows = shape(2, CELLS, GROUP, dtype=F32)
    t_scratch = [pltpu.VMEM((768, KEYS), BF16), pltpu.VMEM((768, KEYS), BF16)]
    packed = shape(224, 128)

    def in_hbm(array):
        return pltpu.with_memory_space_constraint(array, pltpu.HBM)

    def like(arrays):
        return [shape(*array.shape, dtype=array.dtype) for array in arrays]

    hbm_spec = pl.BlockSpec(memory_space=pltpu.HBM)
    fc2_turned = jnp.swapaxes(fc2_weight, 1, 2)
    early = [
        shard[None],
        state.transpose(1, 2, 0, 3).reshape(CELLS, C),
        norm_gains,
        qkv_weight,
        jnp.stack([one_hot(query_order(), TOKENS), one_hot(natural_order(), TOKENS)]),
    ]
    late = [qkv_weight, proj_weight]
    layer = [shape(C, C), shape(C, HIDDEN), shape(C, HIDDEN)]
    other_half = turned(shard, lambda z, x, core: (1 - z, x, core))
    held_shard, x, gains, qkv0, query_choice, first_mask, second_mask, keep = call(
        functools.partial(sliced, fetch_kernel, {4: 0}),
        "fetch",
        1.4,
        like(early[:3])
        + [shape(C, 3 * C)]
        + like(early[4:])
        + [
            shape(8, KEYS, dtype=F32),
            shape(2, TOKENS, KEYS, dtype=F32),
            shape(2, TOKENS, GROUP, dtype=F32),
        ],
        [pltpu.SMEM((LATS * ROWS,), jnp.int32), pltpu.SemaphoreType.DMA((len(early) + 1,))],
        in_hbm(lat_valid),
        *[in_hbm(array) for array in early],
        in_specs=[hbm_spec] * (len(early) + 1),
    )
    halves = call(join_kernel, "halves", 0.2, shape(2, 2, WINDOWS, SHARD), [], held_shard, other_half[None])
    ring = [turned(halves, lambda z, x, core: (z, (x + hop) % 4, core)) for hop in range(1, 4)]
    scores, v, inputs, qkv1, proj1 = call(
        functools.partial(sliced, before_kernel, {5: 1, 6: 1}),
        "before",
        2.5,
        [shape(WINDOWS, HEADS * TOKENS, KEYS, dtype=F32), shape(WINDOWS, KEYS, KEYS), cell_rows]
        + [shape(C, 3 * C), shape(C, C)],
        [pltpu.SemaphoreType.DMA((len(late),))],
        halves, x, gains, qkv0, query_choice,
        *[in_hbm(array) for array in late],
        in_specs=[VMEM_SPEC] * 5 + [hbm_spec] * len(late),
    )
    mine = call(join_kernel, "mine", 0.3, shape(8, 2, WINDOWS, SHARD), [], halves, *ring, v)
    theirs = turned(mine, lambda z, x, core: (z, x, 1 - core))
    proj0, fc1_0, fc2_0, lanes, rows, columns = call(
        functools.partial(sliced, prepare_kernel, {1: 0, 2: 0, 3: 0}),
        "prepare",
        1.2,
        layer + [shape(HALF, KEYS), shape(2, 256, 192), shape(2, HALF, 6 * GROUP)],
        [pltpu.SemaphoreType.DMA((3,))],
        mine, in_hbm(proj_weight), in_hbm(fc1_weight), in_hbm(fc2_turned),
        in_specs=[VMEM_SPEC] + [hbm_spec] * 3,
    )
    to_lat, to_lon, to_both, tables, far, attended = call(
        first_kernel,
        "first",
        4.5,
        [packed, packed, packed, shape(1152, KEYS), shape(3 * TOKENS, C), cell_rows],
        [pltpu.VMEM((1152, KEYS), F32)] + t_scratch,
        mine, theirs, scores, v, first_mask, keep, inputs, gains, query_choice, proj0, fc1_0, fc2_0, lanes, rows,
    )
    from_lat, from_lon, from_both = sent(to_lat, -1, 0), sent(to_lon, 0, 1), sent(to_both, -1, 1)
    bias, near = call(
        bias_kernel,
        "bias",
        0.2,
        [shape(WINDOWS, HEADS * TOKENS, KEYS), shape(TOKENS, C)],
        [pltpu.VMEM((768, 768), F32), pltpu.VMEM((768, 768), F32)],
        tables, second_mask, columns, rows, inputs, attended, gains, fc1_0, fc2_0, keep,
    )
    ready = call(ready_kernel, "ready", 0.4, cell_rows, [], near, from_both, from_lon, gains)
    own, to_lat, to_lon, to_both = call(
        second_kernel,
        "second",
        4.5,
        [shape(TOKENS, C), packed, packed, packed],
        [cells, cells],
        ready, from_lat, bias, gains, qkv1, proj1, query_choice,
    )
    from_lon, from_both, from_lat = sent(to_lon, 0, 1, True), sent(to_both, 1, 1, True), sent(to_lat, 1, 0, True)
    done, fc1_1, fc2_1, merge = call(
        functools.partial(sliced, own_kernel, {0: 1, 1: 1}),
        "own",
        0.5,
        [shape(TOKENS, C)] + layer[1:] + like([merge_weight]),
        [pltpu.SemaphoreType.DMA((3,))],
        in_hbm(fc1_weight), in_hbm(fc2_turned), in_hbm(merge_weight), keep, near, own, gains,
        in_specs=[hbm_spec] * 3 + [VMEM_SPEC] * 4,
    )
    middle = call(
        add_kernel, "add", 0.2, shape(2, TOKENS, C, dtype=F32), [], far, from_both, from_lon
    )
    merged = call(
        last_kernel,
        "last",
        2.0,
        shape(TOKENS, 2 * C),
        [],
        keep, far, done, middle, from_lat, gains, fc1_1, fc2_1, merge_gain.reshape(4, C), merge,
    )
    return merged.reshape(3, 6, LEVELS, 2 * C).transpose(2, 0, 1, 3)


def solution(mesh):
    return jax.shard_map(
        shards,
        mesh=mesh,
        in_specs=(
            P(None, "lat", "lon", None),
            P(),
            P(),
            P(),
            P(),
            P(),
            P(),
            P(None, "lat", None, "lon"),
            P(),
            P(),
        ),
        out_specs=P(None, "lat", "lon", None),
        check_vma=False,
    )
```

```python
import functools

import jax
import jax.numpy as jnp
import numpy as np
from jax import lax
from jax.experimental import pallas as pl
from jax.experimental.pallas import tpu as pltpu
from jax.sharding import PartitionSpec as P

BF16 = jnp.bfloat16
F32 = jnp.float32
C = 192
HEADS = 6
HEAD_SIZE = 32
HIDDEN = 768
LEVELS, ROWS, COLS = 8, 6, 12
WINDOWS = 4
TOKENS = 144
CELLS = 576
RUN = 24
SPAN = 23
HALF = 6 * SPAN
GROUP = 128
KEYS = 2 * GROUP
LATS, LONS = 8, 16
SHARD = 1242
SHIFT = 12.0
MASKED = -1e30


def one_hot(sources, width):
    sources = np.asarray(sources)
    matrix = np.zeros((len(sources), width), np.float32)
    rows = np.nonzero(sources >= 0)[0]
    matrix[rows, sources[rows]] = 1.0
    return jnp.asarray(matrix, BF16)


ROW_HALF = (1, 0, 1, 0)


def own_half(quarter):
    odd = lax.rem(lax.axis_index("lat"), 2)
    return (1 - odd, odd, odd, 1 - odd)[quarter]


def window_half(quarter):
    odd = lax.rem(lax.axis_index("lat"), 2)
    return (odd, odd, 1 - odd, 1 - odd)[quarter]


def query_order():
    return [level * 72 + c * 6 + r for c in range(COLS) for level in range(2) for r in range(ROWS)]


def natural_order():
    return [c * 12 + level * 6 + r for level in range(2) for c in range(COLS) for r in range(ROWS)]


def quarter_runs(qr, qc):
    starts = [qc * (6 * ROWS * LEVELS) + (c * ROWS + 3 * qr) * LEVELS for c in range(6)]
    return [pl.ds(pl.multiple_of(start, LEVELS), RUN) for start in starts]


def level_cells(level):
    return pl.ds(level, ROWS * COLS, stride=LEVELS)


def read_window(cells, first_level):
    parts = [
        jnp.concatenate([cells[0, level_cells(level % LEVELS)], cells[1, level_cells(level % LEVELS)]], axis=1)
        for level in (first_level, first_level + 1)
    ]
    return jnp.concatenate(parts, axis=0)[:, :C]


def write_window(cells, first_level, values):
    wide = jnp.concatenate([values, jnp.zeros((TOKENS, 2 * GROUP - C), F32)], axis=1)
    for offset in range(2):
        rows = wide[offset * 72 : (offset + 1) * 72]
        where = level_cells((first_level + offset) % LEVELS)
        cells[0, where] = rows[:, :GROUP]
        cells[1, where] = rows[:, GROUP:]


def read_quarter(cells, qr, qc):
    parts = [jnp.concatenate([cells[0, run, :], cells[1, run, :]], axis=1) for run in quarter_runs(qr, qc)]
    return jnp.concatenate(parts, axis=0)[:, :C]


def write_quarter(cells, qr, qc, values):
    wide = jnp.concatenate([values, jnp.zeros((TOKENS, 2 * GROUP - C), F32)], axis=1)
    for c, run in enumerate(quarter_runs(qr, qc)):
        cells[0, run, :] = wide[c * RUN : (c + 1) * RUN, :GROUP]
        cells[1, run, :] = wide[c * RUN : (c + 1) * RUN, GROUP:]


def layer_norm(values, scales):
    average = jnp.mean(values, axis=-1, keepdims=True)
    centred = values - average
    spread = jnp.mean(centred * centred, axis=-1, keepdims=True)
    return centred * lax.rsqrt(spread + 1e-05) * scales


def dot(a, b):
    return jnp.dot(a, b, preferred_element_type=F32)


def dot_transposed(a, b):
    return lax.dot_general(a, b, (((1,), (1,)), ((), ())), preferred_element_type=F32)


def moved(choice, rows):
    return dot(choice, rows).astype(BF16)


def head_lanes(head):
    lane = lax.broadcasted_iota(jnp.int32, (1, C), 1)
    return (lane >= head * HEAD_SIZE) & (lane < (head + 1) * HEAD_SIZE)


def project(normed, qkv_weight, orders):
    all_queries = dot(normed, qkv_weight[:, :C]).astype(BF16)
    all_keys = dot(normed, qkv_weight[:, C : 2 * C])
    all_values = dot(normed, qkv_weight[:, 2 * C :])
    pad = jnp.zeros((GROUP - 72, C), F32)
    ones = jnp.ones((KEYS, KEYS - C), BF16)

    def padded(part):
        return jnp.concatenate([part[:72], pad, part[72:], pad], axis=0).astype(BF16)

    results = []
    for p in range(WINDOWS):
        rows = slice(p * TOKENS, (p + 1) * TOKENS)
        values = jnp.concatenate([padded(all_values[rows]), ones], axis=1)
        results.append((moved(orders[0], all_queries[rows]), padded(all_keys[rows]), values))
    return results


def write_attended(cells, first_level, blended, orders, proj):
    natural = jnp.concatenate([moved(orders[1], part) for part in blended], axis=0)
    attended = dot(natural, proj)
    for p in range(WINDOWS):
        write_window(cells, 2 * p + first_level, attended[p * TOKENS : (p + 1) * TOKENS])


def score(queries, keys):
    stacked = jnp.concatenate(
        [jnp.where(head_lanes(h), queries, jnp.zeros((), BF16)) for h in range(HEADS)], axis=0
    )
    return dot_transposed(stacked, keys) * HEAD_SIZE ** (-0.5)


def blend(scores, values, bias_of):
    weights = []
    for h in range(HEADS):
        part = scores[h * TOKENS : (h + 1) * TOKENS] + bias_of(h)
        weights.append(jnp.exp(part).astype(BF16))
    blended = dot(jnp.concatenate(weights, axis=0), values)
    total = jnp.zeros((TOKENS, C), F32)
    result = jnp.zeros((TOKENS, C), F32)
    for h in range(HEADS):
        part = blended[h * TOKENS : (h + 1) * TOKENS]
        result = jnp.where(head_lanes(h), part[:, :C], result)
        total = jnp.where(head_lanes(h), part[:, C : C + 1], total)
    return (result / jnp.maximum(total, np.exp(-SHIFT))).astype(BF16)


def selected_bias(z_even, z_odd, window, head):
    rows = []
    for at in range(6):
        lanes = slice(at * GROUP, (at + 1) * GROUP)
        halves = []
        for key_level in range(2):
            first = head * 128 + (key_level * 4 + window) * 16
            top = z_even[first : first + 16, lanes]
            low = z_odd[first : first + 16, lanes]
            halves.append(jnp.concatenate([top[:8], top[8:] + low[:8], low[8:]], axis=0))
        rows.append(jnp.concatenate(halves, axis=1))
    return jnp.concatenate(rows, axis=0)


def window_lanes(tile, first):
    turn = (GROUP - first) % GROUP
    near = pltpu.roll(tile[:, :GROUP], turn, 1) if turn else tile[:, :GROUP]
    if first + 72 <= GROUP:
        return near
    lane = lax.broadcasted_iota(jnp.int32, (1, GROUP), 1)
    return jnp.where(lane < GROUP - first, near, pltpu.roll(tile[:, GROUP:], turn, 1))


def expanded_bias(t_top, t_low, window, head):
    halves = []
    for key_level in range(2):
        first = head * 128 + (key_level * 4 + window) * 16
        top_tile, low_tile = t_top[first : first + 16], t_low[first : first + 16]
        rows = []
        for column in range(0, 12, 2):
            top = window_lanes(top_tile, (11 - column) * ROWS).astype(F32)
            low = window_lanes(low_tile, (10 - column) * ROWS).astype(F32)
            rows += [top[:8], top[8:] + low[:8], low[8:]]
        halves.append(jnp.concatenate(rows, axis=0))
    return jnp.concatenate(halves, axis=1)


def picked_rows(table_ref, table_choice):
    tops, lows = [], []
    for h in range(HEADS):
        picked = moved(table_choice, table_ref[h * 192 : (h + 1) * 192, :HALF])
        tops.append(picked[:128])
        lows.append(picked[128:])
    return jnp.concatenate(tops, axis=0), jnp.concatenate(lows, axis=0)


def erf_gelu(values):
    return 0.5 * values * (1.0 + lax.erf(values * np.float32(np.sqrt(0.5))))


def feed_forward(middle, gain, fc1, fc2, keep):
    hidden = erf_gelu(dot(layer_norm(middle, gain).astype(BF16), fc1)).astype(BF16)
    return jnp.where(keep, middle + dot_transposed(hidden, fc2), 0.0).astype(BF16)


def finished(quarters, middle, gain, fc1, fc2, keep):
    flags = jnp.concatenate([keep[ROW_HALF[quarter]][:, :1] for quarter in quarters], axis=0) > 0
    return feed_forward(jnp.concatenate(middle, axis=0), gain, fc1[...], fc2[...], flags)


def pack_piece(piece):
    side = jnp.concatenate(
        [piece[:80, 128:], jnp.concatenate([piece[80:, 128:], piece[:16, 128:]], axis=0)], axis=1
    )
    return jnp.concatenate([piece[:, :128], side], axis=0)


def unpack_piece(packed):
    side = packed[TOKENS:]
    ends = jnp.concatenate([side[:, :64], side[: TOKENS - 80, 64:]], axis=0)
    return jnp.concatenate([packed[:TOKENS], ends], axis=1)


def prepare_masks(lat_valid, first_mask, second_mask, keep):
    lat = lax.axis_index("lat")

    def flag(row):
        return lat_valid[row] > 0

    lane = lax.broadcasted_iota(jnp.int32, (8, KEYS), 1)
    inner = lax.rem(lane, GROUP)
    key_row = jnp.where(inner < 72, lax.rem(inner, ROWS), -1)
    mask = jnp.full((8, KEYS), MASKED, F32)
    usable = jnp.full((8, KEYS), MASKED, F32)
    for r in range(ROWS):
        mask = jnp.where((key_row == r) & flag(lat * ROWS + r), -SHIFT, mask)
        rolled = lax.rem(lat * ROWS + 3 + r, LATS * ROWS)
        usable = jnp.where((key_row == r) & flag(rolled), 0.0, usable)
    first_mask[...] = mask
    a = lax.rem(lax.broadcasted_iota(jnp.int32, (TOKENS, 1), 0), 12)
    query_half = jnp.where(lax.rem(a, ROWS) >= 3, 1, 0)
    key_half = jnp.where(key_row[:1] >= 3, 1, 0)
    same_rows = (query_half == key_half) | (lat != LATS - 1)
    same_level = jnp.where(a >= ROWS, 1, 0) == jnp.where(lane[:1] >= GROUP, 1, 0)
    whole = jnp.where(same_rows, usable[:1], MASKED)
    second_mask[0] = whole
    second_mask[1] = jnp.where(same_level, whole, MASKED)
    for half in range(2):
        for r in range(3):
            value = jnp.where(flag(lat * ROWS + 3 * half + r), 1.0, 0.0)
            for c in range(6):
                at = (c * 3 + r) * LEVELS
                keep[half, at : at + LEVELS] = jnp.full((LEVELS, GROUP), value, F32)


def fetch(sources, held, sems):
    copies = [pltpu.make_async_copy(a, b, sems.at[n]) for n, (a, b) in enumerate(zip(sources, held))]
    for copy in copies:
        copy.start()
    return copies


def sliced(kernel, layers, *refs):
    kernel(*[ref.at[layers[at]] if at in layers else ref for at, ref in enumerate(refs)])


def fetch_kernel(*refs):
    sources, held, (first_mask, second_mask, keep, flags, sems) = refs[:6], refs[6:11], refs[11:]
    copies = fetch(sources, (flags,) + tuple(held), sems)
    copies[0].wait()
    prepare_masks(flags, first_mask, second_mask, keep)
    for copy in copies[1:]:
        copy.wait()


def choose(row_keys, lane_keys):
    return jnp.where(row_keys == lane_keys, 1.0, 0.0).astype(BF16)


def prepare_kernel(mine, proj, fc1, fc2, *refs):
    copies = fetch((proj, fc1, fc2), refs[:3], refs[-1])
    lanes, rows, columns = refs[3:6]

    def place(shape, axis):
        return lax.broadcasted_iota(jnp.int32, shape, axis)

    at = place((HALF, 1), 0)
    row, position = at // SPAN, lax.rem(at, SPAN)
    lanes[...] = choose(position * ROWS + row, place((HALF, KEYS), 1))
    at = place((256, 1), 0)
    a = lax.rem(at, 16) - 4 * (at // 128)
    source = (a * 2 + lax.rem(at // 64, 2)) * 8 + lax.rem(at // 16, 4)
    for block in range(2):
        rows[block] = choose(jnp.where((a >= 0) & (a < 12), source + 4 * block, -1), place((256, 192), 1))
    lane = place((1, 6 * GROUP), 1)
    inner = lax.rem(lane, GROUP)
    for parity in range(2):
        met = inner // ROWS - (lane // GROUP * 2 + parity) + 11
        wanted = jnp.where(inner < 72, met * ROWS + lax.rem(inner, ROWS), -1)
        columns[parity] = choose(position * ROWS + row, wanted)
    for copy in copies:
        copy.wait()


def join_kernel(*refs):
    at = 0
    for ref in refs[:-1]:
        if ref.shape[1:] == refs[-1].shape[1:]:
            refs[-1][at : at + ref.shape[0]] = ref[...]
            at += ref.shape[0]


def before_kernel(halves, x, gains, qkv_weight, query_choice, *refs):
    sources, (scores_out, v_out, cells), held, sems = refs[:2], refs[2:5], refs[5:7], refs[7]
    copies = fetch(sources, held, sems)
    wide = jnp.concatenate([x[...].astype(F32), jnp.zeros((CELLS, 2 * GROUP - C), F32)], axis=1)
    for r in range(ROWS):
        for c in range(COLS):
            group = wide[(r * COLS + c) * LEVELS : (r * COLS + c + 1) * LEVELS]
            at = (c * ROWS + r) * LEVELS
            cells[0, at : at + LEVELS] = group[:, :GROUP]
            cells[1, at : at + LEVELS] = group[:, GROUP:]
    windows = jnp.concatenate([read_window(cells, 2 * p) for p in range(WINDOWS)], axis=0)
    normed = layer_norm(windows, gains[0, 0:1]).astype(BF16)
    for p, (q, k, v) in enumerate(project(normed, qkv_weight[...], query_choice)):
        v_out[p] = v
        scores_out[p] = score(q, k)
    for copy in copies:
        copy.wait()


def first_quarters(quarters, inputs, cells, gains, fc1, fc2, keep):
    middle = []
    for quarter in quarters:
        qr, qc = ROW_HALF[quarter], own_half(quarter)
        middle.append(read_quarter(inputs, qr, qc) + read_quarter(cells, qr, qc).astype(BF16).astype(F32))
    return finished(quarters, middle, gains[0, 1:2], fc1, fc2, keep)


def first_kernel(mine, theirs, scores, v, first_mask, keep, inputs, gains, query_choice, proj, fc1, fc2, lanes, rows, sent_lat, sent_lon, sent_both, table_out, out, cells, table_f32, t_top, t_low):
    me = lax.axis_index("lon")
    for g in range(LONS):
        slot = lax.rem(me // 2 - g // 2 + 8, 4) * 2 + jnp.where(me // 8 == g // 8, 0, 1)
        shard = jnp.where(lax.rem(me, 2) == g % 2, mine[slot], theirs[slot]).astype(F32)
        piece = jnp.concatenate([shard[0], shard[1]], axis=0)
        for n in range(9):
            at = (g * 9 + n) * 8
            table_f32[at : at + 8, :HALF] = piece[:, n * HALF : (n + 1) * HALF]
    table_out[:, :HALF] = table_f32[:, :HALF].astype(BF16)
    tops, lows = picked_rows(table_out, rows[0])
    t_top[...] = dot(tops, lanes[...]).astype(BF16)
    t_low[...] = dot(lows, lanes[...]).astype(BF16)
    mask = first_mask[0:1]
    blended = [blend(scores[p], v[p], lambda h: expanded_bias(t_top, t_low, p, h) + mask) for p in range(WINDOWS)]
    write_attended(cells, 0, blended, query_choice, proj[...])
    results = first_quarters((1, 2, 3), inputs, cells, gains, fc1, fc2, keep)
    out[...] = results
    for at, target in enumerate((sent_lat, sent_lon, sent_both)):
        target[...] = pack_piece(results[at * TOKENS : (at + 1) * TOKENS])


def bias_kernel(table, second_mask, columns, rows, inputs, cells, gains, fc1, fc2, keep, bias_out, near, z_even, z_odd):
    near[...] = first_quarters((0,), inputs, cells, gains, fc1, fc2, keep)
    tops, lows = picked_rows(table, rows[1])
    z_even[...] = dot(tops, columns[0])
    z_odd[...] = dot(lows, columns[1])
    for p in range(WINDOWS):
        for h in range(HEADS):
            whole = selected_bias(z_even, z_odd, p, h) + second_mask[1 if p == WINDOWS - 1 else 0]
            bias_out[p, h * TOKENS : (h + 1) * TOKENS] = whole.astype(BF16)


def write_normed(cells, quarter, piece, gains):
    normed = layer_norm(piece.astype(F32), gains[1, 0:1]).astype(BF16)
    write_quarter(cells, 1 - ROW_HALF[quarter], window_half(quarter), normed.astype(F32))


def ready_kernel(near, from_lon, from_both, gains, cells):
    write_normed(cells, 0, near[...], gains)
    write_normed(cells, 2, unpack_piece(from_lon[...]), gains)
    write_normed(cells, 3, unpack_piece(from_both[...]), gains)


def second_kernel(given, from_lat, bias, gains, qkv_weight, proj, query_choice, own, sent_lat, sent_lon, sent_both, cells, results):
    cells[...] = given[...]
    write_normed(cells, 1, unpack_piece(from_lat[...]), gains)
    normed = jnp.concatenate([read_window(cells, 2 * p + 1) for p in range(WINDOWS)], axis=0).astype(BF16)
    blended = []
    for p, (q, k, v) in enumerate(project(normed, qkv_weight[...], query_choice)):

        def bias_of(h):
            return bias[p, h * TOKENS : (h + 1) * TOKENS].astype(F32) - SHIFT

        blended.append(blend(score(q, k), v, bias_of))
    write_attended(results, 1, blended, query_choice, proj[...])
    pieces = [read_quarter(results, 1 - ROW_HALF[k], window_half(k)).astype(BF16) for k in range(4)]
    own[...] = pieces[0]
    sent_lat[...] = pack_piece(pieces[1])
    sent_lon[...] = pack_piece(pieces[2])
    sent_both[...] = pack_piece(pieces[3])


def own_kernel(fc1, fc2, merge, keep, near, own, gains, result, *refs):
    copies = fetch((fc1, fc2, merge), refs[:3], refs[3])
    middle = near[...].astype(F32) + own[...].astype(F32)
    for copy in copies:
        copy.wait()
    result[...] = feed_forward(middle, gains[1, 1:2], refs[0][...], refs[1][...], keep[1][:, :1] > 0)


def add_kernel(keep, far, from_both, from_lon, gains, fc1, fc2, done):
    middle = []
    for at, piece in enumerate((from_lon, from_both)):
        inputs = far[(at + 1) * TOKENS : (at + 2) * TOKENS].astype(F32)
        middle.append(inputs + unpack_piece(piece[...]).astype(F32))
    done[...] = finished((2, 3), middle, gains[1, 1:2], fc1, fc2, keep)


def last_kernel(keep, far, done, middle, from_lat, gains, fc1, fc2, merge_gain, merge_weight, merged):
    upper = far[:TOKENS].astype(F32) + unpack_piece(from_lat[...]).astype(F32)
    fresh = finished((1,), [upper], gains[1, 1:2], fc1, fc2, keep).astype(F32)
    others = middle[...].astype(F32)
    results = [done[...].astype(F32), fresh, others[:TOKENS], others[TOKENS:]]
    odd = lax.rem(lax.axis_index("lat"), 2) == 1
    groups = {}
    for qr, (first, second) in enumerate(((1, 3), (0, 2))):
        turned_round = odd if qr == 1 else jnp.logical_not(odd)
        right = jnp.where(turned_round, results[second], results[first])
        left = jnp.where(turned_round, results[first], results[second])
        for qc, result in enumerate((left, right)):
            for r in range(3):
                for c in range(6):
                    at = (c * 3 + r) * LEVELS
                    groups[3 * qr + r, 6 * qc + c] = result[at : at + LEVELS]
    parts = [
        jnp.concatenate([groups[2 * r + dr, 2 * c + dc] for r in range(3) for c in range(6)], axis=0)
        for dr in range(2)
        for dc in range(2)
    ]
    average = sum(jnp.sum(part, axis=-1, keepdims=True) for part in parts) / (4 * C)
    parts = [part - average for part in parts]
    spread = sum(jnp.sum(part * part, axis=-1, keepdims=True) for part in parts) / (4 * C)
    scale = lax.rsqrt(spread + 1e-05)
    total = jnp.zeros((TOKENS, 2 * C), F32)
    for d, part in enumerate(parts):
        normed = (part * scale * merge_gain[d : d + 1]).astype(BF16)
        total = total + dot(normed, merge_weight[d * C : (d + 1) * C])
    merged[...] = total.astype(BF16)


VMEM_SPEC = pl.BlockSpec(memory_space=pltpu.VMEM)
SMEM_SPEC = pl.BlockSpec(memory_space=pltpu.SMEM)


def call(kernel, name, micros, outs, scratch, *operands, in_specs=None, aliases=None):
    return pl.pallas_call(
        kernel,
        name=name,
        out_shape=outs,
        in_specs=in_specs or [VMEM_SPEC] * len(operands),
        out_specs=jax.tree.map(lambda _: VMEM_SPEC, outs),
        scratch_shapes=scratch,
        input_output_aliases=aliases or {},
        cost_estimate=pl.CostEstimate(flops=int(micros * 1e9), bytes_accessed=2**20, transcendentals=0),
        compiler_params=pltpu.CompilerParams(vmem_limit_bytes=16 * 2**20),
    )(*operands)


def shape(*dims, dtype=BF16):
    return jax.ShapeDtypeStruct(dims, dtype)


def sent(block, rows, across, back=False):
    route = []
    for i in range(LATS):
        for j in range(LONS):
            to = (i + rows) % LATS
            owner = i if back else to
            step = (1 if owner % 2 == 1 else -1) * (-1 if back else 1)
            route.append((i * LONS + j, to * LONS + (j + across * step) % LONS))
    return lax.ppermute(block, ("lat", "lon"), route)


def turned(block, place):
    route = []
    for j in range(LONS):
        z, x, core = place(j // 8, j // 2 % 4, j % 2)
        route.append((j, z * 8 + x * 2 + core))
    return lax.ppermute(block, "lon", route)


def shards(state, lat_valid, norm_gains, qkv_weight, proj_weight, fc1_weight, fc2_weight, earth_bias, merge_gain, merge_weight):
    shard = earth_bias[:, 0]
    cells = pltpu.VMEM((2, CELLS, GROUP), F32)
    cell_rows = shape(2, CELLS, GROUP, dtype=F32)
    t_scratch = [pltpu.VMEM((768, KEYS), BF16), pltpu.VMEM((768, KEYS), BF16)]
    packed = shape(224, 128)

    def in_hbm(array):
        return pltpu.with_memory_space_constraint(array, pltpu.HBM)

    def like(arrays):
        return [shape(*array.shape, dtype=array.dtype) for array in arrays]

    hbm_spec = pl.BlockSpec(memory_space=pltpu.HBM)
    fc2_turned = jnp.swapaxes(fc2_weight, 1, 2)
    early = [
        shard[None],
        state.transpose(1, 2, 0, 3).reshape(CELLS, C),
        norm_gains,
        qkv_weight,
        jnp.stack([one_hot(query_order(), TOKENS), one_hot(natural_order(), TOKENS)]),
    ]
    late = [qkv_weight, proj_weight]
    layer = [shape(C, C), shape(C, HIDDEN), shape(C, HIDDEN)]
    other_half = turned(shard, lambda z, x, core: (1 - z, x, core))
    held_shard, x, gains, qkv0, query_choice, first_mask, second_mask, keep = call(
        functools.partial(sliced, fetch_kernel, {4: 0}),
        "fetch",
        1.4,
        like(early[:3])
        + [shape(C, 3 * C)]
        + like(early[4:])
        + [
            shape(8, KEYS, dtype=F32),
            shape(2, TOKENS, KEYS, dtype=F32),
            shape(2, TOKENS, GROUP, dtype=F32),
        ],
        [pltpu.SMEM((LATS * ROWS,), jnp.int32), pltpu.SemaphoreType.DMA((len(early) + 1,))],
        in_hbm(lat_valid),
        *[in_hbm(array) for array in early],
        in_specs=[hbm_spec] * (len(early) + 1),
    )
    halves = call(join_kernel, "halves", 0.2, shape(2, 2, WINDOWS, SHARD), [], held_shard, other_half[None])
    ring = [turned(halves, lambda z, x, core: (z, (x + hop) % 4, core)) for hop in range(1, 4)]
    scores, v, inputs, qkv1, proj1 = call(
        functools.partial(sliced, before_kernel, {5: 1, 6: 1}),
        "before",
        2.5,
        [shape(WINDOWS, HEADS * TOKENS, KEYS, dtype=F32), shape(WINDOWS, KEYS, KEYS), cell_rows]
        + [shape(C, 3 * C), shape(C, C)],
        [pltpu.SemaphoreType.DMA((len(late),))],
        halves, x, gains, qkv0, query_choice,
        *[in_hbm(array) for array in late],
        in_specs=[VMEM_SPEC] * 5 + [hbm_spec] * len(late),
    )
    mine = call(join_kernel, "mine", 0.3, shape(8, 2, WINDOWS, SHARD), [], halves, *ring, v)
    theirs = turned(mine, lambda z, x, core: (z, x, 1 - core))
    proj0, fc1_0, fc2_0, lanes, rows, columns = call(
        functools.partial(sliced, prepare_kernel, {1: 0, 2: 0, 3: 0}),
        "prepare",
        1.2,
        layer + [shape(HALF, KEYS), shape(2, 256, 192), shape(2, HALF, 6 * GROUP)],
        [pltpu.SemaphoreType.DMA((3,))],
        mine, in_hbm(proj_weight), in_hbm(fc1_weight), in_hbm(fc2_turned),
        in_specs=[VMEM_SPEC] + [hbm_spec] * 3,
    )
    to_lat, to_lon, to_both, tables, far, attended = call(
        first_kernel,
        "first",
        4.5,
        [packed, packed, packed, shape(1152, KEYS), shape(3 * TOKENS, C), cell_rows],
        [pltpu.VMEM((1152, KEYS), F32)] + t_scratch,
        mine, theirs, scores, v, first_mask, keep, inputs, gains, query_choice, proj0, fc1_0, fc2_0, lanes, rows,
    )
    from_lat, from_lon, from_both = sent(to_lat, -1, 0), sent(to_lon, 0, 1), sent(to_both, -1, 1)
    bias, near = call(
        bias_kernel,
        "bias",
        0.2,
        [shape(WINDOWS, HEADS * TOKENS, KEYS), shape(TOKENS, C)],
        [pltpu.VMEM((768, 768), F32), pltpu.VMEM((768, 768), F32)],
        tables, second_mask, columns, rows, inputs, attended, gains, fc1_0, fc2_0, keep,
    )
    ready = call(ready_kernel, "ready", 0.4, cell_rows, [], near, from_lon, from_both, gains)
    own, to_lat, to_lon, to_both = call(
        second_kernel,
        "second",
        4.5,
        [shape(TOKENS, C), packed, packed, packed],
        [cells, cells],
        ready, from_lat, bias, gains, qkv1, proj1, query_choice,
    )
    from_lon, from_both, from_lat = sent(to_lon, 0, 1, True), sent(to_both, 1, 1, True), sent(to_lat, 1, 0, True)
    done, fc1_1, fc2_1, merge = call(
        functools.partial(sliced, own_kernel, {0: 1, 1: 1}),
        "own",
        0.5,
        [shape(TOKENS, C)] + layer[1:] + like([merge_weight]),
        [pltpu.SemaphoreType.DMA((3,))],
        in_hbm(fc1_weight), in_hbm(fc2_turned), in_hbm(merge_weight), keep, near, own, gains,
        in_specs=[hbm_spec] * 3 + [VMEM_SPEC] * 4,
    )
    middle = call(
        add_kernel, "add", 0.7, shape(2 * TOKENS, C), [], keep, far, from_both, from_lon, gains, fc1_1, fc2_1
    )
    merged = call(
        last_kernel,
        "last",
        2.0,
        shape(TOKENS, 2 * C),
        [],
        keep, far, done, middle, from_lat, gains, fc1_1, fc2_1, merge_gain.reshape(4, C), merge,
    )
    return merged.reshape(3, 6, LEVELS, 2 * C).transpose(2, 0, 1, 3)


def solution(mesh):
    return jax.shard_map(
        shards,
        mesh=mesh,
        in_specs=(
            P(None, "lat", "lon", None),
            P(),
            P(),
            P(),
            P(),
            P(),
            P(),
            P(None, "lat", None, "lon"),
            P(),
            P(),
        ),
        out_specs=P(None, "lat", "lon", None),
        check_vma=False,
    )
```
